32 devices in a mesh: groups: 2 (over x), seq: 16 (over z, y, core).
Axes of the slice: x: 2, y: 2, z: 4, core: 2. Of those that a mesh axis runs over, the one named last changes fastest.
Arguments:
- queries: bfloat16 [8192, 2048], P(('groups', 'seq')), parts along dimension 0, may hold values from -400 to 400
- neighbours: bfloat16 [64, 128, 896], P(('groups', 'seq')), parts along dimension 0, may hold values from -500 to 500
- w_key: bfloat16 [896, 2048], replicated, may hold values from -0.1875 to 0.1875
- w_value: bfloat16 [896, 2048], replicated, may hold values from -0.1875 to 0.1875
- retrieval_owner: int32 [128, 2], P(('groups', 'seq')), parts along dimension 0, may hold values from 0 to 15, as said below
- retrieval_slot: int32 [128, 2], P(('groups', 'seq')), parts along dimension 0, may hold values from 0 to 1
- doc_starts: int32 [128], P(('groups', 'seq')), parts along dimension 0, may hold values 0 or 1
Outputs:
- attended: bfloat16 [8192, 2048], P(('groups', 'seq')), parts along dimension 0
The draws below stay inside these ranges and needn't reach their ends.
There are 2 independent parts, one for each index of `groups`. The reference program is written for one: setup_inputs(seed, part) draws one part's arguments, and reference() takes and returns one part's arrays. A program takes and returns all parts, laid end to end along the dimension named above; an argument that names none is the same for every part. Nothing has to cross between parts.
Inputs may be any that keep to these rules, and one draw needn't show every extreme that they name: `retrieval_owner`: among the 8 owners named by the spans of one device, no owner appears more than 1 times, and some owner appears exactly 1 times.
All inputs are finite; a program needn't handle non-finite values. No bound on the sum of `doc_starts` on one device may be relied on, other than what follows from the above.
Results may differ from the reference program's by a relative error of at most 0.0071.
Values may be sent and summed in bfloat16 or wider, within the bound.
No kernel may reach another device: no remote copies, remote signals or barrier semaphores. Data moves between devices by JAX's collectives and lax.ppermute only.
A program may use at most 128 MiB of HBM per device.

```python
import math
import jax
import jax.numpy as jnp
from jax import lax

CH_DEV = 4
SPAN = 64
NBLEN = 128
NW = 896
HEADS = 16
HEAD_DIM = 128
CAP = 1
NB_DEV = 2
TOKENS = 4096
SPANS = 64
N_SEQ = 16


def draw_queries(key, part):
    shape = (TOKENS, HEADS * HEAD_DIM)
    return jax.random.truncated_normal(key, -4.0, 4.0, shape, jnp.float32).astype(jnp.bfloat16)


def draw_neighbours(key, part):
    shape = (NB_DEV * N_SEQ, NBLEN, NW)
    core_key, row_key, col_key = jax.random.split(key, 3)
    row_scale = jnp.exp(jax.random.uniform(row_key, (NB_DEV * N_SEQ, NBLEN, 1), jnp.float32, 0.0, math.log(10.0)))
    col_scale = jnp.exp(jax.random.uniform(col_key, (1, 1, NW), jnp.float32, 0.0, math.log(10.0)))
    core = jax.random.truncated_normal(core_key, -4.0, 4.0, shape, jnp.float32)
    return (core * row_scale * col_scale).astype(jnp.bfloat16)


def owner_list(key, device, hot_owner):
    device_key = jax.random.fold_in(key, device)
    shuffled = jax.random.permutation(device_key, N_SEQ)
    leading = shuffled[0]
    shuffled = jnp.where(shuffled == hot_owner, leading, shuffled)
    shuffled = jnp.where(jnp.arange(N_SEQ) == 0, hot_owner, shuffled)
    repeated = jnp.tile(shuffled, CAP)[:2 * CH_DEV]
    order = jax.random.permutation(jax.random.fold_in(device_key, 7), 2 * CH_DEV)
    return repeated[order]


def draw_retrieval_owner(key, part):
    hot_owner = jax.random.randint(jax.random.fold_in(key, 3), (), 0, N_SEQ)
    lists = jax.vmap(lambda device: owner_list(key, device, hot_owner))(jnp.arange(N_SEQ))
    return lists.reshape(CH_DEV * N_SEQ, 2).astype(jnp.int32)


def touch_ends(entries, own_key, least, top_value):
    index_at = [jax.random.randint(jax.random.fold_in(own_key, axis), (), 0, length) for axis, length in enumerate(entries.shape)]
    widest = entries.shape.index(max(entries.shape))
    beside = index_at[:widest] + [(index_at[widest] + 1) % entries.shape[widest]] + index_at[widest + 1:]
    return entries.at[tuple(index_at)].set(least).at[tuple(beside)].set(top_value)


def scatter_about(rng, dims, scale, limit, held_as=jnp.bfloat16):
    values = scale * jax.random.normal(rng, dims, jnp.float32)
    return jnp.clip(values, min=-limit, max=limit).astype(held_as)


def setup_inputs(seed: int = 0, part: int = 0) -> dict:
    streams_of = jax.random.split(jax.random.key(seed), 8)
    part_splits = jax.random.split(jax.random.fold_in(streams_of[7], part), 8)
    queries = draw_queries(jax.random.fold_in(jax.random.fold_in(streams_of[7], part), 71), part)
    neighbours = draw_neighbours(jax.random.fold_in(jax.random.fold_in(streams_of[7], part), 71), part)
    w_key = scatter_about(streams_of[2], (NW, HEADS * HEAD_DIM), NW ** -0.5, 0.1875)
    w_value = scatter_about(streams_of[3], (NW, HEADS * HEAD_DIM), NW ** -0.5, 0.1875)
    retrieval_owner = draw_retrieval_owner(jax.random.fold_in(jax.random.fold_in(streams_of[7], part), 71), part)
    retrieval_slot = touch_ends(jax.random.randint(part_splits[5], (SPANS, 2), 0, NB_DEV), jax.random.fold_in(part_splits[5], 1), 0, NB_DEV - 1).astype(jnp.int32)
    doc_starts = touch_ends((jax.random.randint(part_splits[6], (SPANS,), 0, 4) < 1).astype(jnp.int32), jax.random.fold_in(part_splits[6], 1), 0, 1)
    return {"queries": queries, "neighbours": neighbours, "w_key": w_key, "w_value": w_value, "retrieval_owner": retrieval_owner, "retrieval_slot": retrieval_slot, "doc_starts": doc_starts}


def normalize(tokens_in):
    widened = tokens_in.astype(jnp.float32)
    factor = lax.rsqrt(lax.optimization_barrier(jnp.mean(widened * widened, axis=-1, keepdims=True)) + 1e-06)
    return (widened * factor).astype(jnp.bfloat16)

def reference(queries, neighbours, w_key, w_value, retrieval_owner, retrieval_slot, doc_starts):
    model_width = HEADS * HEAD_DIM
    token_count = queries.shape[0]
    span_count = doc_starts.shape[0]
    normed = normalize(neighbours).reshape(-1, NW)
    keys_all = jnp.dot(normed, w_key, preferred_element_type=jnp.float32).astype(jnp.bfloat16).reshape(-1, NBLEN, model_width)
    values_all = jnp.dot(normed, w_value, preferred_element_type=jnp.float32).astype(jnp.bfloat16).reshape(-1, NBLEN, model_width)
    neighbour_ids = (retrieval_owner * NB_DEV + retrieval_slot).astype(jnp.int32)
    shifted = jnp.concatenate([queries[SPAN - 1:], jnp.zeros((SPAN - 1, model_width), jnp.bfloat16)], 0)
    shifted = shifted.reshape(span_count, SPAN, model_width)
    later = jnp.concatenate([doc_starts[1:], jnp.ones((1,), jnp.int32)])
    row_index = jnp.arange(SPAN)
    valid = (row_index[None, :] == 0) | (later[:, None] == 0)
    score_scale = 1.0 / jnp.sqrt(jnp.float32(HEAD_DIM))

    def window(packed):
        query_block, pair_ids, kept = packed
        key_block = keys_all[pair_ids].reshape(2 * NBLEN, HEADS, HEAD_DIM).astype(jnp.float32)
        value_block = values_all[pair_ids].reshape(2 * NBLEN, HEADS, HEAD_DIM).astype(jnp.float32)
        query_heads = query_block.reshape(SPAN, HEADS, HEAD_DIM).astype(jnp.float32)
        scores = jnp.einsum('qhd,khd->hqk', query_heads, key_block) * score_scale
        highest = lax.optimization_barrier(jnp.max(scores, axis=-1, keepdims=True))
        powers = jnp.exp(scores - highest)
        totals = lax.optimization_barrier(jnp.sum(powers, axis=-1, keepdims=True))
        weights = lax.optimization_barrier((powers / totals).astype(jnp.bfloat16)).astype(jnp.float32)
        result = jnp.einsum('hqk,khd->qhd', weights, value_block).reshape(SPAN, model_width)
        result = jnp.where(kept[:, None], result, 0.0)
        return result.astype(jnp.bfloat16)
    outputs = lax.map(window, (shifted, neighbour_ids, valid))
    flattened = outputs.reshape(token_count, model_width)
    return jnp.concatenate([jnp.zeros((SPAN - 1, model_width), jnp.bfloat16), flattened[:token_count - SPAN + 1]], 0)
```

```python
import functools
import math

import jax
import jax.numpy as jnp
from jax import lax
from jax.experimental import pallas as pl
from jax.experimental.pallas import tpu as pltpu
from jax.sharding import PartitionSpec as P

SPAN = 64
HEADS = 16
HEAD_DIM = 128
EPS = 1e-6
SCALE = math.log2(math.e) / math.sqrt(HEAD_DIM)


def contract(left, right, dims):
    return lax.dot_general(left, right, (dims, ((), ())), preferred_element_type=jnp.float32)


def fold_kernel(query_ref, key_ref, folded_ref, single_ref):
    blocks = folded_ref.shape[0]
    for head in range(HEADS):
        columns = slice(head * HEAD_DIM, (head + 1) * HEAD_DIM)
        rows = contract(query_ref[:, columns], key_ref[:, columns], ((1,), (1,))) * SCALE
        single_ref[head : head + 1, :] = rows[:1]
        rounded = rows.astype(jnp.bfloat16)
        for block in range(blocks):
            folded_ref[block, head] = rounded[block * SPAN : (block + 1) * SPAN]


def fold(rows, w_key):
    blocks, width = rows.shape[0] // SPAN, w_key.shape[0]
    return pl.pallas_call(
        fold_kernel,
        out_shape=(
            jax.ShapeDtypeStruct((blocks, HEADS, SPAN, width), jnp.bfloat16),
            jax.ShapeDtypeStruct((HEADS, width), jnp.float32),
        ),
        in_specs=[pl.BlockSpec(memory_space=pltpu.VMEM)] * 2,
        out_specs=(pl.BlockSpec(memory_space=pltpu.VMEM),) * 2,
        compiler_params=pltpu.CompilerParams(vmem_limit_bytes=48 * 2**20),
        cost_estimate=pl.CostEstimate(
            flops=2 * rows.size * width, bytes_accessed=16 * 2**20, transcendentals=0
        ),
        name="fold_queries",
    )(rows, w_key)


def mix(scores_of, tokens):
    scores = contract(scores_of, tokens, ((1,), (1,)))
    powers = jnp.exp2(scores - jnp.max(scores, axis=-1, keepdims=True))
    totals = jnp.sum(powers, axis=-1, keepdims=True)
    weights = (powers * (1.0 / totals)).astype(jnp.bfloat16)
    return contract(weights, tokens, ((1,), (0,)))


def attend_kernel(
    ids_ref, keep_ref, folded_hbm, single_ref, store_hbm, value_ref, out_ref,
    folded, raw, tokens, mixed, folded_sems, raw_sems,
):
    blocks = folded.shape[0]
    windows = blocks + 1
    length, width = raw.shape[2], raw.shape[3]

    def fetch_raw(window, part):
        return pltpu.make_async_copy(
            store_hbm.at[ids_ref[window, part]], raw.at[window, part], raw_sems.at[window, part]
        )

    def fetch_folded(block):
        return pltpu.make_async_copy(folded_hbm.at[block], folded.at[block], folded_sems.at[block])

    order = [blocks] + list(range(blocks))
    for window in order:
        for part in range(2):
            fetch_raw(window, part).start()
        if window < blocks:
            fetch_folded(window).start()

    lone = None
    for window in order:
        for part in range(2):
            fetch_raw(window, part).wait()
            widened = raw[window, part].astype(jnp.float32)
            factor = lax.rsqrt(jnp.mean(widened * widened, axis=-1, keepdims=True) + EPS)
            tokens[window, part * length : (part + 1) * length] = (widened * factor).astype(jnp.bfloat16)
        if window == blocks:
            lone = mix(single_ref[...].astype(jnp.bfloat16), tokens[window])
            continue
        fetch_folded(window).wait()
        rows = mix(folded[window].reshape(HEADS * SPAN, width), tokens[window]).reshape(HEADS, SPAN, width)
        if window == 0:
            first = lax.broadcasted_iota(jnp.int32, rows.shape, 1) == 0
            rows = jnp.where(first, lone[:, None, :], rows)
        mixed[:, window * SPAN : (window + 1) * SPAN] = rows.astype(jnp.bfloat16)

    count = blocks * SPAN
    place = lax.broadcasted_iota(jnp.int32, (count, HEAD_DIM), 0)
    kept = place % SPAN == 0
    for block in range(blocks):
        kept = kept | ((place // SPAN == block) & (keep_ref[block] > 0))
    for head in range(HEADS):
        columns = slice(head * HEAD_DIM, (head + 1) * HEAD_DIM)
        rows = contract(mixed[head], value_ref[:, columns], ((1,), (0,)))
        rows = jnp.where(kept, rows, 0.0)
        out_ref[:, columns] = pltpu.roll(rows, count - 1, 0).astype(jnp.bfloat16)


def attend(ids, keep, folded, single, store, w_value):
    blocks, _, _, width = folded.shape
    length = store.shape[1]
    count = blocks * SPAN
    model_width = w_value.shape[1]
    smem, vmem, anywhere = (
        pl.BlockSpec(memory_space=space) for space in (pltpu.SMEM, pltpu.VMEM, pl.ANY)
    )
    return pl.pallas_call(
        attend_kernel,
        out_shape=jax.ShapeDtypeStruct((count, model_width), jnp.bfloat16),
        in_specs=[smem, smem, anywhere, vmem, anywhere, vmem],
        out_specs=vmem,
        scratch_shapes=[
            pltpu.VMEM(folded.shape, jnp.bfloat16),
            pltpu.VMEM((blocks + 1, 2, length, width), jnp.bfloat16),
            pltpu.VMEM((blocks + 1, 2 * length, width), jnp.bfloat16),
            pltpu.VMEM((HEADS, count, width), jnp.bfloat16),
            pltpu.SemaphoreType.DMA((blocks,)),
            pltpu.SemaphoreType.DMA((blocks + 1, 2)),
        ],
        compiler_params=pltpu.CompilerParams(vmem_limit_bytes=56 * 2**20),
        cost_estimate=pl.CostEstimate(
            flops=2 * HEADS * count * width * (4 * length + HEAD_DIM),
            bytes_accessed=16 * 2**20,
            transcendentals=HEADS * count * 2 * length,
        ),
        name="attend_windows",
    )(ids, keep, folded, single, store, w_value)


def body(queries, neighbours, w_key, w_value, retrieval_owner, retrieval_slot, doc_starts):
    devices = lax.axis_size("seq")
    here = lax.axis_index("seq")
    store = lax.all_gather(neighbours, "seq", axis=0, tiled=True)
    own_ids = retrieval_owner * neighbours.shape[0] + retrieval_slot
    ids_before = lax.ppermute(own_ids[-1:], "seq", [(i, i + 1) for i in range(devices - 1)])
    ids = jnp.concatenate([ids_before, own_ids], 0)
    blocks = doc_starts.shape[0]
    opening = (here == 0) & (jnp.arange(blocks) == 0)
    keep = ((doc_starts == 0) & jnp.logical_not(opening)).astype(jnp.int32)
    rows = jnp.concatenate([queries[-1:], queries[:-1]], 0)
    folded, single = fold(rows, w_key)
    return attend(ids, keep, folded, single, store, w_value)


def solution(mesh):
    return jax.shard_map(
        body,
        mesh=mesh,
        in_specs=(
            P(("groups", "seq"), None),
            P(("groups", "seq"), None, None),
            P(),
            P(),
            P(("groups", "seq"), None),
            P(("groups", "seq"), None),
            P(("groups", "seq")),
        ),
        out_specs=P(("groups", "seq"), None),
        check_vma=False,
    )
```

```python
import functools
import math

import jax
import jax.numpy as jnp
from jax import lax
from jax.experimental import pallas as pl
from jax.experimental.pallas import tpu as pltpu
from jax.sharding import PartitionSpec as P

SPAN = 64
HEADS = 16
HEAD_DIM = 128
EPS = 1e-6
SCALE = math.log2(math.e) / math.sqrt(HEAD_DIM)


def contract(left, right, dims):
    return lax.dot_general(left, right, (dims, ((), ())), preferred_element_type=jnp.float32)


def fold_kernel(query_ref, key_ref, folded_ref, single_ref):
    blocks = folded_ref.shape[0]
    for head in range(HEADS):
        columns = slice(head * HEAD_DIM, (head + 1) * HEAD_DIM)
        rows = contract(query_ref[:, columns], key_ref[:, columns], ((1,), (1,))) * SCALE
        single_ref[head : head + 1, :] = rows[:1]
        rounded = rows.astype(jnp.bfloat16)
        for block in range(blocks):
            folded_ref[block, head] = rounded[block * SPAN : (block + 1) * SPAN]


def fold(rows, w_key):
    blocks, width = rows.shape[0] // SPAN, w_key.shape[0]
    return pl.pallas_call(
        fold_kernel,
        out_shape=(
            jax.ShapeDtypeStruct((blocks, HEADS, SPAN, width), jnp.bfloat16),
            jax.ShapeDtypeStruct((HEADS, width), jnp.float32),
        ),
        in_specs=[pl.BlockSpec(memory_space=pltpu.VMEM)] * 2,
        out_specs=(pl.BlockSpec(memory_space=pltpu.VMEM),) * 2,
        compiler_params=pltpu.CompilerParams(vmem_limit_bytes=48 * 2**20),
        cost_estimate=pl.CostEstimate(
            flops=2 * rows.size * width, bytes_accessed=16 * 2**20, transcendentals=0
        ),
        name="fold_queries",
    )(rows, w_key)


def mix(scores_of, tokens):
    scores = contract(scores_of, tokens, ((1,), (1,)))
    powers = jnp.exp2(scores - jnp.max(scores, axis=-1, keepdims=True))
    totals = jnp.sum(powers, axis=-1, keepdims=True)
    weights = (powers * (1.0 / totals)).astype(jnp.bfloat16)
    return contract(weights, tokens, ((1,), (0,)))


def attend_kernel(
    source_ref, block_ref, keep_ref, folded_hbm, single_ref, value_ref, *rest
):
    *stores, out_ref, folded, raw, tokens, mixed, folded_sems, raw_sems = rest
    blocks = folded.shape[0]
    windows = blocks + 1
    length, width = raw.shape[2], raw.shape[3]

    def fetch_raw(window, part, store):
        return pltpu.make_async_copy(
            store.at[block_ref[window, part]], raw.at[window, part], raw_sems.at[window, part]
        )

    def fetch_folded(block):
        return pltpu.make_async_copy(folded_hbm.at[block], folded.at[block], folded_sems.at[block])

    order = [blocks] + list(range(blocks))
    for window in order:
        for part in range(2):
            for place, store in enumerate(stores):

                @pl.when(source_ref[window, part] == place)
                def _(store=store):
                    fetch_raw(window, part, store).start()

        if window < blocks:
            fetch_folded(window).start()

    lone = None
    for window in order:
        for part in range(2):
            fetch_raw(window, part, stores[0]).wait()
            widened = raw[window, part].astype(jnp.float32)
            factor = lax.rsqrt(jnp.mean(widened * widened, axis=-1, keepdims=True) + EPS)
            tokens[window, part * length : (part + 1) * length] = (widened * factor).astype(jnp.bfloat16)
        if window == blocks:
            lone = mix(single_ref[...].astype(jnp.bfloat16), tokens[window])
            continue
        fetch_folded(window).wait()
        rows = mix(folded[window].reshape(HEADS * SPAN, width), tokens[window]).reshape(HEADS, SPAN, width)
        if window == 0:
            first = lax.broadcasted_iota(jnp.int32, rows.shape, 1) == 0
            rows = jnp.where(first, lone[:, None, :], rows)
        mixed[:, window * SPAN : (window + 1) * SPAN] = rows.astype(jnp.bfloat16)

    count = blocks * SPAN
    place = lax.broadcasted_iota(jnp.int32, (count, HEAD_DIM), 0)
    kept = place % SPAN == 0
    for block in range(blocks):
        kept = kept | ((place // SPAN == block) & (keep_ref[block] > 0))
    for head in range(HEADS):
        columns = slice(head * HEAD_DIM, (head + 1) * HEAD_DIM)
        rows = contract(mixed[head], value_ref[:, columns], ((1,), (0,)))
        rows = jnp.where(kept, rows, 0.0)
        out_ref[:, columns] = pltpu.roll(rows, count - 1, 0).astype(jnp.bfloat16)


def attend(source, block, keep, folded, single, stores, w_value):
    blocks, _, _, width = folded.shape
    length = stores[0].shape[1]
    count = blocks * SPAN
    model_width = w_value.shape[1]
    smem, vmem, anywhere = (
        pl.BlockSpec(memory_space=space) for space in (pltpu.SMEM, pltpu.VMEM, pl.ANY)
    )
    return pl.pallas_call(
        attend_kernel,
        out_shape=jax.ShapeDtypeStruct((count, model_width), jnp.bfloat16),
        in_specs=[smem, smem, smem, anywhere, vmem, vmem] + [anywhere] * len(stores),
        out_specs=vmem,
        scratch_shapes=[
            pltpu.VMEM(folded.shape, jnp.bfloat16),
            pltpu.VMEM((blocks + 1, 2, length, width), jnp.bfloat16),
            pltpu.VMEM((blocks + 1, 2 * length, width), jnp.bfloat16),
            pltpu.VMEM((HEADS, count, width), jnp.bfloat16),
            pltpu.SemaphoreType.DMA((blocks,)),
            pltpu.SemaphoreType.DMA((blocks + 1, 2)),
        ],
        compiler_params=pltpu.CompilerParams(vmem_limit_bytes=56 * 2**20),
        cost_estimate=pl.CostEstimate(
            flops=2 * HEADS * count * width * (4 * length + HEAD_DIM),
            bytes_accessed=16 * 2**20,
            transcendentals=HEADS * count * 2 * length,
        ),
        name="attend_windows",
    )(source, block, keep, folded, single, w_value, *stores)


def body(queries, neighbours, w_key, w_value, retrieval_owner, retrieval_slot, doc_starts):
    devices = lax.axis_size("seq")
    here = lax.axis_index("seq")
    cores = 2
    same_core = [list(range(core, devices, cores)) for core in range(cores)]
    mine = lax.all_gather(neighbours, "seq", axis=0, tiled=True, axis_index_groups=same_core)
    other = lax.ppermute(mine, "seq", [(i, i ^ 1) for i in range(devices)])
    owner_slot = jnp.stack([retrieval_owner, retrieval_slot])
    before = lax.ppermute(owner_slot[:, -1:], "seq", [(i, i + 1) for i in range(devices - 1)])
    owner, slot = jnp.concatenate([before, owner_slot], 1)
    source = jnp.where(owner % cores == here % cores, 0, 1)
    block = owner // cores * neighbours.shape[0] + slot
    blocks = doc_starts.shape[0]
    opening = (here == 0) & (jnp.arange(blocks) == 0)
    keep = ((doc_starts == 0) & jnp.logical_not(opening)).astype(jnp.int32)
    rows = jnp.concatenate([queries[-1:], queries[:-1]], 0)
    folded, single = fold(rows, w_key)
    return attend(source, block, keep, folded, single, (mine, other), w_value)


def solution(mesh):
    return jax.shard_map(
        body,
        mesh=mesh,
        in_specs=(
            P(("groups", "seq"), None),
            P(("groups", "seq"), None, None),
            P(),
            P(),
            P(("groups", "seq"), None),
            P(("groups", "seq"), None),
            P(("groups", "seq")),
        ),
        out_specs=P(("groups", "seq"), None),
        check_vma=False,
    )
```

```python
import functools
import math

import jax
import jax.numpy as jnp
from jax import lax
from jax.experimental import pallas as pl
from jax.experimental.pallas import tpu as pltpu
from jax.sharding import PartitionSpec as P

SPAN = 64
HEADS = 16
HEAD_DIM = 128
EPS = 1e-6
SCALE = math.log2(math.e) / math.sqrt(HEAD_DIM)


def contract(left, right, dims):
    return lax.dot_general(left, right, (dims, ((), ())), preferred_element_type=jnp.float32)


def fold_kernel(query_ref, key_ref, folded_ref, single_ref):
    blocks = folded_ref.shape[0]
    for head in range(HEADS):
        columns = slice(head * HEAD_DIM, (head + 1) * HEAD_DIM)
        rows = contract(query_ref[:, columns], key_ref[:, columns], ((1,), (1,))) * SCALE
        single_ref[head : head + 1, :] = rows[:1]
        rounded = rows.astype(jnp.bfloat16)
        for block in range(blocks):
            folded_ref[block, head] = rounded[block * SPAN : (block + 1) * SPAN]


def fold(rows, w_key):
    blocks, width = rows.shape[0] // SPAN, w_key.shape[0]
    return pl.pallas_call(
        fold_kernel,
        out_shape=(
            jax.ShapeDtypeStruct((blocks, HEADS, SPAN, width), jnp.bfloat16),
            jax.ShapeDtypeStruct((HEADS, width), jnp.float32),
        ),
        in_specs=[pl.BlockSpec(memory_space=pltpu.VMEM)] * 2,
        out_specs=(pl.BlockSpec(memory_space=pltpu.VMEM),) * 2,
        compiler_params=pltpu.CompilerParams(vmem_limit_bytes=48 * 2**20),
        cost_estimate=pl.CostEstimate(
            flops=2 * rows.size * width, bytes_accessed=16 * 2**20, transcendentals=0
        ),
        name="fold_queries",
    )(rows, w_key)


def mix(scores_of, tokens):
    scores = contract(scores_of, tokens, ((1,), (1,)))
    powers = jnp.exp2(scores - jnp.max(scores, axis=-1, keepdims=True))
    totals = jnp.sum(powers, axis=-1, keepdims=True)
    weights = (powers * (1.0 / totals)).astype(jnp.bfloat16)
    return contract(weights, tokens, ((1,), (0,)))


def attend_kernel(
    source_ref, block_ref, keep_ref, folded_hbm, single_ref, value_ref, *rest
):
    *stores, out_ref, folded, raw, tokens, mixed, folded_sems, raw_sems = rest
    blocks = folded.shape[0]
    windows = blocks + 1
    length, width = raw.shape[2], raw.shape[3]

    def fetch_raw(window, part, store):
        return pltpu.make_async_copy(
            store.at[block_ref[window, part]], raw.at[window, part], raw_sems.at[window, part]
        )

    def fetch_folded(block):
        return pltpu.make_async_copy(folded_hbm.at[block], folded.at[block], folded_sems.at[block])

    order = [blocks] + list(range(blocks))
    for window in order:
        for part in range(2):
            for place, store in enumerate(stores):

                @pl.when(source_ref[window, part] == place)
                def _(store=store):
                    fetch_raw(window, part, store).start()

        if window < blocks:
            fetch_folded(window).start()

    lone = None
    for window in order:
        for part in range(2):
            fetch_raw(window, part, stores[0]).wait()
            widened = raw[window, part].astype(jnp.float32)
            factor = lax.rsqrt(jnp.mean(widened * widened, axis=-1, keepdims=True) + EPS)
            tokens[window, part * length : (part + 1) * length] = (widened * factor).astype(jnp.bfloat16)
        if window == blocks:
            lone = mix(single_ref[...].astype(jnp.bfloat16), tokens[window])
            continue
        fetch_folded(window).wait()
        rows = mix(folded[window].reshape(HEADS * SPAN, width), tokens[window]).reshape(HEADS, SPAN, width)
        if window == 0:
            first = lax.broadcasted_iota(jnp.int32, rows.shape, 1) == 0
            rows = jnp.where(first, lone[:, None, :], rows)
        mixed[:, window * SPAN : (window + 1) * SPAN] = rows.astype(jnp.bfloat16)

    count = blocks * SPAN
    place = lax.broadcasted_iota(jnp.int32, (count, HEAD_DIM), 0)
    kept = place % SPAN == 0
    for block in range(blocks):
        kept = kept | ((place // SPAN == block) & (keep_ref[block] > 0))
    for head in range(HEADS):
        columns = slice(head * HEAD_DIM, (head + 1) * HEAD_DIM)
        rows = contract(mixed[head], value_ref[:, columns], ((1,), (0,)))
        rows = jnp.where(kept, rows, 0.0)
        out_ref[:, columns] = pltpu.roll(rows, count - 1, 0).astype(jnp.bfloat16)


def attend(source, block, keep, folded, single, stores, w_value):
    blocks, _, _, width = folded.shape
    length = stores[0].shape[1]
    count = blocks * SPAN
    model_width = w_value.shape[1]
    smem, vmem, anywhere = (
        pl.BlockSpec(memory_space=space) for space in (pltpu.SMEM, pltpu.VMEM, pl.ANY)
    )
    return pl.pallas_call(
        attend_kernel,
        out_shape=jax.ShapeDtypeStruct((count, model_width), jnp.bfloat16),
        in_specs=[smem, smem, smem, anywhere, vmem, vmem] + [anywhere] * len(stores),
        out_specs=vmem,
        scratch_shapes=[
            pltpu.VMEM(folded.shape, jnp.bfloat16),
            pltpu.VMEM((blocks + 1, 2, length, width), jnp.bfloat16),
            pltpu.VMEM((blocks + 1, 2 * length, width), jnp.bfloat16),
            pltpu.VMEM((HEADS, count, width), jnp.bfloat16),
            pltpu.SemaphoreType.DMA((blocks,)),
            pltpu.SemaphoreType.DMA((blocks + 1, 2)),
        ],
        compiler_params=pltpu.CompilerParams(vmem_limit_bytes=56 * 2**20),
        cost_estimate=pl.CostEstimate(
            flops=2 * HEADS * count * width * (4 * length + HEAD_DIM),
            bytes_accessed=16 * 2**20,
            transcendentals=HEADS * count * 2 * length,
        ),
        name="attend_windows",
    )(source, block, keep, folded, single, w_value, *stores)


CORES = 2


def chip_ring(mesh):
    row = mesh.devices.reshape(-1, mesh.shape["seq"])[0]
    chips = list(range(len(row) // CORES))
    columns = [tuple(getattr(row[CORES * chip], "coords", (0, 0))[:2]) for chip in chips]
    if len(set(columns)) != 2:
        return chips
    up = [chip for chip in chips if columns[chip] == columns[0]]
    return up + [chip for chip in reversed(chips) if columns[chip] != columns[0]]


def gather(stored, ring):
    size = len(ring)
    half = size // 2

    def turned(value, steps):
        pairs = [
            (CORES * ring[i] + core, CORES * ring[(i + steps) % size] + core)
            for i in range(size)
            for core in range(CORES)
        ]
        return lax.ppermute(value, "seq", pairs)

    ahead, behind = [stored], [stored]
    for _ in range((size - 1) // 2):
        ahead.append(turned(ahead[-1], 1))
        behind.append(turned(behind[-1], -1))
    own = ahead + behind[1:]
    if size % 2 == 0:
        cut = stored.shape[0] // 2
        own += [turned(ahead[-1][:cut], 1), turned(behind[-1][cut:], -1)]
    swap = [(i, i ^ 1) for i in range(CORES * size)]
    return own + [lax.ppermute(value, "seq", swap) for value in own]


def locate(owner, slot, here, stored, ring):
    size = len(ring)
    reach = (size - 1) // 2
    order = jnp.asarray([ring.index(chip) for chip in range(size)], jnp.int32)

    def place_of(device):
        chips = jnp.arange(size)
        return jnp.sum(jnp.where((device // CORES)[..., None] == chips, order, 0), axis=-1)

    away = (place_of(here) - place_of(owner)) % size
    cut = stored // 2
    source = jnp.where(away <= reach, away, reach + size - away)
    block = slot
    if size % 2 == 0:
        middle, late = away == size // 2, slot >= cut
        source = jnp.where(middle, 2 * reach + 1 + late, source)
        block = jnp.where(middle & late, slot - cut, slot)
    count = 2 * reach + 1 + 2 * (size % 2 == 0)
    return source + jnp.where(owner % CORES == here % CORES, 0, count), block


def body(ring, queries, neighbours, w_key, w_value, retrieval_owner, retrieval_slot, doc_starts):
    devices = lax.axis_size("seq")
    here = lax.axis_index("seq")
    stores = gather(neighbours, ring)
    owner_slot = jnp.stack([retrieval_owner, retrieval_slot])
    before = lax.ppermute(owner_slot[:, -1:], "seq", [(i, i + 1) for i in range(devices - 1)])
    owner, slot = jnp.concatenate([before, owner_slot], 1)
    source, block = locate(owner, slot, here, neighbours.shape[0], ring)
    blocks = doc_starts.shape[0]
    opening = (here == 0) & (jnp.arange(blocks) == 0)
    keep = ((doc_starts == 0) & jnp.logical_not(opening)).astype(jnp.int32)
    rows = jnp.concatenate([queries[-1:], queries[:-1]], 0)
    folded, single = fold(rows, w_key)
    return attend(source, block, keep, folded, single, stores, w_value)


def solution(mesh):
    return jax.shard_map(
        functools.partial(body, chip_ring(mesh)),
        mesh=mesh,
        in_specs=(
            P(("groups", "seq"), None),
            P(("groups", "seq"), None, None),
            P(),
            P(),
            P(("groups", "seq"), None),
            P(("groups", "seq"), None),
            P(("groups", "seq")),
        ),
        out_specs=P(("groups", "seq"), None),
        check_vma=False,
    )
```

```python
import functools
import math

import jax
import jax.numpy as jnp
from jax import lax
from jax.experimental import pallas as pl
from jax.experimental.pallas import tpu as pltpu
from jax.sharding import PartitionSpec as P

SPAN = 64
HEADS = 16
HEAD_DIM = 128
EPS = 1e-6
SCALE = math.log2(math.e) / math.sqrt(HEAD_DIM)
CORES = 2
GROUP = 4
MIB = 2**20


SMEM_SPEC = pl.BlockSpec(memory_space=pltpu.SMEM)
VMEM_SPEC = pl.BlockSpec(memory_space=pltpu.VMEM)
ANY_SPEC = pl.BlockSpec(memory_space=pl.ANY)


def contract(left, right, dims):
    return lax.dot_general(left, right, (dims, ((), ())), preferred_element_type=jnp.float32)


def head_columns(head):
    return slice(head * HEAD_DIM, (head + 1) * HEAD_DIM)


def fold_kernel(query_ref, key_ref, folded_ref, single_ref):
    for head in range(HEADS):
        columns = head_columns(head)
        rows = contract(query_ref[:, columns], key_ref[:, columns], ((1,), (1,))) * SCALE
        single_ref[head : head + 1, :] = rows[:1]
        folded_ref[head] = rows.astype(jnp.bfloat16)


def fold(rows, w_key):
    count, width = rows.shape[0], w_key.shape[0]
    return pl.pallas_call(
        fold_kernel,
        out_shape=(
            jax.ShapeDtypeStruct((HEADS, count, width), jnp.bfloat16),
            jax.ShapeDtypeStruct((HEADS, width), jnp.float32),
        ),
        in_specs=[VMEM_SPEC] * 2,
        out_specs=(VMEM_SPEC,) * 2,
        compiler_params=pltpu.CompilerParams(vmem_limit_bytes=32 * MIB),
        cost_estimate=pl.CostEstimate(
            flops=2 * rows.size * width, bytes_accessed=16 * MIB, transcendentals=0
        ),
        name="fold_queries",
    )(rows, w_key)


def normalise(raw, tokens_ref, turned_ref):
    widened = raw.astype(jnp.float32)
    factor = lax.rsqrt(jnp.mean(widened * widened, axis=-1, keepdims=True) + EPS)
    scaled = widened * factor
    tokens_ref[...] = scaled.astype(jnp.bfloat16)
    turned_ref[...] = scaled.T.astype(jnp.bfloat16)


def collect_kernel(source_ref, block_ref, *rest):
    *stores, tokens_ref, turned_ref, raw, sems = rest
    requests = raw.shape[0]

    def fetch(request, store):
        return pltpu.make_async_copy(store.at[block_ref[request]], raw.at[request], sems.at[request])

    def begin(request, carry):
        for place, store in enumerate(stores):

            @pl.when(source_ref[request] == place)
            def _(store=store):
                fetch(request, store).start()

        return carry

    def finish(request, carry):
        @pl.when(source_ref[request] < len(stores))
        def _():
            fetch(request, stores[0]).wait()
            normalise(raw[request], tokens_ref.at[request], turned_ref.at[request])

        return carry

    lax.fori_loop(0, requests, begin, 0)
    lax.fori_loop(0, requests, finish, 0)


def collect(source, block, stores):
    requests = source.shape[0]
    length, width = stores[0].shape[1:]
    return pl.pallas_call(
        collect_kernel,
        out_shape=(
            jax.ShapeDtypeStruct((requests, length, width), jnp.bfloat16),
            jax.ShapeDtypeStruct((requests, width, length), jnp.bfloat16),
        ),
        in_specs=[SMEM_SPEC] * 2 + [ANY_SPEC] * len(stores),
        out_specs=(VMEM_SPEC,) * 2,
        scratch_shapes=[
            pltpu.VMEM((requests, length, width), jnp.bfloat16),
            pltpu.SemaphoreType.DMA((requests,)),
        ],
        compiler_params=pltpu.CompilerParams(vmem_limit_bytes=24 * MIB),
        cost_estimate=pl.CostEstimate(flops=4 * MIB, bytes_accessed=8 * MIB, transcendentals=0),
        name="collect_early",
    )(source, block, *stores)


def weigh(scores):
    powers = jnp.exp2(scores - jnp.max(scores, axis=-1, keepdims=True))
    totals = jnp.sum(powers, axis=-1, keepdims=True)
    return (powers * (1.0 / totals)).astype(jnp.bfloat16)


def attend_kernel(
    early, source_ref, block_ref, keep_ref, folded_ref, single_ref, tokens_in, turned_in, value_ref, *rest
):
    *late, out_ref, tokens, turned, raw, mixed, sems = rest
    requests, length, width = raw.shape
    windows = requests // 2
    blocks = windows - 1

    def fetch_early(request):
        return (
            pltpu.make_async_copy(tokens_in.at[request], tokens.at[request], sems.at[request, 0]),
            pltpu.make_async_copy(turned_in.at[request], turned.at[request], sems.at[request, 1]),
        )

    def fetch_late(request, store):
        return pltpu.make_async_copy(store.at[block_ref[request]], raw.at[request], sems.at[request, 0])

    order = [blocks] + list(range(blocks))
    for window in order:
        for request in (2 * window, 2 * window + 1):

            @pl.when(source_ref[request] < early)
            def _(request=request):
                for copy in fetch_early(request):
                    copy.start()

            for place, store in enumerate(late):

                @pl.when(source_ref[request] == early + place)
                def _(request=request, store=store):
                    fetch_late(request, store).start()

    lone = None
    for window in order:
        for request in (2 * window, 2 * window + 1):

            @pl.when(source_ref[request] < early)
            def _(request=request):
                for copy in fetch_early(request):
                    copy.wait()

            @pl.when(source_ref[request] >= early)
            def _(request=request):
                fetch_late(request, late[0]).wait()
                normalise(raw[request], tokens.at[request], turned.at[request])

        here = tokens[2 * window : 2 * window + 2].reshape(2 * length, width)
        across = jnp.concatenate([turned[2 * window], turned[2 * window + 1]], axis=1)
        if window == blocks:
            weights = weigh(contract(single_ref[...].astype(jnp.bfloat16), across, ((1,), (0,))))
            lone = contract(weights, here, ((1,), (0,)))
            continue
        rows = slice(window * SPAN, (window + 1) * SPAN)

        def score(group):
            taken = folded_ref[group * GROUP : (group + 1) * GROUP, rows].reshape(GROUP * SPAN, width)
            return contract(taken, across, ((1,), (0,)))

        groups = HEADS // GROUP
        scores = score(0)
        for group in range(groups):
            following = score(group + 1) if group + 1 < groups else None
            sums = contract(weigh(scores), here, ((1,), (0,))).reshape(GROUP, SPAN, width)
            heads = slice(group * GROUP, (group + 1) * GROUP)
            if window == 0:
                first = lax.broadcasted_iota(jnp.int32, sums.shape, 1) == 0
                sums = jnp.where(first, lone[heads][:, None, :], sums)
            mixed[heads, rows] = sums.astype(jnp.bfloat16)
            scores = following

    count = blocks * SPAN
    place = lax.broadcasted_iota(jnp.int32, (count, HEAD_DIM), 0)
    kept = place % SPAN == 0
    for block in range(blocks):
        kept = kept | ((place // SPAN == block) & (keep_ref[block] > 0))
    for head in range(HEADS):
        columns = head_columns(head)
        sums = contract(mixed[head], value_ref[:, columns], ((1,), (0,)))
        sums = jnp.where(kept, sums, 0.0)
        out_ref[:, columns] = pltpu.roll(sums, count - 1, 0).astype(jnp.bfloat16)


def attend(early, source, block, keep, folded, single, tokens, turned, w_value, late):
    requests, length, width = tokens.shape
    count = folded.shape[1]
    return pl.pallas_call(
        functools.partial(attend_kernel, early),
        out_shape=jax.ShapeDtypeStruct((count, w_value.shape[1]), jnp.bfloat16),
        in_specs=[SMEM_SPEC] * 3
        + [VMEM_SPEC] * 2
        + [ANY_SPEC] * 2
        + [VMEM_SPEC]
        + [ANY_SPEC] * len(late),
        out_specs=VMEM_SPEC,
        scratch_shapes=[
            pltpu.VMEM(tokens.shape, jnp.bfloat16),
            pltpu.VMEM(turned.shape, jnp.bfloat16),
            pltpu.VMEM(tokens.shape, jnp.bfloat16),
            pltpu.VMEM(folded.shape, jnp.bfloat16),
            pltpu.SemaphoreType.DMA((requests, 2)),
        ],
        compiler_params=pltpu.CompilerParams(vmem_limit_bytes=40 * MIB),
        cost_estimate=pl.CostEstimate(
            flops=2 * HEADS * count * width * (4 * length + HEAD_DIM),
            bytes_accessed=16 * MIB,
            transcendentals=HEADS * count * 2 * length,
        ),
        name="attend_windows",
    )(source, block, keep, folded, single, tokens, turned, w_value, *late)


def chip_ring(mesh):
    row = mesh.devices.reshape(-1, mesh.shape["seq"])[0]
    chips = list(range(len(row) // CORES))
    columns = [tuple(getattr(row[CORES * chip], "coords", (0, 0))[:2]) for chip in chips]
    if len(set(columns)) != 2:
        return chips
    up = [chip for chip in chips if columns[chip] == columns[0]]
    return up + [chip for chip in reversed(chips) if columns[chip] != columns[0]]


class Ring:
    def __init__(self, ring, slots):
        self.ring, self.slots = ring, slots
        self.size = len(ring)
        self.reach = (self.size - 1) // 2
        self.opposite = self.size % 2 == 0
        self.cut = slots // 2

    def turned(self, value, steps):
        size = self.size
        pairs = [
            (CORES * self.ring[i] + core, CORES * self.ring[(i + steps) % size] + core)
            for i in range(size)
            for core in range(CORES)
        ]
        return lax.ppermute(value, "seq", pairs)

    def swapped(self, value):
        return lax.ppermute(value, "seq", [(i, i ^ 1) for i in range(CORES * self.size)])

    def gather(self, stored, beside):
        slots = range(self.slots)
        waves = {1: [stored[slot : slot + 1] for slot in slots], -1: [stored[slot : slot + 1] for slot in slots]}
        early, late = [stored, self.swapped(stored)], []
        for step in range(self.reach):
            arrived = []
            for slot in slots:
                for way in (1, -1):
                    waves[way][slot] = self.turned(waves[way][slot], way)
                    arrived.append(waves[way][slot])
            if step == 0 and self.reach > 1:
                *arrived, beside = lax.optimization_barrier((*arrived, beside))
                for i, slot in enumerate(slots):
                    waves[1][slot], waves[-1][slot] = arrived[2 * i], arrived[2 * i + 1]
            early += arrived + [self.swapped(value) for value in arrived]
        if self.opposite:
            last = [self.turned(waves[1 if slot < self.cut else -1][slot], 1 if slot < self.cut else -1) for slot in slots]
            late = last + [self.swapped(value) for value in last]
        return early, late, beside

    def locate(self, owner, slot, here):
        order = jnp.asarray([self.ring.index(chip) for chip in range(self.size)], jnp.int32)

        def place_of(device):
            chips = jnp.arange(self.size)
            return jnp.sum(jnp.where((device // CORES)[..., None] == chips, order, 0), axis=-1)

        away = (place_of(here) - place_of(owner)) % self.size
        other = (owner % CORES != here % CORES).astype(jnp.int32)
        per_step = 2 * self.slots
        back = away > self.reach
        step = jnp.where(back, self.size - away, away)
        source = 2 + (step - 1) * 2 * per_step + other * per_step + 2 * slot + back
        if self.opposite:
            last = 2 + self.reach * 2 * per_step + other * self.slots + slot
            source = jnp.where(away == self.size // 2, last, source)
        return jnp.where(away == 0, other, source), jnp.where(away == 0, slot, 0)


def body(ring, queries, neighbours, w_key, w_value, retrieval_owner, retrieval_slot, doc_starts):
    devices = lax.axis_size("seq")
    here = lax.axis_index("seq")
    plan = Ring(ring, neighbours.shape[0])
    owner_slot = jnp.stack([retrieval_owner, retrieval_slot])
    before = lax.ppermute(owner_slot[:, -1:], "seq", [(i, i + 1) for i in range(devices - 1)])
    owner, slot = jnp.concatenate([before, owner_slot], 1).reshape(2, -1)
    source, block = plan.locate(owner, slot, here)
    blocks = doc_starts.shape[0]
    opening = (here == 0) & (jnp.arange(blocks) == 0)
    keep = ((doc_starts == 0) & jnp.logical_not(opening)).astype(jnp.int32)
    rows = jnp.concatenate([queries[-1:], queries[:-1]], 0)
    early, late, (folded, single, source, block, keep) = plan.gather(
        neighbours, (*fold(rows, w_key), source, block, keep)
    )
    tokens, turned = collect(source, block, early)
    return attend(len(early), source, block, keep, folded, single, tokens, turned, w_value, late)


def solution(mesh):
    return jax.shard_map(
        functools.partial(body, chip_ring(mesh)),
        mesh=mesh,
        in_specs=(
            P(("groups", "seq"), None),
            P(("groups", "seq"), None, None),
            P(),
            P(),
            P(("groups", "seq"), None),
            P(("groups", "seq"), None),
            P(("groups", "seq")),
        ),
        out_specs=P(("groups", "seq"), None),
        check_vma=False,
    )
```

```python
import functools
import math

import jax
import jax.numpy as jnp
from jax import lax
from jax.experimental import pallas as pl
from jax.experimental.pallas import tpu as pltpu
from jax.sharding import PartitionSpec as P

SPAN = 64
HEADS = 16
HEAD_DIM = 128
EPS = 1e-6
SCALE = math.log2(math.e) / math.sqrt(HEAD_DIM)
CORES = 2
GROUP = 4
MIB = 2**20


SMEM_SPEC = pl.BlockSpec(memory_space=pltpu.SMEM)
VMEM_SPEC = pl.BlockSpec(memory_space=pltpu.VMEM)
ANY_SPEC = pl.BlockSpec(memory_space=pl.ANY)


def contract(left, right, dims):
    return lax.dot_general(left, right, (dims, ((), ())), preferred_element_type=jnp.float32)


def head_columns(head):
    return slice(head * HEAD_DIM, (head + 1) * HEAD_DIM)


def fold_kernel(query_ref, key_hbm, folded_ref, single_ref, key, sems):
    groups = HEADS // GROUP

    def fetch(group):
        columns = slice(group * GROUP * HEAD_DIM, (group + 1) * GROUP * HEAD_DIM)
        return pltpu.make_async_copy(key_hbm.at[:, columns], key.at[:, columns], sems.at[group])

    for group in range(groups):
        fetch(group).start()
    for head in range(HEADS):
        if head % GROUP == 0:
            fetch(head // GROUP).wait()
        columns = head_columns(head)
        queries = pltpu.roll(query_ref[:, columns].astype(jnp.float32), 1, 0).astype(jnp.bfloat16)
        rows = contract(queries, key[:, columns], ((1,), (1,))) * SCALE
        single_ref[head : head + 1, :] = rows[:1]
        folded_ref[head] = rows.astype(jnp.bfloat16)


def fold(queries, w_key):
    count, width = queries.shape[0], w_key.shape[0]
    return pl.pallas_call(
        fold_kernel,
        out_shape=(
            jax.ShapeDtypeStruct((HEADS, count, width), jnp.bfloat16),
            jax.ShapeDtypeStruct((HEADS, width), jnp.float32),
        ),
        in_specs=[VMEM_SPEC, ANY_SPEC],
        out_specs=(VMEM_SPEC,) * 2,
        scratch_shapes=[
            pltpu.VMEM(w_key.shape, jnp.bfloat16),
            pltpu.SemaphoreType.DMA((HEADS // GROUP,)),
        ],
        compiler_params=pltpu.CompilerParams(vmem_limit_bytes=28 * MIB),
        cost_estimate=pl.CostEstimate(
            flops=2 * queries.size * width, bytes_accessed=8 * MIB, transcendentals=0
        ),
        name="fold_queries",
    )(queries, w_key)


def normalise(raw, tokens_ref, turned_ref):
    widened = raw.astype(jnp.float32)
    factor = lax.rsqrt(jnp.mean(widened * widened, axis=-1, keepdims=True) + EPS)
    scaled = widened * factor
    tokens_ref[...] = scaled.astype(jnp.bfloat16)
    turned_ref[...] = scaled.T.astype(jnp.bfloat16)


def among(stores, first, source, act):
    if len(stores) == 1:
        pl.when(source == first)(lambda: act(stores[0]))
        return
    half = len(stores) // 2
    pl.when(source < first + half)(lambda: among(stores[:half], first, source, act))
    pl.when(source >= first + half)(lambda: among(stores[half:], first + half, source, act))


def collect_kernel(source_ref, block_ref, *rest):
    *stores, tokens_ref, turned_ref, raw, sems = rest
    requests = raw.shape[0]

    def fetch(request, store):
        return pltpu.make_async_copy(store.at[block_ref[request]], raw.at[request], sems.at[request])

    def begin(request, carry):
        among(stores, 0, source_ref[request], lambda store: fetch(request, store).start())
        return carry

    def finish(request, carry):
        @pl.when(source_ref[request] < len(stores))
        def _():
            fetch(request, stores[0]).wait()
            normalise(raw[request], tokens_ref.at[request], turned_ref.at[request])

        return carry

    lax.fori_loop(0, requests, begin, 0)
    lax.fori_loop(0, requests, finish, 0)


def collect(source, block, stores):
    requests = source.shape[0]
    length, width = stores[0].shape[1:]
    return pl.pallas_call(
        collect_kernel,
        out_shape=(
            jax.ShapeDtypeStruct((requests, length, width), jnp.bfloat16),
            jax.ShapeDtypeStruct((requests, width, length), jnp.bfloat16),
        ),
        in_specs=[SMEM_SPEC] * 2 + [ANY_SPEC] * len(stores),
        out_specs=(VMEM_SPEC,) * 2,
        scratch_shapes=[
            pltpu.VMEM((requests, length, width), jnp.bfloat16),
            pltpu.SemaphoreType.DMA((requests,)),
        ],
        compiler_params=pltpu.CompilerParams(vmem_limit_bytes=16 * MIB),
        cost_estimate=pl.CostEstimate(flops=4 * MIB, bytes_accessed=8 * MIB, transcendentals=0),
        name="collect_early",
    )(source, block, *stores)


def weigh(scores):
    powers = jnp.exp2(scores - jnp.max(scores, axis=-1, keepdims=True))
    totals = jnp.sum(powers, axis=-1, keepdims=True)
    return (powers * (1.0 / totals)).astype(jnp.bfloat16)


def attend_kernel(
    early, source_ref, block_ref, keep_ref, folded_ref, single_ref, tokens_in, turned_in, value_ref, *rest
):
    *late, out_ref, tokens, turned, raw, scores, weights, mixed, sems = rest
    requests, length, width = raw.shape
    blocks = requests // 2 - 1
    count = blocks * SPAN
    rows_at_once = GROUP * SPAN

    def fetch_early(request):
        return (
            pltpu.make_async_copy(tokens_in.at[request], tokens.at[request], sems.at[request, 0]),
            pltpu.make_async_copy(turned_in.at[request], turned.at[request], sems.at[request, 1]),
        )

    def fetch_late(request, store):
        return pltpu.make_async_copy(store.at[block_ref[request]], raw.at[request], sems.at[request, 0])

    def begin(request, carry):
        @pl.when(source_ref[request] < early)
        def _():
            for copy in fetch_early(request):
                copy.start()

        if late:
            among(late, early, source_ref[request], lambda store: fetch_late(request, store).start())
        return carry

    def finish(request, carry):
        @pl.when(source_ref[request] < early)
        def _():
            for copy in fetch_early(request):
                copy.wait()

        if late:

            @pl.when(source_ref[request] >= early)
            def _():
                fetch_late(request, late[0]).wait()
                normalise(raw[request], tokens.at[request], turned.at[request])

        return carry

    lax.fori_loop(0, requests, begin, 0)
    lax.fori_loop(0, requests, finish, 0)

    def across(window):
        return jnp.concatenate([turned[2 * window], turned[2 * window + 1]], axis=1)

    def along(window):
        return tokens[2 * window : 2 * window + 2].reshape(2 * length, width)

    lone = weigh(contract(single_ref[...].astype(jnp.bfloat16), across(blocks), ((1,), (0,))))
    lone = contract(lone, along(blocks), ((1,), (0,)))

    place = lax.broadcasted_iota(jnp.int32, (count, HEAD_DIM), 0)
    kept = place % SPAN == 0
    for block in range(blocks):
        kept = kept | ((place // SPAN == block) & (keep_ref[block] > 0))

    units = [(group, window) for group in range(HEADS // GROUP) for window in range(blocks)]

    def score(unit):
        group, window = units[unit]
        heads, rows = slice(group * GROUP, (group + 1) * GROUP), slice(window * SPAN, (window + 1) * SPAN)
        taken = folded_ref[heads, rows].reshape(rows_at_once, width)
        scores[unit] = contract(taken, across(window), ((1,), (0,)))

    def soften(unit):
        for part in range(GROUP):
            rows = slice(part * SPAN, (part + 1) * SPAN)
            weights[unit, rows] = weigh(scores[unit, rows])

    def combine(unit):
        group, window = units[unit]
        heads, rows = slice(group * GROUP, (group + 1) * GROUP), slice(window * SPAN, (window + 1) * SPAN)
        sums = contract(weights[unit], along(window), ((1,), (0,))).reshape(GROUP, SPAN, width)
        if window == 0:
            first = lax.broadcasted_iota(jnp.int32, sums.shape, 1) == 0
            sums = jnp.where(first, lone[heads][:, None, :], sums)
        mixed[heads, rows] = sums.astype(jnp.bfloat16)

    def project(group):
        for head in range(group * GROUP, (group + 1) * GROUP):
            columns = head_columns(head)
            sums = contract(mixed[head], value_ref[:, columns], ((1,), (0,)))
            sums = jnp.where(kept, sums, 0.0)
            out_ref[:, columns] = pltpu.roll(sums, count - 1, 0).astype(jnp.bfloat16)

    for step in range(len(units) + 2):
        if step < len(units):
            score(step)
        if step >= 2:
            combine(step - 2)
        if 1 <= step <= len(units):
            soften(step - 1)
        if step >= 2 and units[step - 2][1] == blocks - 1:
            project(units[step - 2][0])


def attend(early, source, block, keep, folded, single, tokens, turned, w_value, late):
    requests, length, width = tokens.shape
    count = folded.shape[1]
    units = HEADS // GROUP * (count // SPAN)
    return pl.pallas_call(
        functools.partial(attend_kernel, early),
        out_shape=jax.ShapeDtypeStruct((count, w_value.shape[1]), jnp.bfloat16),
        in_specs=[SMEM_SPEC] * 3
        + [VMEM_SPEC] * 2
        + [ANY_SPEC] * 2
        + [VMEM_SPEC]
        + [ANY_SPEC] * len(late),
        out_specs=VMEM_SPEC,
        scratch_shapes=[
            pltpu.VMEM(tokens.shape, jnp.bfloat16),
            pltpu.VMEM(turned.shape, jnp.bfloat16),
            pltpu.VMEM(tokens.shape, jnp.bfloat16),
            pltpu.VMEM((units, GROUP * SPAN, 2 * length), jnp.float32),
            pltpu.VMEM((units, GROUP * SPAN, 2 * length), jnp.bfloat16),
            pltpu.VMEM(folded.shape, jnp.bfloat16),
            pltpu.SemaphoreType.DMA((requests, 2)),
        ],
        compiler_params=pltpu.CompilerParams(vmem_limit_bytes=32 * MIB),
        cost_estimate=pl.CostEstimate(
            flops=2 * HEADS * count * width * (4 * length + HEAD_DIM),
            bytes_accessed=16 * MIB,
            transcendentals=HEADS * count * 2 * length,
        ),
        name="attend_windows",
    )(source, block, keep, folded, single, tokens, turned, w_value, *late)


def chip_ring(mesh):
    row = mesh.devices.reshape(-1, mesh.shape["seq"])[0]
    chips = list(range(len(row) // CORES))
    columns = [tuple(getattr(row[CORES * chip], "coords", (0, 0))[:2]) for chip in chips]
    if len(set(columns)) != 2:
        return chips
    up = [chip for chip in chips if columns[chip] == columns[0]]
    return up + [chip for chip in reversed(chips) if columns[chip] != columns[0]]


class Ring:
    def __init__(self, ring, slots):
        self.ring, self.slots = ring, slots
        self.size = len(ring)
        self.reach = (self.size - 1) // 2
        self.opposite = self.size % 2 == 0
        self.cut = slots // 2

    def turned(self, value, steps):
        size = self.size
        pairs = [
            (CORES * self.ring[i] + core, CORES * self.ring[(i + steps) % size] + core)
            for i in range(size)
            for core in range(CORES)
        ]
        return lax.ppermute(value, "seq", pairs)

    def swapped(self, value):
        return lax.ppermute(value, "seq", [(i, i ^ 1) for i in range(CORES * self.size)])

    def gather(self, stored, beside):
        slots = range(self.slots)
        own = self.swapped(stored)
        early, late, swaps = [stored, own], [], []
        waves = {way: [stored[slot : slot + 1] for slot in slots] for way in (1, -1)}
        waiting = []
        for step in range(self.reach + self.opposite):
            last = step == self.reach
            for slot in slots:
                ways = (1, -1) if not last else (1,) if slot < self.cut else (-1,)
                sent = [waves[way][slot] for way in ways]
                if step == 0 and slot == 1:
                    *sent, own = lax.optimization_barrier((*sent, own))
                if step == 1 and slot == self.slots - 1:
                    *sent, beside = lax.optimization_barrier((*sent, beside))
                arrived = [self.turned(value, way) for value, way in zip(sent, ways)]
                for way, value in zip(ways, arrived):
                    waves[way][slot] = value
                if waiting:
                    *waiting, arrived[0] = lax.optimization_barrier((*waiting, arrived[0]))
                    swaps += [self.swapped(value) for value in waiting]
                    waves[ways[0]][slot] = arrived[0]
                waiting = arrived
                (late if last else early).append(arrived)
        swaps += [self.swapped(value) for value in waiting]
        stored, own, *early = early
        count = sum(map(len, early))
        early = [value for arrived in early for value in arrived]
        late = [value for arrived in late for value in arrived]
        return [stored, own, *early, *swaps[:count]], late + swaps[count:], beside

    def locate(self, owner, slot, here):
        order = jnp.asarray([self.ring.index(chip) for chip in range(self.size)], jnp.int32)

        def place_of(device):
            chips = jnp.arange(self.size)
            return jnp.sum(jnp.where((device // CORES)[..., None] == chips, order, 0), axis=-1)

        away = (place_of(here) - place_of(owner)) % self.size
        other = (owner % CORES != here % CORES).astype(jnp.int32)
        per_step = 2 * self.slots
        back = away > self.reach
        step = jnp.where(back, self.size - away, away)
        source = 2 + other * self.reach * per_step + (step - 1) * per_step + 2 * slot + back
        if self.opposite:
            last = 2 + CORES * self.reach * per_step + other * self.slots + slot
            source = jnp.where(away == self.size // 2, last, source)
        return jnp.where(away == 0, other, source), jnp.where(away == 0, slot, 0)


def body(ring, queries, neighbours, w_key, w_value, retrieval_owner, retrieval_slot, doc_starts):
    devices = lax.axis_size("seq")
    here = lax.axis_index("seq")
    plan = Ring(ring, neighbours.shape[0])
    owner_slot = jnp.stack([retrieval_owner, retrieval_slot])
    before = lax.ppermute(owner_slot[:, -1:], "seq", [(i, i + 1) for i in range(devices - 1)])
    owner, slot = jnp.concatenate([before, owner_slot], 1).reshape(2, -1)
    source, block = plan.locate(owner, slot, here)
    blocks = doc_starts.shape[0]
    opening = (here == 0) & (jnp.arange(blocks) == 0)
    keep = ((doc_starts == 0) & jnp.logical_not(opening)).astype(jnp.int32)
    early, late, (folded, single, source, block, keep) = plan.gather(
        neighbours, (*fold(queries, w_key), source, block, keep)
    )
    tokens, turned = collect(source, block, early)
    return attend(len(early), source, block, keep, folded, single, tokens, turned, w_value, late)


def solution(mesh):
    return jax.shard_map(
        functools.partial(body, chip_ring(mesh)),
        mesh=mesh,
        in_specs=(
            P(("groups", "seq"), None),
            P(("groups", "seq"), None, None),
            P(),
            P(),
            P(("groups", "seq"), None),
            P(("groups", "seq"), None),
            P(("groups", "seq")),
        ),
        out_specs=P(("groups", "seq"), None),
        check_vma=False,
    )
```

```python
import functools
import math

import jax
import jax.numpy as jnp
from jax import lax
from jax.experimental import pallas as pl
from jax.experimental.pallas import tpu as pltpu
from jax.sharding import PartitionSpec as P

SPAN = 64
HEADS = 16
HEAD_DIM = 128
EPS = 1e-6
SCALE = math.log2(math.e) / math.sqrt(HEAD_DIM)
CORES = 2
GROUP = 4
MIB = 2**20


SMEM_SPEC = pl.BlockSpec(memory_space=pltpu.SMEM)
VMEM_SPEC = pl.BlockSpec(memory_space=pltpu.VMEM)
ANY_SPEC = pl.BlockSpec(memory_space=pl.ANY)
HBM_SPEC = pl.BlockSpec(memory_space=pltpu.HBM)


def contract(left, right, dims):
    return lax.dot_general(left, right, (dims, ((), ())), preferred_element_type=jnp.float32)


def in_hbm(value):
    return pltpu.with_memory_space_constraint(value, pltpu.HBM)


def head_columns(head):
    return slice(head * HEAD_DIM, (head + 1) * HEAD_DIM)


def fold_kernel(query_hbm, key_hbm, folded_hbm, single_ref, query, key, folded, in_sems, out_sems):
    groups = HEADS // GROUP

    def fetch(group):
        columns = slice(group * GROUP * HEAD_DIM, (group + 1) * GROUP * HEAD_DIM)
        return (
            pltpu.make_async_copy(query_hbm.at[:, columns], query.at[:, columns], in_sems.at[group, 0]),
            pltpu.make_async_copy(key_hbm.at[:, columns], key.at[:, columns], in_sems.at[group, 1]),
        )

    def put(head):
        return pltpu.make_async_copy(folded.at[head], folded_hbm.at[head], out_sems.at[head])

    for group in range(groups):
        for copy in fetch(group):
            copy.start()
    for head in range(HEADS):
        if head % GROUP == 0:
            for copy in fetch(head // GROUP):
                copy.wait()
        columns = head_columns(head)
        queries = pltpu.roll(query[:, columns].astype(jnp.float32), 1, 0).astype(jnp.bfloat16)
        rows = contract(queries, key[:, columns], ((1,), (1,))) * SCALE
        single_ref[head : head + 1, :] = rows[:1]
        folded[head] = rows.astype(jnp.bfloat16)
        put(head).start()
    for head in range(HEADS):
        put(head).wait()


def fold(queries, w_key):
    count, width = queries.shape[0], w_key.shape[0]
    shape = (HEADS, count, width)
    return pl.pallas_call(
        fold_kernel,
        out_shape=(
            pltpu.HBM(shape, jnp.bfloat16),
            jax.ShapeDtypeStruct((HEADS, width), jnp.float32),
        ),
        in_specs=[HBM_SPEC] * 2,
        out_specs=(HBM_SPEC, VMEM_SPEC),
        scratch_shapes=[
            pltpu.VMEM(queries.shape, jnp.bfloat16),
            pltpu.VMEM(w_key.shape, jnp.bfloat16),
            pltpu.VMEM(shape, jnp.bfloat16),
            pltpu.SemaphoreType.DMA((HEADS // GROUP, 2)),
            pltpu.SemaphoreType.DMA((HEADS,)),
        ],
        compiler_params=pltpu.CompilerParams(vmem_limit_bytes=28 * MIB),
        cost_estimate=pl.CostEstimate(
            flops=2 * queries.size * width, bytes_accessed=12 * MIB, transcendentals=0
        ),
        name="fold_queries",
    )(in_hbm(queries), in_hbm(w_key))


def normalise(raw, tokens_ref):
    widened = raw.astype(jnp.float32)
    factor = lax.rsqrt(jnp.mean(widened * widened, axis=-1, keepdims=True) + EPS)
    tokens_ref[...] = (widened * factor).astype(jnp.bfloat16)


def among(stores, first, source, act):
    if len(stores) == 1:
        pl.when(source == first)(lambda: act(stores[0]))
        return
    half = len(stores) // 2
    pl.when(source < first + half)(lambda: among(stores[:half], first, source, act))
    pl.when(source >= first + half)(lambda: among(stores[half:], first + half, source, act))


def collect_kernel(first, source_ref, block_ref, *rest):
    *stores, tokens_ref, raw, sems = rest
    before_ref = stores.pop() if first else None
    requests = raw.shape[0]

    def fetch(request, store):
        return pltpu.make_async_copy(store.at[block_ref[request]], raw.at[request], sems.at[request])

    def begin(request, carry):
        among(stores, first, source_ref[request], lambda store: fetch(request, store).start())
        return carry

    def finish(request, carry):
        source = source_ref[request]
        here = (source >= first) & (source < first + len(stores))

        @pl.when(here)
        def _():
            fetch(request, stores[0]).wait()
            normalise(raw[request], tokens_ref.at[request])

        if before_ref is not None:

            @pl.when(jnp.logical_not(here))
            def _():
                tokens_ref[request] = before_ref[request]

        return carry

    lax.fori_loop(0, requests, begin, 0)
    lax.fori_loop(0, requests, finish, 0)


def collect(first, source, block, stores, before):
    requests = source.shape[0]
    length, width = stores[0].shape[1:]
    shape = (requests, length, width)
    before = [before] if first else []
    return pl.pallas_call(
        functools.partial(collect_kernel, first),
        out_shape=jax.ShapeDtypeStruct(shape, jnp.bfloat16),
        in_specs=[SMEM_SPEC] * 2 + [ANY_SPEC] * len(stores) + [VMEM_SPEC] * len(before),
        out_specs=VMEM_SPEC,
        scratch_shapes=[pltpu.VMEM(shape, jnp.bfloat16), pltpu.SemaphoreType.DMA((requests,))],
        compiler_params=pltpu.CompilerParams(vmem_limit_bytes=16 * MIB),
        cost_estimate=pl.CostEstimate(flops=4 * MIB, bytes_accessed=8 * MIB, transcendentals=0),
        name="collect_blocks",
    )(source, block, *stores, *before)


def weigh(scores):
    powers = jnp.exp2(scores - jnp.max(scores, axis=-1, keepdims=True))
    totals = jnp.sum(powers, axis=-1, keepdims=True)
    return (powers * (1.0 / totals)).astype(jnp.bfloat16)


def attend_kernel(
    early, source_ref, block_ref, keep_ref, folded_hbm, single_ref, tokens_in, value_ref, *rest
):
    *late, out_ref, tokens, raw, folded, scores, weights, mixed, sems, folded_sems = rest
    requests, length, width = raw.shape
    blocks = requests // 2 - 1
    count = blocks * SPAN
    rows_at_once = GROUP * SPAN

    def fetch_folded(group):
        heads = pl.ds(group * GROUP, GROUP)
        return pltpu.make_async_copy(folded_hbm.at[heads], folded.at[heads], folded_sems.at[group])

    def fetch_late(request, store):
        return pltpu.make_async_copy(store.at[block_ref[request]], raw.at[request], sems.at[request])

    def begin(request, carry):
        among(late, early, source_ref[request], lambda store: fetch_late(request, store).start())
        return carry

    def finish(request, carry):
        @pl.when(source_ref[request] < early)
        def _():
            tokens[request] = tokens_in[request]

        if late:

            @pl.when(source_ref[request] >= early)
            def _():
                fetch_late(request, late[0]).wait()
                normalise(raw[request], tokens.at[request])

        return carry

    if late:
        lax.fori_loop(0, requests, begin, 0)
    for group in range(HEADS // GROUP):
        fetch_folded(group).start()
    lax.fori_loop(0, requests, finish, 0)

    def along(window):
        return tokens[2 * window : 2 * window + 2].reshape(2 * length, width)

    lone = weigh(contract(single_ref[...].astype(jnp.bfloat16), along(blocks), ((1,), (1,))))
    lone = contract(lone, along(blocks), ((1,), (0,)))

    place = lax.broadcasted_iota(jnp.int32, (count, HEAD_DIM), 0)
    kept = place % SPAN == 0
    for block in range(blocks):
        kept = kept | ((place // SPAN == block) & (keep_ref[block] > 0))

    units = [(group, window) for group in range(HEADS // GROUP) for window in range(blocks)]

    def score(unit):
        group, window = units[unit]
        heads, rows = slice(group * GROUP, (group + 1) * GROUP), slice(window * SPAN, (window + 1) * SPAN)
        if window == 0:
            fetch_folded(group).wait()
        taken = folded[heads, rows].reshape(rows_at_once, width)
        scores[unit] = contract(taken, along(window), ((1,), (1,)))

    def soften(unit):
        for part in range(GROUP):
            rows = slice(part * SPAN, (part + 1) * SPAN)
            weights[unit, rows] = weigh(scores[unit, rows])

    def combine(unit):
        group, window = units[unit]
        heads, rows = slice(group * GROUP, (group + 1) * GROUP), slice(window * SPAN, (window + 1) * SPAN)
        sums = contract(weights[unit], along(window), ((1,), (0,))).reshape(GROUP, SPAN, width)
        if window == 0:
            first = lax.broadcasted_iota(jnp.int32, sums.shape, 1) == 0
            sums = jnp.where(first, lone[heads][:, None, :], sums)
        mixed[heads, rows] = sums.astype(jnp.bfloat16)

    def project(group):
        for head in range(group * GROUP, (group + 1) * GROUP):
            columns = head_columns(head)
            sums = contract(mixed[head], value_ref[:, columns], ((1,), (0,)))
            sums = jnp.where(kept, sums, 0.0)
            out_ref[:, columns] = pltpu.roll(sums, count - 1, 0).astype(jnp.bfloat16)

    for step in range(len(units) + 2):
        if step < len(units):
            score(step)
        if step >= 2:
            combine(step - 2)
        if 1 <= step <= len(units):
            soften(step - 1)
        if step >= 2 and units[step - 2][1] == blocks - 1:
            project(units[step - 2][0])


def attend(early, source, block, keep, folded, single, tokens, w_value, late):
    requests, length, width = tokens.shape
    count = folded.shape[1]
    units = HEADS // GROUP * (count // SPAN)
    return pl.pallas_call(
        functools.partial(attend_kernel, early),
        out_shape=jax.ShapeDtypeStruct((count, w_value.shape[1]), jnp.bfloat16),
        in_specs=[SMEM_SPEC] * 3
        + [HBM_SPEC]
        + [VMEM_SPEC] * 3
        + [ANY_SPEC] * len(late),
        out_specs=VMEM_SPEC,
        scratch_shapes=[
            pltpu.VMEM(tokens.shape, jnp.bfloat16),
            pltpu.VMEM(tokens.shape, jnp.bfloat16),
            pltpu.VMEM(folded.shape, jnp.bfloat16),
            pltpu.VMEM((units, GROUP * SPAN, 2 * length), jnp.float32),
            pltpu.VMEM((units, GROUP * SPAN, 2 * length), jnp.bfloat16),
            pltpu.VMEM(folded.shape, jnp.bfloat16),
            pltpu.SemaphoreType.DMA((requests,)),
            pltpu.SemaphoreType.DMA((HEADS // GROUP,)),
        ],
        compiler_params=pltpu.CompilerParams(vmem_limit_bytes=40 * MIB),
        cost_estimate=pl.CostEstimate(
            flops=2 * HEADS * count * width * (4 * length + HEAD_DIM),
            bytes_accessed=16 * MIB,
            transcendentals=HEADS * count * 2 * length,
        ),
        name="attend_windows",
    )(source, block, keep, in_hbm(folded), single, tokens, w_value, *late)


def chip_ring(mesh):
    row = mesh.devices.reshape(-1, mesh.shape["seq"])[0]
    chips = list(range(len(row) // CORES))
    columns = [tuple(getattr(row[CORES * chip], "coords", (0, 0))[:2]) for chip in chips]
    if len(set(columns)) != 2:
        return chips
    up = [chip for chip in chips if columns[chip] == columns[0]]
    return up + [chip for chip in reversed(chips) if columns[chip] != columns[0]]


class Ring:
    def __init__(self, ring):
        self.ring = ring
        self.size = len(ring)
        self.reach = (self.size - 1) // 2
        self.opposite = self.size % 2 == 0

    def turned(self, value, steps, cores=range(CORES)):
        size = self.size
        pairs = [
            (CORES * self.ring[i] + core, CORES * self.ring[(i + steps) % size] + core)
            for i in range(size)
            for core in cores
        ]
        return lax.ppermute(value, "seq", pairs)

    def swapped(self, value, cores=range(CORES)):
        return lax.ppermute(value, "seq", [(CORES * i + core, CORES * i + 1 - core) for i in range(self.size) for core in cores])

    def locate(self, owner, here):
        order = jnp.asarray([self.ring.index(chip) for chip in range(self.size)], jnp.int32)

        def place_of(device):
            chips = jnp.arange(self.size)
            return jnp.sum(jnp.where((device // CORES)[..., None] == chips, order, 0), axis=-1)

        away = (place_of(here) - place_of(owner)) % self.size
        back = away > self.reach
        arrival = jnp.where(back, 2 * (self.size - away), jnp.maximum(2 * away - 1, 0))
        if self.opposite:
            arrival = jnp.where(away == self.size // 2, 2 * self.reach + 1 + owner % CORES, arrival)
        return CORES * arrival + (owner % CORES != here % CORES)


def tie(values, others):
    values, others = lax.optimization_barrier((tuple(values), tuple(others)))
    return list(values), list(others)


def body(ring, queries, neighbours, w_key, w_value, retrieval_owner, retrieval_slot, doc_starts):
    devices = lax.axis_size("seq")
    here = lax.axis_index("seq")
    plan = Ring(ring)
    owner_slot = jnp.stack([retrieval_owner, retrieval_slot])
    before = lax.ppermute(owner_slot[:, -1:], "seq", [(i, i + 1) for i in range(devices - 1)])
    owner, slot = jnp.concatenate([before, owner_slot], 1).reshape(2, -1)
    source, block = plan.locate(owner, here), slot
    blocks = doc_starts.shape[0]
    opening = (here == 0) & (jnp.arange(blocks) == 0)
    keep = ((doc_starts == 0) & jnp.logical_not(opening)).astype(jnp.int32)
    beside = [*fold(queries, w_key), source, block, keep]
    ahead = behind = neighbours
    stores, tokens, done = [neighbours, plan.swapped(neighbours)], None, 0
    for step in range(plan.reach):
        if step == 1:
            (ahead, behind), beside = tie((ahead, behind), beside)
        if step == 2:
            done = 6
            tokens = collect(0, beside[2], beside[3], stores[:done], None)
            (ahead, behind), (tokens,) = tie((ahead, behind), (tokens,))
        ahead, behind = plan.turned(ahead, 1), plan.turned(behind, -1)
        stores += [ahead, plan.swapped(ahead), behind, plan.swapped(behind)]
    folded, single, source, block, keep = beside
    late = []
    if plan.opposite:
        ahead, behind = plan.turned(ahead, 1, (0,)), plan.turned(behind, -1, (1,))
        late = [ahead, plan.swapped(ahead, (0,)), behind, plan.swapped(behind, (1,))]
    tokens = collect(done, source, block, stores[done:], tokens)
    return attend(len(stores), source, block, keep, folded, single, tokens, w_value, late)


def solution(mesh):
    return jax.shard_map(
        functools.partial(body, chip_ring(mesh)),
        mesh=mesh,
        in_specs=(
            P(("groups", "seq"), None),
            P(("groups", "seq"), None, None),
            P(),
            P(),
            P(("groups", "seq"), None),
            P(("groups", "seq"), None),
            P(("groups", "seq")),
        ),
        out_specs=P(("groups", "seq"), None),
        check_vma=False,
    )
```

```python
import functools
import math

import jax
import jax.numpy as jnp
from jax import lax
from jax.experimental import pallas as pl
from jax.experimental.pallas import tpu as pltpu
from jax.sharding import PartitionSpec as P

SPAN = 64
HEADS = 16
HEAD_DIM = 128
EPS = 1e-6
SCALE = math.log2(math.e) / math.sqrt(HEAD_DIM)
CORES = 2
GROUP = 4
MIB = 2**20


SMEM_SPEC = pl.BlockSpec(memory_space=pltpu.SMEM)
VMEM_SPEC = pl.BlockSpec(memory_space=pltpu.VMEM)
ANY_SPEC = pl.BlockSpec(memory_space=pl.ANY)
HBM_SPEC = pl.BlockSpec(memory_space=pltpu.HBM)


def contract(left, right, dims):
    return lax.dot_general(left, right, (dims, ((), ())), preferred_element_type=jnp.float32)


def in_hbm(value):
    return pltpu.with_memory_space_constraint(value, pltpu.HBM)


def head_columns(head):
    return slice(head * HEAD_DIM, (head + 1) * HEAD_DIM)


def fold_kernel(query_hbm, key_hbm, folded_hbm, single_ref, query, key, folded, in_sems, out_sems):
    groups = HEADS // GROUP

    def fetch(group):
        columns = slice(group * GROUP * HEAD_DIM, (group + 1) * GROUP * HEAD_DIM)
        return (
            pltpu.make_async_copy(query_hbm.at[:, columns], query.at[:, columns], in_sems.at[group, 0]),
            pltpu.make_async_copy(key_hbm.at[:, columns], key.at[:, columns], in_sems.at[group, 1]),
        )

    def put(head):
        return pltpu.make_async_copy(folded.at[head], folded_hbm.at[head], out_sems.at[head])

    for group in range(groups):
        for copy in fetch(group):
            copy.start()
    for head in range(HEADS):
        if head % GROUP == 0:
            for copy in fetch(head // GROUP):
                copy.wait()
        columns = head_columns(head)
        queries = pltpu.roll(query[:, columns].astype(jnp.float32), 1, 0).astype(jnp.bfloat16)
        rows = contract(queries, key[:, columns], ((1,), (1,))) * SCALE
        single_ref[head : head + 1, :] = rows[:1]
        folded[head] = rows.astype(jnp.bfloat16)
        put(head).start()
    for head in range(HEADS):
        put(head).wait()


def fold(queries, w_key):
    count, width = queries.shape[0], w_key.shape[0]
    shape = (HEADS, count, width)
    return pl.pallas_call(
        fold_kernel,
        out_shape=(
            pltpu.HBM(shape, jnp.bfloat16),
            jax.ShapeDtypeStruct((HEADS, width), jnp.float32),
        ),
        in_specs=[HBM_SPEC] * 2,
        out_specs=(HBM_SPEC, VMEM_SPEC),
        scratch_shapes=[
            pltpu.VMEM(queries.shape, jnp.bfloat16),
            pltpu.VMEM(w_key.shape, jnp.bfloat16),
            pltpu.VMEM(shape, jnp.bfloat16),
            pltpu.SemaphoreType.DMA((HEADS // GROUP, 2)),
            pltpu.SemaphoreType.DMA((HEADS,)),
        ],
        compiler_params=pltpu.CompilerParams(vmem_limit_bytes=28 * MIB),
        cost_estimate=pl.CostEstimate(
            flops=2 * queries.size * width, bytes_accessed=12 * MIB, transcendentals=0
        ),
        name="fold_queries",
    )(in_hbm(queries), in_hbm(w_key))


def normalise(raw, tokens_ref):
    widened = raw.astype(jnp.float32)
    factor = lax.rsqrt(jnp.mean(widened * widened, axis=-1, keepdims=True) + EPS)
    tokens_ref[...] = (widened * factor).astype(jnp.bfloat16)


def among(stores, first, source, act):
    if len(stores) == 1:
        pl.when(source == first)(lambda: act(stores[0]))
        return
    half = len(stores) // 2
    pl.when(source < first + half)(lambda: among(stores[:half], first, source, act))
    pl.when(source >= first + half)(lambda: among(stores[half:], first + half, source, act))


def collect_kernel(first, source_ref, block_ref, *rest):
    *stores, tokens_ref, raw, sems = rest
    before_ref = stores.pop() if first else None
    requests = raw.shape[0]

    def fetch(request, store):
        return pltpu.make_async_copy(store.at[block_ref[request]], raw.at[request], sems.at[request])

    def begin(request, carry):
        among(stores, first, source_ref[request], lambda store: fetch(request, store).start())
        return carry

    def finish(request, carry):
        source = source_ref[request]
        here = (source >= first) & (source < first + len(stores))

        @pl.when(here)
        def _():
            fetch(request, stores[0]).wait()
            normalise(raw[request], tokens_ref.at[request])

        if before_ref is not None:

            @pl.when(jnp.logical_not(here))
            def _():
                tokens_ref[request] = before_ref[request]

        return carry

    lax.fori_loop(0, requests, begin, 0)
    lax.fori_loop(0, requests, finish, 0)


def collect(first, source, block, stores, before):
    requests = source.shape[0]
    length, width = stores[0].shape[1:]
    shape = (requests, length, width)
    before = [before] if first else []
    return pl.pallas_call(
        functools.partial(collect_kernel, first),
        out_shape=jax.ShapeDtypeStruct(shape, jnp.bfloat16),
        in_specs=[SMEM_SPEC] * 2 + [ANY_SPEC] * len(stores) + [VMEM_SPEC] * len(before),
        out_specs=VMEM_SPEC,
        scratch_shapes=[pltpu.VMEM(shape, jnp.bfloat16), pltpu.SemaphoreType.DMA((requests,))],
        compiler_params=pltpu.CompilerParams(vmem_limit_bytes=16 * MIB),
        cost_estimate=pl.CostEstimate(flops=4 * MIB, bytes_accessed=8 * MIB, transcendentals=0),
        name="collect_blocks",
    )(source, block, *stores, *before)


def weigh(scores):
    powers = jnp.exp2(scores - jnp.max(scores, axis=-1, keepdims=True))
    totals = jnp.sum(powers, axis=-1, keepdims=True)
    return (powers * (1.0 / totals)).astype(jnp.bfloat16)


def attend_kernel(
    early, source_ref, block_ref, keep_ref, folded_hbm, single_ref, tokens_in, value_ref, *rest
):
    *late, out_ref, tokens, raw, folded, scores, weights, mixed, sems, folded_sems = rest
    requests, length, width = raw.shape
    blocks = requests // 2 - 1
    count = blocks * SPAN
    rows_at_once = GROUP * SPAN

    def fetch_folded(group):
        heads = pl.ds(group * GROUP, GROUP)
        return pltpu.make_async_copy(folded_hbm.at[heads], folded.at[heads], folded_sems.at[group])

    def fetch_late(request, store):
        return pltpu.make_async_copy(store.at[block_ref[request]], raw.at[request], sems.at[request])

    def begin(request, carry):
        among(late, early, source_ref[request], lambda store: fetch_late(request, store).start())
        return carry

    def finish(request, carry):
        @pl.when(source_ref[request] < early)
        def _():
            tokens[request] = tokens_in[request]

        if late:

            @pl.when(source_ref[request] >= early)
            def _():
                fetch_late(request, late[0]).wait()
                normalise(raw[request], tokens.at[request])

        return carry

    if late:
        lax.fori_loop(0, requests, begin, 0)
    for group in range(HEADS // GROUP):
        fetch_folded(group).start()
    lax.fori_loop(0, requests, finish, 0)

    def along(window):
        return tokens[2 * window : 2 * window + 2].reshape(2 * length, width)

    lone = weigh(contract(single_ref[...].astype(jnp.bfloat16), along(blocks), ((1,), (1,))))
    lone = contract(lone, along(blocks), ((1,), (0,)))

    place = lax.broadcasted_iota(jnp.int32, (count, HEAD_DIM), 0)
    kept = place % SPAN == 0
    for block in range(blocks):
        kept = kept | ((place // SPAN == block) & (keep_ref[block] > 0))

    units = [(group, window) for group in range(HEADS // GROUP) for window in range(blocks)]

    def score(unit):
        group, window = units[unit]
        heads, rows = slice(group * GROUP, (group + 1) * GROUP), slice(window * SPAN, (window + 1) * SPAN)
        if window == 0:
            fetch_folded(group).wait()
        taken = folded[heads, rows].reshape(rows_at_once, width)
        scores[unit] = contract(taken, along(window), ((1,), (1,)))

    def soften(unit):
        for part in range(GROUP):
            rows = slice(part * SPAN, (part + 1) * SPAN)
            weights[unit, rows] = weigh(scores[unit, rows])

    def combine(unit):
        group, window = units[unit]
        heads, rows = slice(group * GROUP, (group + 1) * GROUP), slice(window * SPAN, (window + 1) * SPAN)
        sums = contract(weights[unit], along(window), ((1,), (0,))).reshape(GROUP, SPAN, width)
        if window == 0:
            first = lax.broadcasted_iota(jnp.int32, sums.shape, 1) == 0
            sums = jnp.where(first, lone[heads][:, None, :], sums)
        mixed[heads, rows] = sums.astype(jnp.bfloat16)

    def project(group):
        for head in range(group * GROUP, (group + 1) * GROUP):
            columns = head_columns(head)
            sums = contract(mixed[head], value_ref[:, columns], ((1,), (0,)))
            sums = jnp.where(kept, sums, 0.0)
            out_ref[:, columns] = pltpu.roll(sums, count - 1, 0).astype(jnp.bfloat16)

    for step in range(len(units) + 2):
        if step < len(units):
            score(step)
        if step >= 2:
            combine(step - 2)
        if 1 <= step <= len(units):
            soften(step - 1)
        if step >= 2 and units[step - 2][1] == blocks - 1:
            project(units[step - 2][0])


def attend(early, source, block, keep, folded, single, tokens, w_value, late):
    requests, length, width = tokens.shape
    count = folded.shape[1]
    units = HEADS // GROUP * (count // SPAN)
    return pl.pallas_call(
        functools.partial(attend_kernel, early),
        out_shape=jax.ShapeDtypeStruct((count, w_value.shape[1]), jnp.bfloat16),
        in_specs=[SMEM_SPEC] * 3
        + [HBM_SPEC]
        + [VMEM_SPEC] * 3
        + [ANY_SPEC] * len(late),
        out_specs=VMEM_SPEC,
        scratch_shapes=[
            pltpu.VMEM(tokens.shape, jnp.bfloat16),
            pltpu.VMEM(tokens.shape, jnp.bfloat16),
            pltpu.VMEM(folded.shape, jnp.bfloat16),
            pltpu.VMEM((units, GROUP * SPAN, 2 * length), jnp.float32),
            pltpu.VMEM((units, GROUP * SPAN, 2 * length), jnp.bfloat16),
            pltpu.VMEM(folded.shape, jnp.bfloat16),
            pltpu.SemaphoreType.DMA((requests,)),
            pltpu.SemaphoreType.DMA((HEADS // GROUP,)),
        ],
        compiler_params=pltpu.CompilerParams(vmem_limit_bytes=40 * MIB),
        cost_estimate=pl.CostEstimate(
            flops=2 * HEADS * count * width * (4 * length + HEAD_DIM),
            bytes_accessed=16 * MIB,
            transcendentals=HEADS * count * 2 * length,
        ),
        name="attend_windows",
    )(source, block, keep, in_hbm(folded), single, tokens, w_value, *late)


def chip_ring(mesh):
    row = mesh.devices.reshape(-1, mesh.shape["seq"])[0]
    chips = list(range(len(row) // CORES))
    columns = [tuple(getattr(row[CORES * chip], "coords", (0, 0))[:2]) for chip in chips]
    if len(set(columns)) != 2:
        return chips
    up = [chip for chip in chips if columns[chip] == columns[0]]
    return up + [chip for chip in reversed(chips) if columns[chip] != columns[0]]


class Ring:
    def __init__(self, ring, slots):
        self.ring, self.slots = ring, slots
        self.size = len(ring)
        self.reach = (self.size - 1) // 2
        self.opposite = self.size % 2 == 0

    def turned(self, value, steps):
        size = self.size
        pairs = [
            (CORES * self.ring[i] + core, CORES * self.ring[(i + steps) % size] + core)
            for i in range(size)
            for core in range(CORES)
        ]
        return lax.ppermute(value, "seq", pairs)

    def swapped(self, value):
        return lax.ppermute(value, "seq", [(i, i ^ 1) for i in range(CORES * self.size)])

    def ways(self, step, slot):
        if step < self.reach:
            return (1, -1)
        return (1,) if slot < self.slots // 2 else (-1,)

    def locate(self, owner, slot, here):
        order = jnp.asarray([self.ring.index(chip) for chip in range(self.size)], jnp.int32)

        def place_of(device):
            chips = jnp.arange(self.size)
            return jnp.sum(jnp.where((device // CORES)[..., None] == chips, order, 0), axis=-1)

        away = (place_of(here) - place_of(owner)) % self.size
        back = away > self.reach
        step = jnp.where(back, self.size - away, away) - 1
        arrival = 1 + 2 * self.slots * step + 2 * slot + back
        if self.opposite:
            arrival = jnp.where(away == self.size // 2, 1 + 2 * self.slots * self.reach + slot, arrival)
        arrival = jnp.where(away == 0, 0, arrival)
        return CORES * arrival + (owner % CORES != here % CORES), jnp.where(away == 0, slot, 0)


def after(values, others):
    return list(lax.optimization_barrier((tuple(values), tuple(others)))[0])


def body(ring, queries, neighbours, w_key, w_value, retrieval_owner, retrieval_slot, doc_starts):
    devices = lax.axis_size("seq")
    here = lax.axis_index("seq")
    plan = Ring(ring, neighbours.shape[0])
    owner_slot = jnp.stack([retrieval_owner, retrieval_slot])
    before = lax.ppermute(owner_slot[:, -1:], "seq", [(i, i + 1) for i in range(devices - 1)])
    owner, slot = jnp.concatenate([before, owner_slot], 1).reshape(2, -1)
    source, block = plan.locate(owner, slot, here)
    blocks = doc_starts.shape[0]
    opening = (here == 0) & (jnp.arange(blocks) == 0)
    keep = ((doc_starts == 0) & jnp.logical_not(opening)).astype(jnp.int32)
    slots = range(plan.slots)
    folded, single = fold(queries, w_key)
    own = plan.swapped(neighbours)
    waves = {(slot, way): neighbours[slot : slot + 1] for slot in slots for way in (1, -1)}
    stores, swaps, waves_in, marks = [neighbours], [own], [], []
    tokens, done = None, 0
    for step in range(plan.reach + plan.opposite):
        marks.append(len(stores))
        for slot in slots:
            ways = plan.ways(step, slot)
            sent = [waves[slot, way] for way in ways]
            if step == 0 and slot == 1:
                sent = after(sent, [own])
            if len(waves_in) > plan.slots:
                sent = after(sent, waves_in[-plan.slots - 1])
            if step == 1 and slot == plan.slots - 1:
                sent = after(sent, [folded, source, block, keep])
            arrived = [plan.turned(value, way) for value, way in zip(sent, ways)]
            for way, value in zip(ways, arrived):
                waves[slot, way] = value
            stores += arrived
            if waves_in:
                swaps += [plan.swapped(value) for value in after(waves_in[-1], arrived[:1])]
            waves_in.append(arrived)
    swaps += [plan.swapped(value) for value in waves_in[-1]]
    stores = [value for pair in zip(stores, swaps) for value in pair]
    early = CORES * (marks[-1] if plan.opposite else len(stores) // CORES)
    tokens = collect(0, source, block, stores[:early], None)
    return attend(early, source, block, keep, folded, single, tokens, w_value, stores[early:])


def solution(mesh):
    return jax.shard_map(
        functools.partial(body, chip_ring(mesh)),
        mesh=mesh,
        in_specs=(
            P(("groups", "seq"), None),
            P(("groups", "seq"), None, None),
            P(),
            P(),
            P(("groups", "seq"), None),
            P(("groups", "seq"), None),
            P(("groups", "seq")),
        ),
        out_specs=P(("groups", "seq"), None),
        check_vma=False,
    )
```

```python
import functools
import math

import jax
import jax.numpy as jnp
from jax import lax
from jax.experimental import pallas as pl
from jax.experimental.pallas import tpu as pltpu
from jax.sharding import PartitionSpec as P

SPAN = 64
HEADS = 16
HEAD_DIM = 128
EPS = 1e-6
SCALE = math.log2(math.e) / math.sqrt(HEAD_DIM)
CORES = 2
GROUP = 4
MIB = 2**20


SMEM_SPEC = pl.BlockSpec(memory_space=pltpu.SMEM)
VMEM_SPEC = pl.BlockSpec(memory_space=pltpu.VMEM)
HBM_SPEC = pl.BlockSpec(memory_space=pltpu.HBM)


def contract(left, right, dims):
    return lax.dot_general(left, right, (dims, ((), ())), preferred_element_type=jnp.float32)


def in_hbm(value):
    return pltpu.with_memory_space_constraint(value, pltpu.HBM)


def head_columns(head):
    return slice(head * HEAD_DIM, (head + 1) * HEAD_DIM)


def fold_kernel(query_hbm, key_hbm, folded_hbm, single_ref, query, key, folded, in_sems, out_sems):
    groups = HEADS // GROUP

    def fetch(group):
        columns = slice(group * GROUP * HEAD_DIM, (group + 1) * GROUP * HEAD_DIM)
        return (
            pltpu.make_async_copy(query_hbm.at[:, columns], query.at[:, columns], in_sems.at[group, 0]),
            pltpu.make_async_copy(key_hbm.at[:, columns], key.at[:, columns], in_sems.at[group, 1]),
        )

    def put(head):
        return pltpu.make_async_copy(folded.at[head], folded_hbm.at[head], out_sems.at[head])

    for group in range(groups):
        for copy in fetch(group):
            copy.start()
    for head in range(HEADS):
        if head % GROUP == 0:
            for copy in fetch(head // GROUP):
                copy.wait()
        columns = head_columns(head)
        queries = pltpu.roll(query[:, columns].astype(jnp.float32), 1, 0).astype(jnp.bfloat16)
        rows = contract(queries, key[:, columns], ((1,), (1,))) * SCALE
        single_ref[head : head + 1, :] = rows[:1]
        folded[head] = rows.astype(jnp.bfloat16)
        put(head).start()
    for head in range(HEADS):
        put(head).wait()


def fold(queries, w_key):
    count, width = queries.shape[0], w_key.shape[0]
    shape = (HEADS, count, width)
    return pl.pallas_call(
        fold_kernel,
        out_shape=(
            pltpu.HBM(shape, jnp.bfloat16),
            jax.ShapeDtypeStruct((HEADS, width), jnp.float32),
        ),
        in_specs=[HBM_SPEC] * 2,
        out_specs=(HBM_SPEC, VMEM_SPEC),
        scratch_shapes=[
            pltpu.VMEM(queries.shape, jnp.bfloat16),
            pltpu.VMEM(w_key.shape, jnp.bfloat16),
            pltpu.VMEM(shape, jnp.bfloat16),
            pltpu.SemaphoreType.DMA((HEADS // GROUP, 2)),
            pltpu.SemaphoreType.DMA((HEADS,)),
        ],
        compiler_params=pltpu.CompilerParams(vmem_limit_bytes=28 * MIB),
        cost_estimate=pl.CostEstimate(
            flops=2 * queries.size * width, bytes_accessed=12 * MIB, transcendentals=0
        ),
        name="fold_queries",
    )(in_hbm(queries), in_hbm(w_key))


def prepare_kernel(raw_ref, *slot_refs):
    for slot, slot_ref in enumerate(slot_refs):
        widened = raw_ref[slot].astype(jnp.float32)
        factor = lax.rsqrt(jnp.mean(widened * widened, axis=-1, keepdims=True) + EPS)
        slot_ref[0] = (widened * factor).astype(jnp.bfloat16)


def prepare(neighbours):
    slots, length, width = neighbours.shape
    return pl.pallas_call(
        prepare_kernel,
        out_shape=(jax.ShapeDtypeStruct((1, length, width), jnp.bfloat16),) * slots,
        in_specs=[VMEM_SPEC],
        out_specs=(VMEM_SPEC,) * slots,
        compiler_params=pltpu.CompilerParams(vmem_limit_bytes=8 * MIB),
        cost_estimate=pl.CostEstimate(flops=4 * neighbours.size, bytes_accessed=MIB, transcendentals=0),
        name="normalise_own",
    )(neighbours)


def among(stores, first, source, act):
    if len(stores) == 1:
        pl.when(source == first)(lambda: act(stores[0]))
        return
    half = len(stores) // 2
    pl.when(source < first + half)(lambda: among(stores[:half], first, source, act))
    pl.when(source >= first + half)(lambda: among(stores[half:], first + half, source, act))


def weigh(scores):
    powers = jnp.exp2(scores - jnp.max(scores, axis=-1, keepdims=True))
    totals = jnp.sum(powers, axis=-1, keepdims=True)
    return (powers * (1.0 / totals)).astype(jnp.bfloat16)


def attend_kernel(source_ref, block_ref, keep_ref, folded_hbm, single_ref, value_ref, *rest):
    *stores, out_ref, tokens, folded, scores, weights, mixed, sems, folded_sems = rest
    requests, length, width = tokens.shape
    blocks = requests // 2 - 1
    count = blocks * SPAN
    rows_at_once = GROUP * SPAN

    def fetch_folded(group):
        heads = pl.ds(group * GROUP, GROUP)
        return pltpu.make_async_copy(folded_hbm.at[heads], folded.at[heads], folded_sems.at[group])

    def fetch(request, store):
        return pltpu.make_async_copy(store.at[block_ref[request]], tokens.at[request], sems.at[request])

    def arrive(window):
        for request in (2 * window, 2 * window + 1):
            fetch(request, stores[0]).wait()

    for request in [2 * blocks, 2 * blocks + 1, *range(2 * blocks)]:
        among(stores, 0, source_ref[request], lambda store: fetch(request, store).start())
        if request == 1:
            fetch_folded(0).start()
    for group in range(1, HEADS // GROUP):
        fetch_folded(group).start()

    def along(window):
        return tokens[2 * window : 2 * window + 2].reshape(2 * length, width)

    arrive(blocks)
    lone = weigh(contract(single_ref[...].astype(jnp.bfloat16), along(blocks), ((1,), (1,))))
    lone = contract(lone, along(blocks), ((1,), (0,)))

    place = lax.broadcasted_iota(jnp.int32, (count, HEAD_DIM), 0)
    kept = place % SPAN == 0
    for block in range(blocks):
        kept = kept | ((place // SPAN == block) & (keep_ref[block] > 0))

    units = [(group, window) for group in range(HEADS // GROUP) for window in range(blocks)]

    def score(unit):
        group, window = units[unit]
        heads, rows = slice(group * GROUP, (group + 1) * GROUP), slice(window * SPAN, (window + 1) * SPAN)
        if group == 0:
            arrive(window)
        if window == 0:
            fetch_folded(group).wait()
        taken = folded[heads, rows].reshape(rows_at_once, width)
        scores[unit] = contract(taken, along(window), ((1,), (1,)))

    def soften(unit):
        for part in range(GROUP):
            rows = slice(part * SPAN, (part + 1) * SPAN)
            weights[unit, rows] = weigh(scores[unit, rows])

    def combine(unit):
        group, window = units[unit]
        heads, rows = slice(group * GROUP, (group + 1) * GROUP), slice(window * SPAN, (window + 1) * SPAN)
        sums = contract(weights[unit], along(window), ((1,), (0,))).reshape(GROUP, SPAN, width)
        if window == 0:
            first = lax.broadcasted_iota(jnp.int32, sums.shape, 1) == 0
            sums = jnp.where(first, lone[heads][:, None, :], sums)
        mixed[heads, rows] = sums.astype(jnp.bfloat16)

    def project(group):
        for head in range(group * GROUP, (group + 1) * GROUP):
            columns = head_columns(head)
            sums = contract(mixed[head], value_ref[:, columns], ((1,), (0,)))
            sums = jnp.where(kept, sums, 0.0)
            out_ref[:, columns] = pltpu.roll(sums, count - 1, 0).astype(jnp.bfloat16)

    for step in range(len(units) + 2):
        if step < len(units):
            score(step)
        if step >= 2:
            combine(step - 2)
        if 1 <= step <= len(units):
            soften(step - 1)
        if step >= 2 and units[step - 2][1] == blocks - 1:
            project(units[step - 2][0])


def attend(source, block, keep, folded, single, w_value, stores):
    requests = source.shape[0]
    length, width = stores[0].shape[1:]
    count = folded.shape[1]
    units = HEADS // GROUP * (count // SPAN)
    return pl.pallas_call(
        attend_kernel,
        out_shape=jax.ShapeDtypeStruct((count, w_value.shape[1]), jnp.bfloat16),
        in_specs=[SMEM_SPEC] * 3 + [HBM_SPEC] + [VMEM_SPEC] * 2 + [HBM_SPEC] * len(stores),
        out_specs=VMEM_SPEC,
        scratch_shapes=[
            pltpu.VMEM((requests, length, width), jnp.bfloat16),
            pltpu.VMEM(folded.shape, jnp.bfloat16),
            pltpu.VMEM((units, GROUP * SPAN, 2 * length), jnp.float32),
            pltpu.VMEM((units, GROUP * SPAN, 2 * length), jnp.bfloat16),
            pltpu.VMEM(folded.shape, jnp.bfloat16),
            pltpu.SemaphoreType.DMA((requests,)),
            pltpu.SemaphoreType.DMA((HEADS // GROUP,)),
        ],
        compiler_params=pltpu.CompilerParams(vmem_limit_bytes=40 * MIB),
        cost_estimate=pl.CostEstimate(
            flops=2 * HEADS * count * width * (4 * length + HEAD_DIM),
            bytes_accessed=16 * MIB,
            transcendentals=HEADS * count * 2 * length,
        ),
        name="attend_windows",
    )(source, block, keep, in_hbm(folded), single, w_value, *map(in_hbm, stores))


def chip_ring(mesh):
    row = mesh.devices.reshape(-1, mesh.shape["seq"])[0]
    chips = list(range(len(row) // CORES))
    columns = [tuple(getattr(row[CORES * chip], "coords", (0, 0))[:2]) for chip in chips]
    if len(set(columns)) != 2:
        return chips
    up = [chip for chip in chips if columns[chip] == columns[0]]
    return up + [chip for chip in reversed(chips) if columns[chip] != columns[0]]


def body(ring, queries, neighbours, w_key, w_value, retrieval_owner, retrieval_slot, doc_starts):
    devices = lax.axis_size("seq")
    here = lax.axis_index("seq")
    along = [CORES * chip + core for chip in ring for core in range(CORES)]
    orders = [along[:: 1 if slot % 2 == 0 else -1] for slot in range(neighbours.shape[0])]
    stores = [
        lax.all_gather(rows, "seq", axis=0, tiled=True, axis_index_groups=[order])
        for rows, order in zip(prepare(neighbours), orders)
    ]
    owner_slot = jnp.stack([retrieval_owner, retrieval_slot])
    before = lax.ppermute(owner_slot[:, -1:], "seq", [(i, i + 1) for i in range(devices - 1)])
    owner, source = jnp.concatenate([before, owner_slot], 1).reshape(2, -1)
    block = jnp.zeros_like(owner)
    for slot, order in enumerate(orders):
        places = jnp.asarray([order.index(device) for device in range(devices)], jnp.int32)
        found = jnp.sum(jnp.where(owner[:, None] == jnp.arange(devices), places, 0), axis=-1)
        block = jnp.where(source == slot, found, block)
    blocks = doc_starts.shape[0]
    opening = (here == 0) & (jnp.arange(blocks) == 0)
    keep = ((doc_starts == 0) & jnp.logical_not(opening)).astype(jnp.int32)
    folded, single = fold(queries, w_key)
    return attend(source, block, keep, folded, single, w_value, stores)


def solution(mesh):
    return jax.shard_map(
        functools.partial(body, chip_ring(mesh)),
        mesh=mesh,
        in_specs=(
            P(("groups", "seq"), None),
            P(("groups", "seq"), None, None),
            P(),
            P(),
            P(("groups", "seq"), None),
            P(("groups", "seq"), None),
            P(("groups", "seq")),
        ),
        out_specs=P(("groups", "seq"), None),
        check_vma=False,
    )
```

```python
import functools
import math

import jax
import jax.numpy as jnp
from jax import lax
from jax.experimental import pallas as pl
from jax.experimental.pallas import tpu as pltpu
from jax.sharding import PartitionSpec as P

SPAN = 64
HEADS = 16
HEAD_DIM = 128
EPS = 1e-6
SCALE = math.log2(math.e) / math.sqrt(HEAD_DIM)
CORES = 2
GROUP = 4
MIB = 2**20


SMEM_SPEC = pl.BlockSpec(memory_space=pltpu.SMEM)
VMEM_SPEC = pl.BlockSpec(memory_space=pltpu.VMEM)
ANY_SPEC = pl.BlockSpec(memory_space=pl.ANY)
HBM_SPEC = pl.BlockSpec(memory_space=pltpu.HBM)


def contract(left, right, dims):
    return lax.dot_general(left, right, (dims, ((), ())), preferred_element_type=jnp.float32)


def in_hbm(value):
    return pltpu.with_memory_space_constraint(value, pltpu.HBM)


def head_columns(head):
    return slice(head * HEAD_DIM, (head + 1) * HEAD_DIM)


def fold_kernel(query_hbm, key_hbm, folded_hbm, single_ref, query, key, folded, in_sems, out_sems):
    groups = HEADS // GROUP

    def fetch(group):
        columns = slice(group * GROUP * HEAD_DIM, (group + 1) * GROUP * HEAD_DIM)
        return (
            pltpu.make_async_copy(query_hbm.at[:, columns], query.at[:, columns], in_sems.at[group, 0]),
            pltpu.make_async_copy(key_hbm.at[:, columns], key.at[:, columns], in_sems.at[group, 1]),
        )

    def put(head):
        return pltpu.make_async_copy(folded.at[head], folded_hbm.at[head], out_sems.at[head])

    for group in range(groups):
        for copy in fetch(group):
            copy.start()
    for head in range(HEADS):
        if head % GROUP == 0:
            for copy in fetch(head // GROUP):
                copy.wait()
        columns = head_columns(head)
        queries = pltpu.roll(query[:, columns].astype(jnp.float32), 1, 0).astype(jnp.bfloat16)
        rows = contract(queries, key[:, columns], ((1,), (1,))) * SCALE
        single_ref[head : head + 1, :] = rows[:1]
        folded[head] = rows.astype(jnp.bfloat16)
        put(head).start()
    for head in range(HEADS):
        put(head).wait()


def fold(queries, w_key):
    count, width = queries.shape[0], w_key.shape[0]
    shape = (HEADS, count, width)
    return pl.pallas_call(
        fold_kernel,
        out_shape=(
            pltpu.HBM(shape, jnp.bfloat16),
            jax.ShapeDtypeStruct((HEADS, width), jnp.float32),
        ),
        in_specs=[HBM_SPEC] * 2,
        out_specs=(HBM_SPEC, VMEM_SPEC),
        scratch_shapes=[
            pltpu.VMEM(queries.shape, jnp.bfloat16),
            pltpu.VMEM(w_key.shape, jnp.bfloat16),
            pltpu.VMEM(shape, jnp.bfloat16),
            pltpu.SemaphoreType.DMA((HEADS // GROUP, 2)),
            pltpu.SemaphoreType.DMA((HEADS,)),
        ],
        compiler_params=pltpu.CompilerParams(vmem_limit_bytes=28 * MIB),
        cost_estimate=pl.CostEstimate(
            flops=2 * queries.size * width, bytes_accessed=12 * MIB, transcendentals=0
        ),
        name="fold_queries",
    )(in_hbm(queries), in_hbm(w_key))


def normalise(raw, tokens_ref):
    widened = raw.astype(jnp.float32)
    factor = lax.rsqrt(jnp.mean(widened * widened, axis=-1, keepdims=True) + EPS)
    tokens_ref[...] = (widened * factor).astype(jnp.bfloat16)


def among(stores, first, source, act):
    if len(stores) == 1:
        pl.when(source == first)(lambda: act(stores[0]))
        return
    half = len(stores) // 2
    pl.when(source < first + half)(lambda: among(stores[:half], first, source, act))
    pl.when(source >= first + half)(lambda: among(stores[half:], first + half, source, act))


def locate(request, plan_refs, size):
    here_ref, place_ref, before_ref, owner_ref, slot_ref = plan_refs
    window, part = request // 2, request % 2
    own = jnp.maximum(window - 1, 0)
    owner = jnp.where(window == 0, before_ref[0, part], owner_ref[own, part])
    slot = jnp.where(window == 0, before_ref[1, part], slot_ref[own, part])
    here = here_ref[0]
    away = place_ref[here // CORES] - place_ref[owner // CORES]
    away = jnp.where(away < 0, away + size, away)
    reach = (size - 1) // 2
    core, opposite = owner % CORES, size - reach - 1
    holder = jnp.where((away == 0) | ((away > reach) & (away <= opposite)), core, jnp.where(away <= reach, 0, 1))
    step = jnp.where(away <= opposite, away, size - away)
    arrival = jnp.where(away == 0, 0, 2 * step - 1 + jnp.where(core == holder, 0, 1))
    return CORES * arrival + jnp.where(holder == here % CORES, 0, 1), slot


def collect_kernel(first, size, *refs):
    plan_refs, (*stores, tokens_ref, raw, sems) = refs[:5], refs[5:]
    before_ref = stores.pop() if first else None
    requests = raw.shape[0]

    def fetch(request, store, block):
        return pltpu.make_async_copy(store.at[block], raw.at[request], sems.at[request])

    def begin(request, carry):
        source, block = locate(request, plan_refs, size)
        among(stores, first, source, lambda store: fetch(request, store, block).start())
        return carry

    def finish(request, carry):
        source, block = locate(request, plan_refs, size)
        here = (source >= first) & (source < first + len(stores))

        @pl.when(here)
        def _():
            fetch(request, stores[0], block).wait()
            normalise(raw[request], tokens_ref.at[request])

        if before_ref is not None:

            @pl.when(jnp.logical_not(here))
            def _():
                tokens_ref[request] = before_ref[request]

        return carry

    lax.fori_loop(0, requests, begin, 0)
    lax.fori_loop(0, requests, finish, 0)


def collect(first, size, plan, stores, before):
    requests = 2 * plan[3].shape[0] + 2
    length, width = stores[0].shape[1:]
    shape = (requests, length, width)
    before = [before] if first else []
    return pl.pallas_call(
        functools.partial(collect_kernel, first, size),
        out_shape=jax.ShapeDtypeStruct(shape, jnp.bfloat16),
        in_specs=[SMEM_SPEC] * 5 + [ANY_SPEC] * len(stores) + [VMEM_SPEC] * len(before),
        out_specs=VMEM_SPEC,
        scratch_shapes=[pltpu.VMEM(shape, jnp.bfloat16), pltpu.SemaphoreType.DMA((requests,))],
        compiler_params=pltpu.CompilerParams(vmem_limit_bytes=16 * MIB),
        cost_estimate=pl.CostEstimate(flops=4 * MIB, bytes_accessed=8 * MIB, transcendentals=0),
        name="collect_blocks",
    )(*plan, *stores, *before)


def weigh(scores):
    powers = jnp.exp2(scores - jnp.max(scores, axis=-1, keepdims=True))
    totals = jnp.sum(powers, axis=-1, keepdims=True)
    return (powers * (1.0 / totals)).astype(jnp.bfloat16)


def attend_kernel(early, size, *refs):
    plan_refs, (starts_ref, folded_hbm, single_ref, tokens_in, value_ref, *rest) = refs[:5], refs[5:]
    *late, out_ref, tokens, raw, folded, scores, weights, mixed, sems, folded_sems = rest
    requests, length, width = raw.shape
    blocks = requests // 2 - 1
    count = blocks * SPAN
    rows_at_once = GROUP * SPAN

    def fetch_folded(group):
        heads = pl.ds(group * GROUP, GROUP)
        return pltpu.make_async_copy(folded_hbm.at[heads], folded.at[heads], folded_sems.at[group])

    def fetch_late(request, store, block):
        return pltpu.make_async_copy(store.at[block], raw.at[request], sems.at[request])

    def begin(request, carry):
        source, block = locate(request, plan_refs, size)
        among(late, early, source, lambda store: fetch_late(request, store, block).start())
        return carry

    def finish(request, carry):
        source, block = locate(request, plan_refs, size)

        @pl.when(source < early)
        def _():
            tokens[request] = tokens_in[request]

        if late:

            @pl.when(source >= early)
            def _():
                fetch_late(request, late[0], block).wait()
                normalise(raw[request], tokens.at[request])

        return carry

    if late:
        lax.fori_loop(0, requests, begin, 0)
    for group in range(HEADS // GROUP):
        fetch_folded(group).start()
    lax.fori_loop(0, requests, finish, 0)

    def along(window):
        return tokens[2 * window : 2 * window + 2].reshape(2 * length, width)

    lone = weigh(contract(single_ref[...].astype(jnp.bfloat16), along(blocks), ((1,), (1,))))
    lone = contract(lone, along(blocks), ((1,), (0,)))

    place = lax.broadcasted_iota(jnp.int32, (count, HEAD_DIM), 0)
    kept = place % SPAN == 0
    for block in range(blocks):
        fresh = starts_ref[block] == 0
        if block == 0:
            fresh = fresh & (plan_refs[0][0] > 0)
        kept = kept | ((place // SPAN == block) & fresh)

    units = [(group, window) for group in range(HEADS // GROUP) for window in range(blocks)]

    def score(unit):
        group, window = units[unit]
        heads, rows = slice(group * GROUP, (group + 1) * GROUP), slice(window * SPAN, (window + 1) * SPAN)
        if window == 0:
            fetch_folded(group).wait()
        taken = folded[heads, rows].reshape(rows_at_once, width)
        scores[unit] = contract(taken, along(window), ((1,), (1,)))

    def soften(unit):
        for part in range(GROUP):
            rows = slice(part * SPAN, (part + 1) * SPAN)
            weights[unit, rows] = weigh(scores[unit, rows])

    def combine(unit):
        group, window = units[unit]
        heads, rows = slice(group * GROUP, (group + 1) * GROUP), slice(window * SPAN, (window + 1) * SPAN)
        sums = contract(weights[unit], along(window), ((1,), (0,))).reshape(GROUP, SPAN, width)
        if window == 0:
            first = lax.broadcasted_iota(jnp.int32, sums.shape, 1) == 0
            sums = jnp.where(first, lone[heads][:, None, :], sums)
        mixed[heads, rows] = sums.astype(jnp.bfloat16)

    def project(group):
        for head in range(group * GROUP, (group + 1) * GROUP):
            columns = head_columns(head)
            sums = contract(mixed[head], value_ref[:, columns], ((1,), (0,)))
            sums = jnp.where(kept, sums, 0.0)
            out_ref[:, columns] = pltpu.roll(sums, count - 1, 0).astype(jnp.bfloat16)

    for step in range(len(units) + 2):
        if step < len(units):
            score(step)
        if step >= 2:
            combine(step - 2)
        if 1 <= step <= len(units):
            soften(step - 1)
        if step >= 2 and units[step - 2][1] == blocks - 1:
            project(units[step - 2][0])


def attend(early, size, plan, doc_starts, folded, single, tokens, w_value, late):
    requests, length, width = tokens.shape
    count = folded.shape[1]
    units = HEADS // GROUP * (count // SPAN)
    return pl.pallas_call(
        functools.partial(attend_kernel, early, size),
        out_shape=jax.ShapeDtypeStruct((count, w_value.shape[1]), jnp.bfloat16),
        in_specs=[SMEM_SPEC] * 6
        + [HBM_SPEC]
        + [VMEM_SPEC] * 3
        + [ANY_SPEC] * len(late),
        out_specs=VMEM_SPEC,
        scratch_shapes=[
            pltpu.VMEM(tokens.shape, jnp.bfloat16),
            pltpu.VMEM(tokens.shape, jnp.bfloat16),
            pltpu.VMEM(folded.shape, jnp.bfloat16),
            pltpu.VMEM((units, GROUP * SPAN, 2 * length), jnp.float32),
            pltpu.VMEM((units, GROUP * SPAN, 2 * length), jnp.bfloat16),
            pltpu.VMEM(folded.shape, jnp.bfloat16),
            pltpu.SemaphoreType.DMA((requests,)),
            pltpu.SemaphoreType.DMA((HEADS // GROUP,)),
        ],
        compiler_params=pltpu.CompilerParams(vmem_limit_bytes=40 * MIB),
        cost_estimate=pl.CostEstimate(
            flops=2 * HEADS * count * width * (4 * length + HEAD_DIM),
            bytes_accessed=16 * MIB,
            transcendentals=HEADS * count * 2 * length,
        ),
        name="attend_windows",
    )(*plan, doc_starts, in_hbm(folded), single, tokens, w_value, *late)


def chip_ring(mesh):
    row = mesh.devices.reshape(-1, mesh.shape["seq"])[0]
    chips = list(range(len(row) // CORES))
    columns = [tuple(getattr(row[CORES * chip], "coords", (0, 0))[:2]) for chip in chips]
    if len(set(columns)) != 2:
        return chips
    up = [chip for chip in chips if columns[chip] == columns[0]]
    return up + [chip for chip in reversed(chips) if columns[chip] != columns[0]]


def after(values, others):
    return list(lax.optimization_barrier((tuple(values), tuple(others)))[0])


def body(ring, queries, neighbours, w_key, w_value, retrieval_owner, retrieval_slot, doc_starts):
    devices = lax.axis_size("seq")
    size = len(ring)
    reach = (size - 1) // 2

    ways = [
        (CORES * ring[i] + core, CORES * ring[(i + way) % size] + core)
        for i in range(size)
        for core, way in enumerate((1, -1))
    ]
    onwards = functools.partial(lax.ppermute, axis_name="seq", perm=ways)
    swapped = functools.partial(lax.ppermute, axis_name="seq", perm=[(i, i ^ 1) for i in range(devices)])

    folded, single = fold(queries, w_key)
    owner_slot = jnp.stack([retrieval_owner[-1], retrieval_slot[-1]])
    before = lax.ppermute(owner_slot, "seq", [(i, i + 1) for i in range(devices - 1)])
    places = jnp.asarray([ring.index(chip) for chip in range(size)], jnp.int32)
    plan = [lax.axis_index("seq").reshape(1), places, before, retrieval_owner, retrieval_slot]

    chains = [neighbours, swapped(neighbours)]
    stores, tokens, done = list(chains), None, 0
    for step in range(reach):
        for chain in range(2):
            sent = [chains[chain]]
            if step == 1 and chain == 0:
                sent = after(sent, [folded, single])
            if step == reach - 1 and chain == 1 and reach > 1:
                done = CORES * (2 * reach - 3)
                tokens = collect(0, size, plan, stores[:done], None)
                sent = after(sent, [tokens])
            chains[chain] = onwards(sent[0])
            stores += [chains[chain], swapped(chains[chain])]
    tokens = collect(done, size, plan, stores[done:], tokens)
    late = []
    if size % 2 == 0:
        last = onwards(chains[0])
        late = [last, swapped(after([last], [tokens])[0])]
    return attend(len(stores), size, plan, doc_starts, folded, single, tokens, w_value, late)


def solution(mesh):
    return jax.shard_map(
        functools.partial(body, chip_ring(mesh)),
        mesh=mesh,
        in_specs=(
            P(("groups", "seq"), None),
            P(("groups", "seq"), None, None),
            P(),
            P(),
            P(("groups", "seq"), None),
            P(("groups", "seq"), None),
            P(("groups", "seq")),
        ),
        out_specs=P(("groups", "seq"), None),
        check_vma=False,
    )
```

```python
import functools
import math

import jax
import jax.numpy as jnp
from jax import lax
from jax.experimental import pallas as pl
from jax.experimental.pallas import tpu as pltpu
from jax.sharding import PartitionSpec as P

SPAN = 64
HEADS = 16
HEAD_DIM = 128
EPS = 1e-6
SCALE = math.log2(math.e) / math.sqrt(HEAD_DIM)
CORES = 2
GROUP = 4
MIB = 2**20


SMEM_SPEC = pl.BlockSpec(memory_space=pltpu.SMEM)
VMEM_SPEC = pl.BlockSpec(memory_space=pltpu.VMEM)
ANY_SPEC = pl.BlockSpec(memory_space=pl.ANY)
HBM_SPEC = pl.BlockSpec(memory_space=pltpu.HBM)


def contract(left, right, dims):
    return lax.dot_general(left, right, (dims, ((), ())), preferred_element_type=jnp.float32)


def in_hbm(value):
    return pltpu.with_memory_space_constraint(value, pltpu.HBM)


def head_columns(head):
    return slice(head * HEAD_DIM, (head + 1) * HEAD_DIM)


def fold_kernel(query_hbm, key_hbm, folded_hbm, single_ref, query, key, folded, in_sems, out_sems):
    groups = HEADS // GROUP

    def fetch(group):
        columns = slice(group * GROUP * HEAD_DIM, (group + 1) * GROUP * HEAD_DIM)
        return (
            pltpu.make_async_copy(query_hbm.at[:, columns], query.at[:, columns], in_sems.at[group, 0]),
            pltpu.make_async_copy(key_hbm.at[:, columns], key.at[:, columns], in_sems.at[group, 1]),
        )

    def put(head):
        return pltpu.make_async_copy(folded.at[head], folded_hbm.at[head], out_sems.at[head])

    for group in range(groups):
        for copy in fetch(group):
            copy.start()
    for head in range(HEADS):
        if head % GROUP == 0:
            for copy in fetch(head // GROUP):
                copy.wait()
        columns = head_columns(head)
        queries = pltpu.roll(query[:, columns].astype(jnp.float32), 1, 0).astype(jnp.bfloat16)
        rows = contract(queries, key[:, columns], ((1,), (1,))) * SCALE
        single_ref[head : head + 1, :] = rows[:1]
        folded[head] = rows.astype(jnp.bfloat16)
        put(head).start()
    for head in range(HEADS):
        put(head).wait()


def fold(queries, w_key):
    count, width = queries.shape[0], w_key.shape[0]
    shape = (HEADS, count, width)
    return pl.pallas_call(
        fold_kernel,
        out_shape=(
            pltpu.HBM(shape, jnp.bfloat16),
            jax.ShapeDtypeStruct((HEADS, width), jnp.float32),
        ),
        in_specs=[HBM_SPEC] * 2,
        out_specs=(HBM_SPEC, VMEM_SPEC),
        scratch_shapes=[
            pltpu.VMEM(queries.shape, jnp.bfloat16),
            pltpu.VMEM(w_key.shape, jnp.bfloat16),
            pltpu.VMEM(shape, jnp.bfloat16),
            pltpu.SemaphoreType.DMA((HEADS // GROUP, 2)),
            pltpu.SemaphoreType.DMA((HEADS,)),
        ],
        compiler_params=pltpu.CompilerParams(vmem_limit_bytes=28 * MIB),
        cost_estimate=pl.CostEstimate(
            flops=2 * queries.size * width, bytes_accessed=12 * MIB, transcendentals=0
        ),
        name="fold_queries",
    )(in_hbm(queries), in_hbm(w_key))


def normalise(raw, tokens_ref):
    widened = raw.astype(jnp.float32)
    factor = lax.rsqrt(jnp.mean(widened * widened, axis=-1, keepdims=True) + EPS)
    tokens_ref[...] = (widened * factor).astype(jnp.bfloat16)


def among(stores, first, source, act):
    if len(stores) == 1:
        pl.when(source == first)(lambda: act(stores[0]))
        return
    half = len(stores) // 2
    pl.when(source < first + half)(lambda: among(stores[:half], first, source, act))
    pl.when(source >= first + half)(lambda: among(stores[half:], first + half, source, act))


def plan_kernel(size, here_ref, place_ref, before_ref, owner_ref, slot_ref, source_ref, block_ref):
    reach = (size - 1) // 2
    opposite = size - reach - 1
    here = here_ref[0]

    def place(request, carry):
        window, part = request // 2, request % 2
        own = jnp.maximum(window - 1, 0)
        owner = jnp.where(window == 0, before_ref[0, part], owner_ref[own, part])
        away = place_ref[here // CORES] - place_ref[owner // CORES]
        away = jnp.where(away < 0, away + size, away)
        core = owner % CORES
        holder = jnp.where((away == 0) | ((away > reach) & (away <= opposite)), core, jnp.where(away <= reach, 0, 1))
        step = jnp.where(away <= opposite, away, size - away)
        arrival = jnp.where(away == 0, 0, 2 * step - 1 + jnp.where(core == holder, 0, 1))
        source_ref[request] = CORES * arrival + jnp.where(holder == here % CORES, 0, 1)
        block_ref[request] = jnp.where(window == 0, before_ref[1, part], slot_ref[own, part])
        return carry

    lax.fori_loop(0, source_ref.shape[0], place, 0)


def plan_requests(size, here, places, before, owner, slot):
    requests = 2 * owner.shape[0] + 2
    return pl.pallas_call(
        functools.partial(plan_kernel, size),
        out_shape=(jax.ShapeDtypeStruct((requests,), jnp.int32),) * 2,
        in_specs=[SMEM_SPEC] * 5,
        out_specs=(SMEM_SPEC,) * 2,
        name="plan_requests",
    )(here, places, before, owner, slot)


def weigh(scores):
    powers = jnp.exp2(scores - jnp.max(scores, axis=-1, keepdims=True))
    totals = jnp.sum(powers, axis=-1, keepdims=True)
    return (powers * (1.0 / totals)).astype(jnp.bfloat16)


def attend_kernel(
    source_ref, block_ref, here_ref, starts_ref, folded_hbm, single_ref, value_ref, *rest
):
    *stores, out_hbm, tokens, raw, folded, scores, weights, mixed, out, sems, folded_sems, out_sems = rest
    requests, length, width = raw.shape
    blocks = requests // 2 - 1
    count = blocks * SPAN
    rows_at_once = GROUP * SPAN
    groups = HEADS // GROUP
    lone_window = blocks
    order = [*range(1, blocks), lone_window, 0]

    def fetch(request, store):
        return pltpu.make_async_copy(store.at[block_ref[request]], raw.at[request], sems.at[request])

    def fetch_folded(group):
        heads = pl.ds(group * GROUP, GROUP)
        return pltpu.make_async_copy(folded_hbm.at[heads], folded.at[heads], folded_sems.at[group])

    def put(group):
        columns = pl.ds(group * GROUP * HEAD_DIM, GROUP * HEAD_DIM)
        return pltpu.make_async_copy(out.at[:, columns], out_hbm.at[:, columns], out_sems.at[group])

    for window in order:
        for request in (2 * window, 2 * window + 1):
            among(stores, 0, source_ref[request], lambda store: fetch(request, store).start())
        if window == order[0]:
            fetch_folded(0).start()
    for group in range(1, groups):
        fetch_folded(group).start()

    place = lax.broadcasted_iota(jnp.int32, (count, HEAD_DIM), 0)
    kept = place % SPAN == 0
    for block in range(blocks):
        fresh = starts_ref[block] == 0
        if block == 0:
            fresh = fresh & (here_ref[0] > 0)
        kept = kept | ((place // SPAN == block) & fresh)

    def ready(window):
        for request in (2 * window, 2 * window + 1):
            fetch(request, stores[0]).wait()
        for request in (2 * window, 2 * window + 1):
            normalise(raw[request], tokens.at[request])

    def along(window):
        return tokens[2 * window : 2 * window + 2].reshape(2 * length, width)

    units = [(group, window) for group in range(groups) for window in order if group == 0 or window != lone_window]
    lone = {}

    def place_of(unit):
        group, window = units[unit]
        slot = group * blocks + window
        return slot, slice(group * GROUP, (group + 1) * GROUP), slice(window * SPAN, (window + 1) * SPAN)

    def score(unit):
        window = units[unit][1]
        if window == lone_window:
            lone["scores"] = contract(single_ref[...].astype(jnp.bfloat16), along(window), ((1,), (1,)))
            return
        slot, heads, rows = place_of(unit)
        taken = folded[heads, rows].reshape(rows_at_once, width)
        scores[slot] = contract(taken, along(window), ((1,), (1,)))

    def soften(unit):
        if units[unit][1] == lone_window:
            lone["weights"] = weigh(lone["scores"])
            return
        slot, _, _ = place_of(unit)
        for part in range(GROUP):
            rows = slice(part * SPAN, (part + 1) * SPAN)
            weights[slot, rows] = weigh(scores[slot, rows])

    def combine(unit):
        window = units[unit][1]
        if window == lone_window:
            lone["sums"] = contract(lone["weights"], along(window), ((1,), (0,)))
            return
        slot, heads, rows = place_of(unit)
        sums = contract(weights[slot], along(window), ((1,), (0,))).reshape(GROUP, SPAN, width)
        if window == 0:
            first = lax.broadcasted_iota(jnp.int32, sums.shape, 1) == 0
            sums = jnp.where(first, lone["sums"][heads][:, None, :], sums)
        mixed[heads, rows] = sums.astype(jnp.bfloat16)

    def project(group):
        for head in range(group * GROUP, (group + 1) * GROUP):
            columns = head_columns(head)
            sums = contract(mixed[head], value_ref[:, columns], ((1,), (0,)))
            sums = jnp.where(kept, sums, 0.0)
            out[:, columns] = pltpu.roll(sums, count - 1, 0).astype(jnp.bfloat16)
        put(group).start()

    ready(order[0])
    for step in range(len(units) + 2):
        if step == 0:
            fetch_folded(0).wait()
        if step == len(order):
            for group in range(1, groups):
                fetch_folded(group).wait()
        if step + 1 < len(order):
            ready(order[step + 1])
        if step < len(units):
            score(step)
        if step >= 2:
            combine(step - 2)
        if 1 <= step <= len(units):
            soften(step - 1)
        if step >= 2 and units[step - 2][1] == order[-1]:
            project(units[step - 2][0])
    for group in range(groups):
        put(group).wait()


def attend(source, block, here, doc_starts, folded, single, w_value, stores):
    requests = source.shape[0]
    length, width = stores[0].shape[1:]
    count = folded.shape[1]
    groups = HEADS // GROUP
    units = groups * (count // SPAN)
    model_width = w_value.shape[1]
    return pl.pallas_call(
        attend_kernel,
        out_shape=jax.ShapeDtypeStruct((count, model_width), jnp.bfloat16),
        in_specs=[SMEM_SPEC] * 4 + [HBM_SPEC] + [VMEM_SPEC] * 2 + [ANY_SPEC] * len(stores),
        out_specs=HBM_SPEC,
        scratch_shapes=[
            pltpu.VMEM((requests, length, width), jnp.bfloat16),
            pltpu.VMEM((requests, length, width), jnp.bfloat16),
            pltpu.VMEM(folded.shape, jnp.bfloat16),
            pltpu.VMEM((units, GROUP * SPAN, 2 * length), jnp.float32),
            pltpu.VMEM((units, GROUP * SPAN, 2 * length), jnp.bfloat16),
            pltpu.VMEM(folded.shape, jnp.bfloat16),
            pltpu.VMEM((count, model_width), jnp.bfloat16),
            pltpu.SemaphoreType.DMA((requests,)),
            pltpu.SemaphoreType.DMA((groups,)),
            pltpu.SemaphoreType.DMA((groups,)),
        ],
        compiler_params=pltpu.CompilerParams(vmem_limit_bytes=40 * MIB),
        cost_estimate=pl.CostEstimate(
            flops=2 * HEADS * count * width * (4 * length + HEAD_DIM),
            bytes_accessed=16 * MIB,
            transcendentals=HEADS * count * 2 * length,
        ),
        name="attend_windows",
    )(source, block, here, doc_starts, in_hbm(folded), single, w_value, *stores)


def chip_ring(mesh):
    row = mesh.devices.reshape(-1, mesh.shape["seq"])[0]
    chips = list(range(len(row) // CORES))
    columns = [tuple(getattr(row[CORES * chip], "coords", (0, 0))[:2]) for chip in chips]
    if len(set(columns)) != 2:
        return chips
    up = [chip for chip in chips if columns[chip] == columns[0]]
    return up + [chip for chip in reversed(chips) if columns[chip] != columns[0]]


def after(values, others):
    return list(lax.optimization_barrier((tuple(values), tuple(others)))[0])


def body(ring, queries, neighbours, w_key, w_value, retrieval_owner, retrieval_slot, doc_starts):
    devices = lax.axis_size("seq")
    size = len(ring)
    reach = (size - 1) // 2

    ways = [
        (CORES * ring[i] + core, CORES * ring[(i + way) % size] + core)
        for i in range(size)
        for core, way in enumerate((1, -1))
    ]
    onwards = functools.partial(lax.ppermute, axis_name="seq", perm=ways)
    swapped = functools.partial(lax.ppermute, axis_name="seq", perm=[(i, i ^ 1) for i in range(devices)])

    chains = [neighbours, swapped(neighbours)]
    stores = list(chains)
    folded, single = fold(*after([queries], [chains[1]]), w_key)

    owner_slot = jnp.stack([retrieval_owner[-1], retrieval_slot[-1]])
    before = lax.ppermute(*after([owner_slot], [single]), "seq", [(i, i + 1) for i in range(devices - 1)])
    places = jnp.asarray([ring.index(chip) for chip in range(size)], jnp.int32)
    here = lax.axis_index("seq").reshape(1)
    source, block = plan_requests(size, here, places, before, retrieval_owner, retrieval_slot)

    beside = {(1, 0): [folded, single], (1, 1): [before]}
    for step in range(reach):
        for chain in range(2):
            others = beside.get((step, chain), []) + (stores[2 * chain + 4 * step - 5 :][:1] if step > 1 else [])
            sent = after([chains[chain]], others) if others else [chains[chain]]
            chains[chain] = onwards(sent[0])
            stores += [chains[chain], swapped(chains[chain])]
    if size % 2 == 0:
        sent = after([chains[0]], stores[-7:-4:2]) if reach > 1 else [chains[0]]
        last = onwards(sent[0])
        if reach:
            stores[-1] = swapped(after([chains[1]], [last, stores[-3], source, block])[0])
        stores += [last, swapped(last)]
    return attend(source, block, here, doc_starts, folded, single, w_value, stores)


def solution(mesh):
    return jax.shard_map(
        functools.partial(body, chip_ring(mesh)),
        mesh=mesh,
        in_specs=(
            P(("groups", "seq"), None),
            P(("groups", "seq"), None, None),
            P(),
            P(),
            P(("groups", "seq"), None),
            P(("groups", "seq"), None),
            P(("groups", "seq")),
        ),
        out_specs=P(("groups", "seq"), None),
        check_vma=False,
    )
```

```python
import functools
import math

import jax
import jax.numpy as jnp
from jax import lax
from jax.experimental import pallas as pl
from jax.experimental.pallas import tpu as pltpu
from jax.sharding import PartitionSpec as P

SPAN = 64
HEADS = 16
HEAD_DIM = 128
EPS = 1e-6
SCALE = math.log2(math.e) / math.sqrt(HEAD_DIM)
CORES = 2
GROUP = 4
MIB = 2**20


SMEM_SPEC = pl.BlockSpec(memory_space=pltpu.SMEM)
VMEM_SPEC = pl.BlockSpec(memory_space=pltpu.VMEM)
ANY_SPEC = pl.BlockSpec(memory_space=pl.ANY)
HBM_SPEC = pl.BlockSpec(memory_space=pltpu.HBM)


def contract(left, right, dims):
    return lax.dot_general(left, right, (dims, ((), ())), preferred_element_type=jnp.float32)


def in_hbm(value):
    return pltpu.with_memory_space_constraint(value, pltpu.HBM)


def head_columns(head):
    return slice(head * HEAD_DIM, (head + 1) * HEAD_DIM)


def fold_kernel(query_hbm, key_hbm, folded_hbm, single_ref, query, key, folded, in_sems, out_sems):
    groups = HEADS // GROUP

    def fetch(group):
        columns = slice(group * GROUP * HEAD_DIM, (group + 1) * GROUP * HEAD_DIM)
        return (
            pltpu.make_async_copy(query_hbm.at[:, columns], query.at[:, columns], in_sems.at[group, 0]),
            pltpu.make_async_copy(key_hbm.at[:, columns], key.at[:, columns], in_sems.at[group, 1]),
        )

    def put(head):
        return pltpu.make_async_copy(folded.at[head], folded_hbm.at[head], out_sems.at[head])

    for group in range(groups):
        for copy in fetch(group):
            copy.start()
    for head in range(HEADS):
        if head % GROUP == 0:
            for copy in fetch(head // GROUP):
                copy.wait()
        columns = head_columns(head)
        queries = pltpu.roll(query[:, columns].astype(jnp.float32), 1, 0).astype(jnp.bfloat16)
        rows = contract(queries, key[:, columns], ((1,), (1,))) * SCALE
        single_ref[head : head + 1, :] = rows[:1]
        folded[head] = rows.astype(jnp.bfloat16)
        put(head).start()
    for head in range(HEADS):
        put(head).wait()


def fold(queries, w_key):
    count, width = queries.shape[0], w_key.shape[0]
    shape = (HEADS, count, width)
    return pl.pallas_call(
        fold_kernel,
        out_shape=(
            pltpu.HBM(shape, jnp.bfloat16),
            jax.ShapeDtypeStruct((HEADS, width), jnp.float32),
        ),
        in_specs=[HBM_SPEC] * 2,
        out_specs=(HBM_SPEC, VMEM_SPEC),
        scratch_shapes=[
            pltpu.VMEM(queries.shape, jnp.bfloat16),
            pltpu.VMEM(w_key.shape, jnp.bfloat16),
            pltpu.VMEM(shape, jnp.bfloat16),
            pltpu.SemaphoreType.DMA((HEADS // GROUP, 2)),
            pltpu.SemaphoreType.DMA((HEADS,)),
        ],
        compiler_params=pltpu.CompilerParams(vmem_limit_bytes=28 * MIB),
        cost_estimate=pl.CostEstimate(
            flops=2 * queries.size * width, bytes_accessed=12 * MIB, transcendentals=0
        ),
        name="fold_queries",
    )(in_hbm(queries), in_hbm(w_key))


def normalise(raw, tokens_ref):
    widened = raw.astype(jnp.float32)
    factor = lax.rsqrt(jnp.mean(widened * widened, axis=-1, keepdims=True) + EPS)
    tokens_ref[...] = (widened * factor).astype(jnp.bfloat16)


def among(stores, first, source, act):
    if len(stores) == 1:
        pl.when(source == first)(lambda: act(stores[0]))
        return
    half = len(stores) // 2
    pl.when(source < first + half)(lambda: among(stores[:half], first, source, act))
    pl.when(source >= first + half)(lambda: among(stores[half:], first + half, source, act))


def locate(request, plan_refs, size):
    here_ref, place_ref, before_ref, owner_ref, slot_ref = plan_refs
    window, part = divmod(request, 2)
    owner = before_ref[0, part] if window == 0 else owner_ref[window - 1, part]
    slot = before_ref[1, part] if window == 0 else slot_ref[window - 1, part]
    reach = (size - 1) // 2
    opposite = size - reach - 1
    here = here_ref[0]
    away = place_ref[here // CORES] - place_ref[owner // CORES]
    away = jnp.where(away < 0, away + size, away)
    core = owner % CORES
    holder = jnp.where((away == 0) | ((away > reach) & (away <= opposite)), core, jnp.where(away <= reach, 0, 1))
    step = jnp.where(away <= opposite, away, size - away)
    arrival = jnp.where(away == 0, 0, 2 * step - 1 + jnp.where(core == holder, 0, 1))
    return CORES * arrival + jnp.where(holder == here % CORES, 0, 1), slot


def weigh(scores):
    powers = jnp.exp2(scores - jnp.max(scores, axis=-1, keepdims=True))
    totals = jnp.sum(powers, axis=-1, keepdims=True)
    return (powers * (1.0 / totals)).astype(jnp.bfloat16)


def attend_kernel(size, *refs):
    plan_refs, (starts_ref, folded_hbm, single_ref, value_ref, *rest) = refs[:5], refs[5:]
    *stores, out_hbm, tokens, raw, folded, scores, weights, mixed, out, sems, folded_sems, out_sems = rest
    requests, length, width = raw.shape
    blocks = requests // 2 - 1
    count = blocks * SPAN
    rows_at_once = GROUP * SPAN
    groups = HEADS // GROUP
    lone_window = blocks
    order = [*range(1, blocks), lone_window, 0]

    def fetch(request, store, block):
        return pltpu.make_async_copy(store.at[block], raw.at[request], sems.at[request])

    def fetch_folded(group):
        heads = pl.ds(group * GROUP, GROUP)
        return pltpu.make_async_copy(folded_hbm.at[heads], folded.at[heads], folded_sems.at[group])

    def put(group):
        columns = pl.ds(group * GROUP * HEAD_DIM, GROUP * HEAD_DIM)
        return pltpu.make_async_copy(out.at[:, columns], out_hbm.at[:, columns], out_sems.at[group])

    for window in order:
        for request in (2 * window, 2 * window + 1):
            source, block = locate(request, plan_refs, size)
            among(stores, 0, source, lambda store: fetch(request, store, block).start())
        if window == order[0]:
            fetch_folded(0).start()
    for group in range(1, groups):
        fetch_folded(group).start()

    place = lax.broadcasted_iota(jnp.int32, (count, HEAD_DIM), 0)
    kept = place % SPAN == 0
    for block in range(blocks):
        fresh = starts_ref[block] == 0
        if block == 0:
            fresh = fresh & (plan_refs[0][0] > 0)
        kept = kept | ((place // SPAN == block) & fresh)

    def ready(window):
        for request in (2 * window, 2 * window + 1):
            fetch(request, stores[0], 0).wait()
        for request in (2 * window, 2 * window + 1):
            normalise(raw[request], tokens.at[request])

    def along(window):
        return tokens[2 * window : 2 * window + 2].reshape(2 * length, width)

    units = [(group, window) for group in range(groups) for window in order if group == 0 or window != lone_window]
    lone = {}

    def place_of(unit):
        group, window = units[unit]
        heads, rows = slice(group * GROUP, (group + 1) * GROUP), slice(window * SPAN, (window + 1) * SPAN)
        return unit % len(scores), heads, rows

    def score(unit):
        window = units[unit][1]
        if window == lone_window:
            lone["scores"] = contract(single_ref[...].astype(jnp.bfloat16), along(window), ((1,), (1,)))
            return
        slot, heads, rows = place_of(unit)
        taken = folded[heads, rows].reshape(rows_at_once, width)
        scores[slot] = contract(taken, along(window), ((1,), (1,)))

    def soften(unit):
        if units[unit][1] == lone_window:
            lone["weights"] = weigh(lone["scores"])
            return
        slot, _, _ = place_of(unit)
        for part in range(GROUP):
            rows = slice(part * SPAN, (part + 1) * SPAN)
            weights[slot, rows] = weigh(scores[slot, rows])

    def combine(unit):
        window = units[unit][1]
        if window == lone_window:
            lone["sums"] = contract(lone["weights"], along(window), ((1,), (0,)))
            return
        slot, heads, rows = place_of(unit)
        sums = contract(weights[slot], along(window), ((1,), (0,))).reshape(GROUP, SPAN, width)
        if window == 0:
            first = lax.broadcasted_iota(jnp.int32, sums.shape, 1) == 0
            sums = jnp.where(first, lone["sums"][heads][:, None, :], sums)
        mixed[units[unit][0] % 2, :, rows] = sums.astype(jnp.bfloat16)

    def project(group):
        for head in range(group * GROUP, (group + 1) * GROUP):
            columns = head_columns(head)
            sums = contract(mixed[group % 2, head % GROUP], value_ref[:, columns], ((1,), (0,)))
            sums = jnp.where(kept, sums, 0.0)
            out[:, columns] = pltpu.roll(sums, count - 1, 0).astype(jnp.bfloat16)
        put(group).start()

    ready(order[0])
    for step in range(len(units) + 2):
        if step == 0:
            fetch_folded(0).wait()
        if step == len(order):
            for group in range(1, groups):
                fetch_folded(group).wait()
        if step + 1 < len(order):
            ready(order[step + 1])
        if step < len(units):
            score(step)
        if step >= 2:
            combine(step - 2)
        if 1 <= step <= len(units):
            soften(step - 1)
        if step >= 2 and units[step - 2][1] == order[-1]:
            project(units[step - 2][0])
    for group in range(groups):
        put(group).wait()


def attend(size, plan, doc_starts, folded, single, w_value, stores):
    requests = 2 * plan[3].shape[0] + 2
    length, width = stores[0].shape[1:]
    count = folded.shape[1]
    groups = HEADS // GROUP
    model_width = w_value.shape[1]
    return pl.pallas_call(
        functools.partial(attend_kernel, size),
        out_shape=jax.ShapeDtypeStruct((count, model_width), jnp.bfloat16),
        in_specs=[SMEM_SPEC] * 6 + [HBM_SPEC] + [VMEM_SPEC] * 2 + [ANY_SPEC] * len(stores),
        out_specs=HBM_SPEC,
        scratch_shapes=[
            pltpu.VMEM((requests, length, width), jnp.bfloat16),
            pltpu.VMEM((requests, length, width), jnp.bfloat16),
            pltpu.VMEM(folded.shape, jnp.bfloat16),
            pltpu.VMEM((5, GROUP * SPAN, 2 * length), jnp.float32),
            pltpu.VMEM((5, GROUP * SPAN, 2 * length), jnp.bfloat16),
            pltpu.VMEM((2, GROUP, count, width), jnp.bfloat16),
            pltpu.VMEM((count, model_width), jnp.bfloat16),
            pltpu.SemaphoreType.DMA((requests,)),
            pltpu.SemaphoreType.DMA((groups,)),
            pltpu.SemaphoreType.DMA((groups,)),
        ],
        compiler_params=pltpu.CompilerParams(vmem_limit_bytes=24 * MIB),
        cost_estimate=pl.CostEstimate(
            flops=2 * HEADS * count * width * (4 * length + HEAD_DIM),
            bytes_accessed=16 * MIB,
            transcendentals=HEADS * count * 2 * length,
        ),
        name="attend_windows",
    )(*plan, doc_starts, in_hbm(folded), single, w_value, *stores)


def chip_ring(mesh):
    row = mesh.devices.reshape(-1, mesh.shape["seq"])[0]
    chips = list(range(len(row) // CORES))
    columns = [tuple(getattr(row[CORES * chip], "coords", (0, 0))[:2]) for chip in chips]
    if len(set(columns)) != 2:
        return chips
    up = [chip for chip in chips if columns[chip] == columns[0]]
    return up + [chip for chip in reversed(chips) if columns[chip] != columns[0]]


def after(values, others):
    return list(lax.optimization_barrier((tuple(values), tuple(others)))[0])


def body(ring, queries, neighbours, w_key, w_value, retrieval_owner, retrieval_slot, doc_starts):
    devices = lax.axis_size("seq")
    size = len(ring)
    reach = (size - 1) // 2

    ways = [
        (CORES * ring[i] + core, CORES * ring[(i + way) % size] + core)
        for i in range(size)
        for core, way in enumerate((1, -1))
    ]
    onwards = functools.partial(lax.ppermute, axis_name="seq", perm=ways)
    swapped = functools.partial(lax.ppermute, axis_name="seq", perm=[(i, i ^ 1) for i in range(devices)])

    chains = [neighbours, swapped(neighbours)]
    stores = list(chains)
    folded, single = fold(*after([queries], [chains[1]]), w_key)

    beside = {(1, 0): [folded, single]}
    for step in range(reach):
        for chain in range(2):
            others = beside.get((step, chain), []) + (stores[2 * chain + 4 * step - 5 :][:1] if step > 1 else [])
            sent = after([chains[chain]], others) if others else [chains[chain]]
            chains[chain] = onwards(sent[0])
            stores += [chains[chain], swapped(chains[chain])]
            if (step, chain) == (0, 1):
                owner, slot = after([retrieval_owner, retrieval_slot], [chains[1]])
                asked = jnp.stack([owner[-1], slot[-1]])
                before = lax.ppermute(asked, "seq", [(i, i + 1) for i in range(devices - 1)])
                beside[reach - 1, 1] = [before]
    places = jnp.asarray([ring.index(chip) for chip in range(size)], jnp.int32)
    plan = [lax.axis_index("seq").reshape(1), places, before, owner, slot]
    if size % 2 == 0:
        sent = after([chains[0]], stores[-7:-4:2]) if reach > 1 else [chains[0]]
        last = onwards(sent[0])
        if reach:
            stores[-1] = swapped(after([chains[1]], [last, stores[-3]])[0])
        stores += [last, swapped(last)]
    return attend(size, plan, doc_starts, folded, single, w_value, stores)


def solution(mesh):
    return jax.shard_map(
        functools.partial(body, chip_ring(mesh)),
        mesh=mesh,
        in_specs=(
            P(("groups", "seq"), None),
            P(("groups", "seq"), None, None),
            P(),
            P(),
            P(("groups", "seq"), None),
            P(("groups", "seq"), None),
            P(("groups", "seq")),
        ),
        out_specs=P(("groups", "seq"), None),
        check_vma=False,
    )
```

```python
import functools
import math

import jax
import jax.numpy as jnp
from jax import lax
from jax.experimental import pallas as pl
from jax.experimental.pallas import tpu as pltpu
from jax.sharding import PartitionSpec as P

SPAN = 64
HEADS = 16
HEAD_DIM = 128
EPS = 1e-6
SCALE = math.log2(math.e) / math.sqrt(HEAD_DIM)
CORES = 2
GROUP = 4
MIB = 2**20


SMEM_SPEC = pl.BlockSpec(memory_space=pltpu.SMEM)
VMEM_SPEC = pl.BlockSpec(memory_space=pltpu.VMEM)
ANY_SPEC = pl.BlockSpec(memory_space=pl.ANY)
HBM_SPEC = pl.BlockSpec(memory_space=pltpu.HBM)


def contract(left, right, dims):
    return lax.dot_general(left, right, (dims, ((), ())), preferred_element_type=jnp.float32)


def in_hbm(value):
    return pltpu.with_memory_space_constraint(value, pltpu.HBM)


def head_columns(head):
    return slice(head * HEAD_DIM, (head + 1) * HEAD_DIM)


def group_heads(group):
    return pl.ds(group * GROUP, GROUP)


def group_columns(group):
    return pl.ds(group * GROUP * HEAD_DIM, GROUP * HEAD_DIM)


def fold_kernel(query_hbm, key_hbm, folded_hbm, single_ref, query, key, folded, in_sems, out_sems):
    groups = HEADS // GROUP

    def fetch(group):
        columns = group_columns(group)
        return (
            pltpu.make_async_copy(query_hbm.at[:, columns], query.at[:, columns], in_sems.at[group, 0]),
            pltpu.make_async_copy(key_hbm.at[:, columns], key.at[:, columns], in_sems.at[group, 1]),
        )

    def put(head):
        return pltpu.make_async_copy(folded.at[head], folded_hbm.at[head], out_sems.at[head])

    for group in range(groups):
        for copy in fetch(group):
            copy.start()
    for head in range(HEADS):
        if head % GROUP == 0:
            for copy in fetch(head // GROUP):
                copy.wait()
        columns = head_columns(head)
        queries = pltpu.roll(query[:, columns].astype(jnp.float32), 1, 0).astype(jnp.bfloat16)
        rows = contract(queries, key[:, columns], ((1,), (1,))) * SCALE
        single_ref[head : head + 1, :] = rows[:1]
        folded[head] = rows.astype(jnp.bfloat16)
        put(head).start()
    for head in range(HEADS):
        put(head).wait()


def fold(queries, w_key):
    count, width = queries.shape[0], w_key.shape[0]
    shape = (HEADS, count, width)
    return pl.pallas_call(
        fold_kernel,
        out_shape=(
            pltpu.HBM(shape, jnp.bfloat16),
            jax.ShapeDtypeStruct((HEADS, width), jnp.float32),
        ),
        in_specs=[HBM_SPEC] * 2,
        out_specs=(HBM_SPEC, VMEM_SPEC),
        scratch_shapes=[
            pltpu.VMEM(queries.shape, jnp.bfloat16),
            pltpu.VMEM(w_key.shape, jnp.bfloat16),
            pltpu.VMEM(shape, jnp.bfloat16),
            pltpu.SemaphoreType.DMA((HEADS // GROUP, 2)),
            pltpu.SemaphoreType.DMA((HEADS,)),
        ],
        compiler_params=pltpu.CompilerParams(vmem_limit_bytes=28 * MIB),
        cost_estimate=pl.CostEstimate(
            flops=2 * queries.size * width, bytes_accessed=12 * MIB, transcendentals=0
        ),
        name="fold_queries",
    )(in_hbm(queries), in_hbm(w_key))


def normalise(raw, tokens_ref):
    widened = raw.astype(jnp.float32)
    factor = lax.rsqrt(jnp.mean(widened * widened, axis=-1, keepdims=True) + EPS)
    tokens_ref[...] = (widened * factor).astype(jnp.bfloat16)


def among(stores, first, source, act):
    if len(stores) == 1:
        pl.when(source == first)(lambda: act(stores[0]))
        return
    half = len(stores) // 2
    pl.when(source < first + half)(lambda: among(stores[:half], first, source, act))
    pl.when(source >= first + half)(lambda: among(stores[half:], first + half, source, act))


def locate(request, plan_refs, size):
    here_ref, place_ref, owner_before_ref, slot_before_ref, owner_ref, slot_ref = plan_refs
    window, part = divmod(request, 2)
    if window == 0:
        last = owner_before_ref.shape[1] - 1
        owner, slot = owner_before_ref[part, last], slot_before_ref[part, last]
    else:
        owner, slot = owner_ref[part, window - 1], slot_ref[part, window - 1]
    reach = (size - 1) // 2
    opposite = size - reach - 1
    here = here_ref[0]
    away = place_ref[here // CORES] - place_ref[owner // CORES]
    away = jnp.where(away < 0, away + size, away)
    core = owner % CORES
    holder = jnp.where((away == 0) | ((away > reach) & (away <= opposite)), core, jnp.where(away <= reach, 0, 1))
    step = jnp.where(away <= opposite, away, size - away)
    arrival = jnp.where(away == 0, 0, 2 * step - 1 + jnp.where(core == holder, 0, 1))
    return CORES * arrival + jnp.where(holder == here % CORES, 0, 1), slot


def weigh(scores):
    powers = jnp.exp2(scores - jnp.max(scores, axis=-1, keepdims=True))
    totals = jnp.sum(powers, axis=-1, keepdims=True)
    return (powers * (1.0 / totals)).astype(jnp.bfloat16)


def attend_kernel(size, *refs):
    plan_refs, (starts_ref, folded_hbm, single_ref, value_hbm, *rest) = refs[:6], refs[6:]
    *stores, out_hbm, tokens, raw, folded, value, scores, weights, mixed, out, sems, group_sems = rest
    requests, length, width = raw.shape
    blocks = requests // 2 - 1
    count = blocks * SPAN
    rows_at_once = GROUP * SPAN
    groups = HEADS // GROUP
    lone_window = blocks
    order = [*range(1, blocks), lone_window, 0]

    def fetch(request, store, block):
        return pltpu.make_async_copy(store.at[block], raw.at[request], sems.at[request])

    def fetch_group(group):
        heads, columns = group_heads(group), group_columns(group)
        return (
            pltpu.make_async_copy(folded_hbm.at[heads], folded.at[heads], group_sems.at[group, 0]),
            pltpu.make_async_copy(value_hbm.at[:, columns], value.at[:, columns], group_sems.at[group, 1]),
        )

    def put(group):
        columns = group_columns(group)
        return pltpu.make_async_copy(out.at[:, columns], out_hbm.at[:, columns], group_sems.at[group, 2])

    for window in order:
        for request in (2 * window, 2 * window + 1):
            source, block = locate(request, plan_refs, size)
            among(stores, 0, source, lambda store: fetch(request, store, block).start())
        if window == order[0]:
            fetch_group(0)[0].start()
    fetch_group(0)[1].start()
    for group in range(1, groups):
        for copy in fetch_group(group):
            copy.start()

    place = lax.broadcasted_iota(jnp.int32, (count, HEAD_DIM), 0)
    kept = place % SPAN == 0
    for block in range(blocks):
        fresh = starts_ref[block] == 0
        if block == 0:
            fresh = fresh & (plan_refs[0][0] > 0)
        kept = kept | ((place // SPAN == block) & fresh)

    def ready(window):
        for request in (2 * window, 2 * window + 1):
            fetch(request, stores[0], 0).wait()
        for request in (2 * window, 2 * window + 1):
            normalise(raw[request], tokens.at[request])

    def along(window):
        return tokens[2 * window : 2 * window + 2].reshape(2 * length, width)

    units = [(group, window) for group in range(groups) for window in order if group == 0 or window != lone_window]
    lone = {}

    def place_of(unit):
        group, window = units[unit]
        heads, rows = slice(group * GROUP, (group + 1) * GROUP), slice(window * SPAN, (window + 1) * SPAN)
        return unit % len(scores), heads, rows

    def score(unit):
        window = units[unit][1]
        if window == lone_window:
            lone["scores"] = contract(single_ref[...].astype(jnp.bfloat16), along(window), ((1,), (1,)))
            return
        slot, heads, rows = place_of(unit)
        taken = folded[heads, rows].reshape(rows_at_once, width)
        scores[slot] = contract(taken, along(window), ((1,), (1,)))

    def soften(unit):
        if units[unit][1] == lone_window:
            lone["weights"] = weigh(lone["scores"])
            return
        slot, _, _ = place_of(unit)
        for part in range(GROUP):
            rows = slice(part * SPAN, (part + 1) * SPAN)
            weights[slot, rows] = weigh(scores[slot, rows])

    def combine(unit):
        window = units[unit][1]
        if window == lone_window:
            lone["sums"] = contract(lone["weights"], along(window), ((1,), (0,)))
            return
        slot, heads, rows = place_of(unit)
        sums = contract(weights[slot], along(window), ((1,), (0,))).reshape(GROUP, SPAN, width)
        if window == 0:
            first = lax.broadcasted_iota(jnp.int32, sums.shape, 1) == 0
            sums = jnp.where(first, lone["sums"][heads][:, None, :], sums)
        mixed[units[unit][0] % 2, :, rows] = sums.astype(jnp.bfloat16)

    def project(group):
        for head in range(group * GROUP, (group + 1) * GROUP):
            columns = head_columns(head)
            sums = contract(mixed[group % 2, head % GROUP], value[:, columns], ((1,), (0,)))
            sums = jnp.where(kept, sums, 0.0)
            out[:, columns] = pltpu.roll(sums, count - 1, 0).astype(jnp.bfloat16)
        put(group).start()

    ready(order[0])
    for step in range(len(units) + 2):
        if step == 0:
            fetch_group(0)[0].wait()
        if step == len(order):
            fetch_group(0)[1].wait()
            for group in range(1, groups):
                for copy in fetch_group(group):
                    copy.wait()
        if step + 1 < len(order):
            ready(order[step + 1])
        if step < len(units):
            score(step)
        if step >= 2:
            combine(step - 2)
        if 1 <= step <= len(units):
            soften(step - 1)
        if step >= 2 and units[step - 2][1] == order[-1]:
            project(units[step - 2][0])
    for group in range(groups):
        put(group).wait()


def attend(size, plan, doc_starts, folded, single, w_value, stores):
    requests = plan[-1].size + 2
    length, width = stores[0].shape[1:]
    count = folded.shape[1]
    groups = HEADS // GROUP
    model_width = w_value.shape[1]
    return pl.pallas_call(
        functools.partial(attend_kernel, size),
        out_shape=jax.ShapeDtypeStruct((count, model_width), jnp.bfloat16),
        in_specs=[SMEM_SPEC] * 7 + [HBM_SPEC, VMEM_SPEC, HBM_SPEC] + [ANY_SPEC] * len(stores),
        out_specs=HBM_SPEC,
        scratch_shapes=[
            pltpu.VMEM((requests, length, width), jnp.bfloat16),
            pltpu.VMEM((requests, length, width), jnp.bfloat16),
            pltpu.VMEM(folded.shape, jnp.bfloat16),
            pltpu.VMEM(w_value.shape, jnp.bfloat16),
            pltpu.VMEM((5, GROUP * SPAN, 2 * length), jnp.float32),
            pltpu.VMEM((5, GROUP * SPAN, 2 * length), jnp.bfloat16),
            pltpu.VMEM((2, GROUP, count, width), jnp.bfloat16),
            pltpu.VMEM((count, model_width), jnp.bfloat16),
            pltpu.SemaphoreType.DMA((requests,)),
            pltpu.SemaphoreType.DMA((groups, 3)),
        ],
        compiler_params=pltpu.CompilerParams(vmem_limit_bytes=28 * MIB),
        cost_estimate=pl.CostEstimate(
            flops=2 * HEADS * count * width * (4 * length + HEAD_DIM),
            bytes_accessed=16 * MIB,
            transcendentals=HEADS * count * 2 * length,
        ),
        name="attend_windows",
    )(*plan, doc_starts, in_hbm(folded), single, in_hbm(w_value), *stores)


def chip_ring(mesh):
    row = mesh.devices.reshape(-1, mesh.shape["seq"])[0]
    chips = list(range(len(row) // CORES))
    columns = [tuple(getattr(row[CORES * chip], "coords", (0, 0))[:2]) for chip in chips]
    if len(set(columns)) != 2:
        return chips
    up = [chip for chip in chips if columns[chip] == columns[0]]
    return up + [chip for chip in reversed(chips) if columns[chip] != columns[0]]


def after(values, others):
    return list(lax.optimization_barrier((tuple(values), tuple(others)))[0])


def body(ring, queries, neighbours, w_key, w_value, retrieval_owner, retrieval_slot, doc_starts):
    devices = lax.axis_size("seq")
    size = len(ring)
    reach = (size - 1) // 2

    ways = [
        (CORES * ring[i] + core, CORES * ring[(i + way) % size] + core)
        for i in range(size)
        for core, way in enumerate((1, -1))
    ]
    onwards = functools.partial(lax.ppermute, axis_name="seq", perm=ways)
    swapped = functools.partial(lax.ppermute, axis_name="seq", perm=[(i, i ^ 1) for i in range(devices)])

    wanted = [retrieval_owner.T, retrieval_slot.T]
    before = [lax.ppermute(rows, "seq", [(i, i + 1) for i in range(devices - 1)]) for rows in wanted]
    neighbours, *before = lax.optimization_barrier((neighbours, *before))
    chains = [neighbours, swapped(neighbours)]
    stores = [neighbours, in_hbm(chains[1])]
    folded, single = fold(*after([queries], [chains[1]]), w_key)

    beside = {(1, 0): [folded, single]}
    for step in range(reach):
        for chain in range(2):
            others = beside.get((step, chain), []) + (stores[2 * chain + 4 * step - 5 :][:1] if step > 1 else [])
            sent = after([chains[chain]], others) if others else [chains[chain]]
            chains[chain] = onwards(sent[0])
            other = swapped(chains[chain])
            stores += [chains[chain], in_hbm(other) if step + 1 < reach else other]
    places = jnp.asarray([ring.index(chip) for chip in range(size)], jnp.int32)
    plan = [lax.axis_index("seq").reshape(1), places, *before, *wanted]
    if size % 2 == 0:
        sent = after([chains[0]], stores[-7:-4:2]) if reach > 1 else [chains[0]]
        last = onwards(sent[0])
        if reach:
            stores[-1] = swapped(after([chains[1]], [last, stores[-3]])[0])
        stores += [last, swapped(last)]
    return attend(size, plan, doc_starts, folded, single, w_value, stores)


def solution(mesh):
    return jax.shard_map(
        functools.partial(body, chip_ring(mesh)),
        mesh=mesh,
        in_specs=(
            P(("groups", "seq"), None),
            P(("groups", "seq"), None, None),
            P(),
            P(),
            P(("groups", "seq"), None),
            P(("groups", "seq"), None),
            P(("groups", "seq")),
        ),
        out_specs=P(("groups", "seq"), None),
        check_vma=False,
    )
```

```python
import functools
import math

import jax
import jax.numpy as jnp
from jax import lax
from jax.experimental import pallas as pl
from jax.experimental.pallas import tpu as pltpu
from jax.sharding import PartitionSpec as P

SPAN = 64
HEADS = 16
HEAD_DIM = 128
EPS = 1e-6
SCALE = math.log2(math.e) / math.sqrt(HEAD_DIM)
CORES = 2
GROUP = 4
MIB = 2**20


SMEM_SPEC = pl.BlockSpec(memory_space=pltpu.SMEM)
VMEM_SPEC = pl.BlockSpec(memory_space=pltpu.VMEM)
ANY_SPEC = pl.BlockSpec(memory_space=pl.ANY)
HBM_SPEC = pl.BlockSpec(memory_space=pltpu.HBM)


def contract(left, right, dims):
    return lax.dot_general(left, right, (dims, ((), ())), preferred_element_type=jnp.float32)


def in_hbm(value):
    return pltpu.with_memory_space_constraint(value, pltpu.HBM)


def head_columns(head):
    return slice(head * HEAD_DIM, (head + 1) * HEAD_DIM)


def group_heads(group):
    return pl.ds(group * GROUP, GROUP)


def group_columns(group):
    return pl.ds(group * GROUP * HEAD_DIM, GROUP * HEAD_DIM)


def fold_kernel(query_hbm, key_hbm, folded_hbm, single_ref, query, key, folded, in_sems, out_sems):
    groups = HEADS // GROUP

    def fetch(group):
        columns = group_columns(group)
        return (
            pltpu.make_async_copy(query_hbm.at[:, columns], query.at[:, columns], in_sems.at[group, 0]),
            pltpu.make_async_copy(key_hbm.at[:, columns], key.at[:, columns], in_sems.at[group, 1]),
        )

    def put(head):
        return pltpu.make_async_copy(folded.at[head], folded_hbm.at[head], out_sems.at[head])

    for group in range(groups):
        for copy in fetch(group):
            copy.start()
    for head in range(HEADS):
        if head % GROUP == 0:
            for copy in fetch(head // GROUP):
                copy.wait()
        columns = head_columns(head)
        queries = pltpu.roll(query[:, columns].astype(jnp.float32), 1, 0).astype(jnp.bfloat16)
        rows = contract(queries, key[:, columns], ((1,), (1,))) * SCALE
        single_ref[head : head + 1, :] = rows[:1]
        folded[head] = rows.astype(jnp.bfloat16)
        put(head).start()
    for head in range(HEADS):
        put(head).wait()


def fold(queries, w_key):
    count, width = queries.shape[0], w_key.shape[0]
    shape = (HEADS, count, width)
    return pl.pallas_call(
        fold_kernel,
        out_shape=(
            pltpu.HBM(shape, jnp.bfloat16),
            jax.ShapeDtypeStruct((HEADS, width), jnp.float32),
        ),
        in_specs=[HBM_SPEC] * 2,
        out_specs=(HBM_SPEC, VMEM_SPEC),
        scratch_shapes=[
            pltpu.VMEM(queries.shape, jnp.bfloat16),
            pltpu.VMEM(w_key.shape, jnp.bfloat16),
            pltpu.VMEM(shape, jnp.bfloat16),
            pltpu.SemaphoreType.DMA((HEADS // GROUP, 2)),
            pltpu.SemaphoreType.DMA((HEADS,)),
        ],
        compiler_params=pltpu.CompilerParams(vmem_limit_bytes=28 * MIB),
        cost_estimate=pl.CostEstimate(
            flops=2 * queries.size * width, bytes_accessed=12 * MIB, transcendentals=0
        ),
        name="fold_queries",
    )(in_hbm(queries), in_hbm(w_key))


def normalise(raw, tokens_ref):
    widened = raw.astype(jnp.float32)
    factor = lax.rsqrt(jnp.mean(widened * widened, axis=-1, keepdims=True) + EPS)
    tokens_ref[...] = (widened * factor).astype(jnp.bfloat16)


def among(stores, first, source, act):
    if len(stores) == 1:
        pl.when(source == first)(lambda: act(stores[0]))
        return
    half = len(stores) // 2
    pl.when(source < first + half)(lambda: among(stores[:half], first, source, act))
    pl.when(source >= first + half)(lambda: among(stores[half:], first + half, source, act))


def locate(request, plan_refs, size, stored):
    here_ref, place_ref, before_ref, wanted_ref = plan_refs
    window, part = divmod(request, 2)
    wanted = before_ref[part, before_ref.shape[1] - 1] if window == 0 else wanted_ref[part, window - 1]
    owner, slot = wanted // stored, wanted % stored
    reach = (size - 1) // 2
    opposite = size - reach - 1
    here = here_ref[0]
    away = place_ref[here // CORES] - place_ref[owner // CORES]
    away = jnp.where(away < 0, away + size, away)
    core = owner % CORES
    holder = jnp.where((away == 0) | ((away > reach) & (away <= opposite)), core, jnp.where(away <= reach, 0, 1))
    step = jnp.where(away <= opposite, away, size - away)
    arrival = jnp.where(away == 0, 0, 2 * step - 1 + jnp.where(core == holder, 0, 1))
    return CORES * arrival + jnp.where(holder == here % CORES, 0, 1), slot


def weigh(scores):
    powers = jnp.exp2(scores - jnp.max(scores, axis=-1, keepdims=True))
    totals = jnp.sum(powers, axis=-1, keepdims=True)
    return (powers * (1.0 / totals)).astype(jnp.bfloat16)


def attend_kernel(size, *refs):
    plan_refs, (starts_ref, folded_hbm, single_ref, value_hbm, *rest) = refs[:4], refs[4:]
    *stores, out_hbm, tokens, raw, folded, value, scores, weights, mixed, out, sems, group_sems = rest
    requests, length, width = raw.shape
    blocks = requests // 2 - 1
    count = blocks * SPAN
    rows_at_once = GROUP * SPAN
    groups = HEADS // GROUP
    lone_window = blocks
    order = [*range(1, blocks), lone_window, 0]

    def fetch(request, store, block):
        return pltpu.make_async_copy(store.at[block], raw.at[request], sems.at[request])

    def fetch_group(group):
        heads, columns = group_heads(group), group_columns(group)
        return (
            pltpu.make_async_copy(folded_hbm.at[heads], folded.at[heads], group_sems.at[group, 0]),
            pltpu.make_async_copy(value_hbm.at[:, columns], value.at[:, columns], group_sems.at[group, 1]),
        )

    def put(group):
        columns = group_columns(group)
        return pltpu.make_async_copy(out.at[:, columns], out_hbm.at[:, columns], group_sems.at[group, 2])

    for window in order:
        for request in (2 * window, 2 * window + 1):
            source, block = locate(request, plan_refs, size, stores[0].shape[0])
            among(stores, 0, source, lambda store: fetch(request, store, block).start())
        if window == order[0]:
            fetch_group(0)[0].start()
    fetch_group(0)[1].start()
    for group in range(1, groups):
        for copy in fetch_group(group):
            copy.start()

    place = lax.broadcasted_iota(jnp.int32, (count, HEAD_DIM), 0)
    kept = place % SPAN == 0
    for block in range(blocks):
        fresh = starts_ref[block] == 0
        if block == 0:
            fresh = fresh & (plan_refs[0][0] > 0)
        kept = kept | ((place // SPAN == block) & fresh)

    def ready(window):
        for request in (2 * window, 2 * window + 1):
            fetch(request, stores[0], 0).wait()
        for request in (2 * window, 2 * window + 1):
            normalise(raw[request], tokens.at[request])

    def along(window):
        return tokens[2 * window : 2 * window + 2].reshape(2 * length, width)

    units = [(group, window) for group in range(groups) for window in order if group == 0 or window != lone_window]
    lone = {}

    def place_of(unit):
        group, window = units[unit]
        heads, rows = slice(group * GROUP, (group + 1) * GROUP), slice(window * SPAN, (window + 1) * SPAN)
        return unit % len(scores), heads, rows

    def score(unit):
        window = units[unit][1]
        if window == lone_window:
            lone["scores"] = contract(single_ref[...].astype(jnp.bfloat16), along(window), ((1,), (1,)))
            return
        slot, heads, rows = place_of(unit)
        taken = folded[heads, rows].reshape(rows_at_once, width)
        scores[slot] = contract(taken, along(window), ((1,), (1,)))

    def soften(unit):
        if units[unit][1] == lone_window:
            lone["weights"] = weigh(lone["scores"])
            return
        slot, _, _ = place_of(unit)
        for part in range(GROUP):
            rows = slice(part * SPAN, (part + 1) * SPAN)
            weights[slot, rows] = weigh(scores[slot, rows])

    def combine(unit):
        window = units[unit][1]
        if window == lone_window:
            lone["sums"] = contract(lone["weights"], along(window), ((1,), (0,)))
            return
        slot, heads, rows = place_of(unit)
        sums = contract(weights[slot], along(window), ((1,), (0,))).reshape(GROUP, SPAN, width)
        if window == 0:
            first = lax.broadcasted_iota(jnp.int32, sums.shape, 1) == 0
            sums = jnp.where(first, lone["sums"][heads][:, None, :], sums)
        mixed[units[unit][0] % 2, :, rows] = sums.astype(jnp.bfloat16)

    def project(group):
        for head in range(group * GROUP, (group + 1) * GROUP):
            columns = head_columns(head)
            sums = contract(mixed[group % 2, head % GROUP], value[:, columns], ((1,), (0,)))
            sums = jnp.where(kept, sums, 0.0)
            out[:, columns] = pltpu.roll(sums, count - 1, 0).astype(jnp.bfloat16)
        put(group).start()

    ready(order[0])
    for step in range(len(units) + 2):
        if step == 0:
            fetch_group(0)[0].wait()
        if step == len(order):
            fetch_group(0)[1].wait()
            for group in range(1, groups):
                for copy in fetch_group(group):
                    copy.wait()
        if step + 1 < len(order):
            ready(order[step + 1])
        if step < len(units):
            score(step)
        if step >= 2:
            combine(step - 2)
        if 1 <= step <= len(units):
            soften(step - 1)
        if step >= 2 and units[step - 2][1] == order[-1]:
            project(units[step - 2][0])
    for group in range(groups):
        put(group).wait()


def attend(size, plan, doc_starts, folded, single, w_value, stores):
    requests = plan[-1].size + 2
    length, width = stores[0].shape[1:]
    count = folded.shape[1]
    groups = HEADS // GROUP
    model_width = w_value.shape[1]
    return pl.pallas_call(
        functools.partial(attend_kernel, size),
        out_shape=jax.ShapeDtypeStruct((count, model_width), jnp.bfloat16),
        in_specs=[SMEM_SPEC] * 5 + [HBM_SPEC, VMEM_SPEC, HBM_SPEC] + [ANY_SPEC] * len(stores),
        out_specs=HBM_SPEC,
        scratch_shapes=[
            pltpu.VMEM((requests, length, width), jnp.bfloat16),
            pltpu.VMEM((requests, length, width), jnp.bfloat16),
            pltpu.VMEM(folded.shape, jnp.bfloat16),
            pltpu.VMEM(w_value.shape, jnp.bfloat16),
            pltpu.VMEM((5, GROUP * SPAN, 2 * length), jnp.float32),
            pltpu.VMEM((5, GROUP * SPAN, 2 * length), jnp.bfloat16),
            pltpu.VMEM((2, GROUP, count, width), jnp.bfloat16),
            pltpu.VMEM((count, model_width), jnp.bfloat16),
            pltpu.SemaphoreType.DMA((requests,)),
            pltpu.SemaphoreType.DMA((groups, 3)),
        ],
        compiler_params=pltpu.CompilerParams(vmem_limit_bytes=28 * MIB),
        cost_estimate=pl.CostEstimate(
            flops=2 * HEADS * count * width * (4 * length + HEAD_DIM),
            bytes_accessed=16 * MIB,
            transcendentals=HEADS * count * 2 * length,
        ),
        name="attend_windows",
    )(*plan, doc_starts, in_hbm(folded), single, in_hbm(w_value), *stores)


def chip_ring(mesh):
    row = mesh.devices.reshape(-1, mesh.shape["seq"])[0]
    chips = list(range(len(row) // CORES))
    columns = [tuple(getattr(row[CORES * chip], "coords", (0, 0))[:2]) for chip in chips]
    if len(set(columns)) != 2:
        return chips
    up = [chip for chip in chips if columns[chip] == columns[0]]
    return up + [chip for chip in reversed(chips) if columns[chip] != columns[0]]


def after(values, others):
    return list(lax.optimization_barrier((tuple(values), tuple(others)))[0])


def body(ring, queries, neighbours, w_key, w_value, retrieval_owner, retrieval_slot, doc_starts):
    devices = lax.axis_size("seq")
    size = len(ring)
    reach = (size - 1) // 2

    ways = [
        (CORES * ring[i] + core, CORES * ring[(i + way) % size] + core)
        for i in range(size)
        for core, way in enumerate((1, -1))
    ]
    onwards = functools.partial(lax.ppermute, axis_name="seq", perm=ways)
    swapped = functools.partial(lax.ppermute, axis_name="seq", perm=[(i, i ^ 1) for i in range(devices)])

    stored = neighbours.shape[0]
    wanted = (retrieval_owner * stored + retrieval_slot).T
    chains = [neighbours, swapped(neighbours)]
    stores = [neighbours, in_hbm(chains[1])]
    folded, single = fold(*after([queries], [chains[1]]), w_key)

    beside = {(1, 0): [folded, single]}
    for step in range(reach):
        for chain in range(2):
            others = beside.get((step, chain), []) + (stores[2 * chain + 4 * step - 5 :][:1] if step > 1 else [])
            sent = after([chains[chain]], others) if others else [chains[chain]]
            chains[chain] = onwards(sent[0])
            stores += [chains[chain], in_hbm(swapped(chains[chain]))]
            if (step, chain) == (0, 1):
                asked = after([wanted], [chains[1]])[0]
                before = lax.ppermute(asked, "seq", [(i, i + 1) for i in range(devices - 1)])
                beside[2, 0] = [before]
    places = jnp.asarray([ring.index(chip) for chip in range(size)], jnp.int32)
    plan = [lax.axis_index("seq").reshape(1), places, before, wanted]
    if size % 2 == 0:
        sent = after([chains[0]], stores[-7:-4:2]) if reach > 1 else [chains[0]]
        last = onwards(sent[0])
        if reach:
            stores[-1] = swapped(after([chains[1]], [last, stores[-3]])[0])
        stores += [last, swapped(last)]
    return attend(size, plan, doc_starts, folded, single, w_value, stores)


def solution(mesh):
    return jax.shard_map(
        functools.partial(body, chip_ring(mesh)),
        mesh=mesh,
        in_specs=(
            P(("groups", "seq"), None),
            P(("groups", "seq"), None, None),
            P(),
            P(),
            P(("groups", "seq"), None),
            P(("groups", "seq"), None),
            P(("groups", "seq")),
        ),
        out_specs=P(("groups", "seq"), None),
        check_vma=False,
    )
```

```python
import functools
import math

import jax
import jax.numpy as jnp
from jax import lax
from jax.experimental import pallas as pl
from jax.experimental.pallas import tpu as pltpu
from jax.sharding import PartitionSpec as P

SPAN = 64
HEADS = 16
HEAD_DIM = 128
EPS = 1e-6
SCALE = math.log2(math.e) / math.sqrt(HEAD_DIM)
CORES = 2
GROUP = 4
MIB = 2**20


SMEM_SPEC = pl.BlockSpec(memory_space=pltpu.SMEM)
VMEM_SPEC = pl.BlockSpec(memory_space=pltpu.VMEM)
ANY_SPEC = pl.BlockSpec(memory_space=pl.ANY)
HBM_SPEC = pl.BlockSpec(memory_space=pltpu.HBM)


def contract(left, right, dims):
    return lax.dot_general(left, right, (dims, ((), ())), preferred_element_type=jnp.float32)


def in_hbm(value):
    return pltpu.with_memory_space_constraint(value, pltpu.HBM)


def head_columns(head):
    return slice(head * HEAD_DIM, (head + 1) * HEAD_DIM)


def group_heads(group):
    return pl.ds(group * GROUP, GROUP)


def group_columns(group):
    return pl.ds(group * GROUP * HEAD_DIM, GROUP * HEAD_DIM)


def fold_kernel(query_hbm, key_hbm, folded_hbm, single_ref, query, key, folded, in_sems, out_sems):
    groups = HEADS // GROUP

    def fetch(group):
        columns = group_columns(group)
        return (
            pltpu.make_async_copy(query_hbm.at[:, columns], query.at[:, columns], in_sems.at[group, 0]),
            pltpu.make_async_copy(key_hbm.at[:, columns], key.at[:, columns], in_sems.at[group, 1]),
        )

    def put(head):
        return pltpu.make_async_copy(folded.at[head], folded_hbm.at[head], out_sems.at[head])

    for group in range(groups):
        for copy in fetch(group):
            copy.start()
    for head in range(HEADS):
        if head % GROUP == 0:
            for copy in fetch(head // GROUP):
                copy.wait()
        columns = head_columns(head)
        queries = pltpu.roll(query[:, columns].astype(jnp.float32), 1, 0).astype(jnp.bfloat16)
        rows = contract(queries, key[:, columns], ((1,), (1,))) * SCALE
        single_ref[head : head + 1, :] = rows[:1]
        folded[head] = rows.astype(jnp.bfloat16)
        put(head).start()
    for head in range(HEADS):
        put(head).wait()


def fold(queries, w_key):
    count, width = queries.shape[0], w_key.shape[0]
    shape = (HEADS, count, width)
    return pl.pallas_call(
        fold_kernel,
        out_shape=(
            pltpu.HBM(shape, jnp.bfloat16),
            jax.ShapeDtypeStruct((HEADS, width), jnp.float32),
        ),
        in_specs=[HBM_SPEC] * 2,
        out_specs=(HBM_SPEC, VMEM_SPEC),
        scratch_shapes=[
            pltpu.VMEM(queries.shape, jnp.bfloat16),
            pltpu.VMEM(w_key.shape, jnp.bfloat16),
            pltpu.VMEM(shape, jnp.bfloat16),
            pltpu.SemaphoreType.DMA((HEADS // GROUP, 2)),
            pltpu.SemaphoreType.DMA((HEADS,)),
        ],
        compiler_params=pltpu.CompilerParams(vmem_limit_bytes=28 * MIB),
        cost_estimate=pl.CostEstimate(
            flops=2 * queries.size * width, bytes_accessed=12 * MIB, transcendentals=0
        ),
        name="fold_queries",
    )(in_hbm(queries), in_hbm(w_key))


def normalise(raw, tokens_ref):
    widened = raw.astype(jnp.float32)
    factor = lax.rsqrt(jnp.mean(widened * widened, axis=-1, keepdims=True) + EPS)
    tokens_ref[...] = (widened * factor).astype(jnp.bfloat16)


def among(stores, first, source, act):
    if len(stores) == 1:
        pl.when(source == first)(lambda: act(stores[0]))
        return
    half = len(stores) // 2
    pl.when(source < first + half)(lambda: among(stores[:half], first, source, act))
    pl.when(source >= first + half)(lambda: among(stores[half:], first + half, source, act))


def locate(request, plan_refs, size, stored):
    here_ref, place_ref, before_ref, wanted_ref = plan_refs
    window, part = divmod(request, 2)
    wanted = before_ref[part, before_ref.shape[1] - 1] if window == 0 else wanted_ref[part, window - 1]
    owner, slot = wanted // stored, wanted % stored
    reach = (size - 1) // 2
    opposite = size - reach - 1
    here = here_ref[0]
    away = place_ref[here // CORES] - place_ref[owner // CORES]
    away = jnp.where(away < 0, away + size, away)
    core = owner % CORES
    holder = jnp.where((away == 0) | ((away > reach) & (away <= opposite)), core, jnp.where(away <= reach, 0, 1))
    step = jnp.where(away <= opposite, away, size - away)
    arrival = jnp.where(away == 0, 0, 2 * step - 1 + jnp.where(core == holder, 0, 1))
    return CORES * arrival + jnp.where(holder == here % CORES, 0, 1), slot


def weigh(scores):
    powers = jnp.exp2(scores - jnp.max(scores, axis=-1, keepdims=True))
    totals = jnp.sum(powers, axis=-1, keepdims=True)
    return (powers * (1.0 / totals)).astype(jnp.bfloat16)


def attend_kernel(size, *refs):
    plan_refs, (starts_ref, folded_hbm, single_ref, value_hbm, *rest) = refs[:4], refs[4:]
    *stores, out_hbm, tokens, turned, raw, folded, value, scores, weights, mixed, out, sems, group_sems = rest
    requests, length, width = raw.shape
    blocks = requests // 2 - 1
    count = blocks * SPAN
    rows_at_once = GROUP * SPAN
    groups = HEADS // GROUP
    lone_window = blocks
    order = [*range(1, blocks), lone_window, 0]

    def fetch(request, store, block):
        return pltpu.make_async_copy(store.at[block], raw.at[request], sems.at[request])

    def fetch_group(group):
        heads, columns = group_heads(group), group_columns(group)
        return (
            pltpu.make_async_copy(folded_hbm.at[heads], folded.at[heads], group_sems.at[group, 0]),
            pltpu.make_async_copy(value_hbm.at[:, columns], value.at[:, columns], group_sems.at[group, 1]),
        )

    def put(group):
        columns = group_columns(group)
        return pltpu.make_async_copy(out.at[:, columns], out_hbm.at[:, columns], group_sems.at[group, 2])

    for window in order:
        for request in (2 * window, 2 * window + 1):
            source, block = locate(request, plan_refs, size, stores[0].shape[0])
            among(stores, 0, source, lambda store: fetch(request, store, block).start())
        if window == order[0]:
            fetch_group(0)[0].start()
    fetch_group(0)[1].start()
    for group in range(1, groups):
        for copy in fetch_group(group):
            copy.start()

    place = lax.broadcasted_iota(jnp.int32, (count, HEAD_DIM), 0)
    kept = place % SPAN == 0
    for block in range(blocks):
        fresh = starts_ref[block] == 0
        if block == 0:
            fresh = fresh & (plan_refs[0][0] > 0)
        kept = kept | ((place // SPAN == block) & fresh)

    def ready(window):
        for request in (2 * window, 2 * window + 1):
            fetch(request, stores[0], 0).wait()
        for request in (2 * window, 2 * window + 1):
            normalise(raw[request], tokens.at[request])
            turned[request] = tokens[request].T

    def across(window):
        return jnp.concatenate([turned[2 * window], turned[2 * window + 1]], axis=1)

    def along(window):
        return tokens[2 * window : 2 * window + 2].reshape(2 * length, width)

    units = [(group, window) for group in range(groups) for window in order if group == 0 or window != lone_window]
    lone = {}

    def place_of(unit):
        group, window = units[unit]
        heads, rows = slice(group * GROUP, (group + 1) * GROUP), slice(window * SPAN, (window + 1) * SPAN)
        return unit % len(scores), heads, rows

    def score(unit):
        window = units[unit][1]
        if window == lone_window:
            lone["scores"] = contract(single_ref[...].astype(jnp.bfloat16), across(window), ((1,), (0,)))
            return
        slot, heads, rows = place_of(unit)
        taken = folded[heads, rows].reshape(rows_at_once, width)
        scores[slot] = contract(taken, across(window), ((1,), (0,)))

    def soften(unit):
        if units[unit][1] == lone_window:
            lone["weights"] = weigh(lone["scores"])
            return
        slot, _, _ = place_of(unit)
        for part in range(GROUP):
            rows = slice(part * SPAN, (part + 1) * SPAN)
            weights[slot, rows] = weigh(scores[slot, rows])

    def combine(unit):
        window = units[unit][1]
        if window == lone_window:
            lone["sums"] = contract(lone["weights"], along(window), ((1,), (0,)))
            return
        slot, heads, rows = place_of(unit)
        sums = contract(weights[slot], along(window), ((1,), (0,))).reshape(GROUP, SPAN, width)
        if window == 0:
            first = lax.broadcasted_iota(jnp.int32, sums.shape, 1) == 0
            sums = jnp.where(first, lone["sums"][heads][:, None, :], sums)
        mixed[units[unit][0] % 2, :, rows] = sums.astype(jnp.bfloat16)

    def project(group):
        for head in range(group * GROUP, (group + 1) * GROUP):
            columns = head_columns(head)
            sums = contract(mixed[group % 2, head % GROUP], value[:, columns], ((1,), (0,)))
            sums = jnp.where(kept, sums, 0.0)
            out[:, columns] = pltpu.roll(sums, count - 1, 0).astype(jnp.bfloat16)
        put(group).start()

    ready(order[0])
    for step in range(len(units) + 2):
        if step == 0:
            fetch_group(0)[0].wait()
        if step == len(order):
            fetch_group(0)[1].wait()
            for group in range(1, groups):
                for copy in fetch_group(group):
                    copy.wait()
        if step + 1 < len(order):
            ready(order[step + 1])
        if step < len(units):
            score(step)
        if step >= 2:
            combine(step - 2)
        if 1 <= step <= len(units):
            soften(step - 1)
        if step >= 2 and units[step - 2][1] == order[-1]:
            project(units[step - 2][0])
    for group in range(groups):
        put(group).wait()


def attend(size, plan, doc_starts, folded, single, w_value, stores):
    requests = plan[-1].size + 2
    length, width = stores[0].shape[1:]
    count = folded.shape[1]
    groups = HEADS // GROUP
    model_width = w_value.shape[1]
    return pl.pallas_call(
        functools.partial(attend_kernel, size),
        out_shape=jax.ShapeDtypeStruct((count, model_width), jnp.bfloat16),
        in_specs=[SMEM_SPEC] * 5 + [HBM_SPEC, VMEM_SPEC, HBM_SPEC] + [ANY_SPEC] * len(stores),
        out_specs=HBM_SPEC,
        scratch_shapes=[
            pltpu.VMEM((requests, length, width), jnp.bfloat16),
            pltpu.VMEM((requests, width, length), jnp.bfloat16),
            pltpu.VMEM((requests, length, width), jnp.bfloat16),
            pltpu.VMEM(folded.shape, jnp.bfloat16),
            pltpu.VMEM(w_value.shape, jnp.bfloat16),
            pltpu.VMEM((5, GROUP * SPAN, 2 * length), jnp.float32),
            pltpu.VMEM((5, GROUP * SPAN, 2 * length), jnp.bfloat16),
            pltpu.VMEM((2, GROUP, count, width), jnp.bfloat16),
            pltpu.VMEM((count, model_width), jnp.bfloat16),
            pltpu.SemaphoreType.DMA((requests,)),
            pltpu.SemaphoreType.DMA((groups, 3)),
        ],
        compiler_params=pltpu.CompilerParams(vmem_limit_bytes=28 * MIB),
        cost_estimate=pl.CostEstimate(
            flops=2 * HEADS * count * width * (4 * length + HEAD_DIM),
            bytes_accessed=16 * MIB,
            transcendentals=HEADS * count * 2 * length,
        ),
        name="attend_windows",
    )(*plan, doc_starts, in_hbm(folded), single, in_hbm(w_value), *stores)


def chip_ring(mesh):
    row = mesh.devices.reshape(-1, mesh.shape["seq"])[0]
    chips = list(range(len(row) // CORES))
    columns = [tuple(getattr(row[CORES * chip], "coords", (0, 0))[:2]) for chip in chips]
    if len(set(columns)) != 2:
        return chips
    up = [chip for chip in chips if columns[chip] == columns[0]]
    return up + [chip for chip in reversed(chips) if columns[chip] != columns[0]]


def after(values, others):
    return list(lax.optimization_barrier((tuple(values), tuple(others)))[0])


def body(ring, queries, neighbours, w_key, w_value, retrieval_owner, retrieval_slot, doc_starts):
    devices = lax.axis_size("seq")
    size = len(ring)
    reach = (size - 1) // 2

    ways = [
        (CORES * ring[i] + core, CORES * ring[(i + way) % size] + core)
        for i in range(size)
        for core, way in enumerate((1, -1))
    ]
    onwards = functools.partial(lax.ppermute, axis_name="seq", perm=ways)
    swapped = functools.partial(lax.ppermute, axis_name="seq", perm=[(i, i ^ 1) for i in range(devices)])

    stored = neighbours.shape[0]
    wanted = (retrieval_owner * stored + retrieval_slot).T
    chains = [neighbours, swapped(neighbours)]
    stores = [neighbours, in_hbm(chains[1])]
    folded, single = fold(*after([queries], [chains[1]]), w_key)

    asked = after([wanted], [single])[0]
    before = lax.ppermute(asked, "seq", [(i, i + 1) for i in range(devices - 1)])
    beside = {(1, 0): [folded, single], (1, 1): [before]}
    for step in range(reach):
        for chain in range(2):
            others = beside.get((step, chain), []) + (stores[2 * chain + 4 * step - 5 :][:1] if step > 1 else [])
            sent = after([chains[chain]], others) if others else [chains[chain]]
            chains[chain] = onwards(sent[0])
            stores += [chains[chain], in_hbm(swapped(chains[chain]))]
    places = jnp.asarray([ring.index(chip) for chip in range(size)], jnp.int32)
    plan = [lax.axis_index("seq").reshape(1), places, before, wanted]
    if size % 2 == 0:
        sent = after([chains[0]], [before, *stores[-7:-4:2]]) if reach > 1 else [chains[0]]
        last = onwards(sent[0])
        if reach:
            stores[-1] = swapped(after([chains[1]], [last, stores[-3]])[0])
        stores += [last, swapped(last)]
    return attend(size, plan, doc_starts, folded, single, w_value, stores)


def solution(mesh):
    return jax.shard_map(
        functools.partial(body, chip_ring(mesh)),
        mesh=mesh,
        in_specs=(
            P(("groups", "seq"), None),
            P(("groups", "seq"), None, None),
            P(),
            P(),
            P(("groups", "seq"), None),
            P(("groups", "seq"), None),
            P(("groups", "seq")),
        ),
        out_specs=P(("groups", "seq"), None),
        check_vma=False,
    )
```

```python
import functools
import math

import jax
import jax.numpy as jnp
from jax import lax
from jax.experimental import pallas as pl
from jax.experimental.pallas import tpu as pltpu
from jax.sharding import PartitionSpec as P

SPAN = 64
HEADS = 16
HEAD_DIM = 128
EPS = 1e-6
SCALE = math.log2(math.e) / math.sqrt(HEAD_DIM)
CORES = 2
GROUP = 4
FOLDS = 2
MIB = 2**20


SMEM_SPEC = pl.BlockSpec(memory_space=pltpu.SMEM)
VMEM_SPEC = pl.BlockSpec(memory_space=pltpu.VMEM)
ANY_SPEC = pl.BlockSpec(memory_space=pl.ANY)
HBM_SPEC = pl.BlockSpec(memory_space=pltpu.HBM)


def contract(left, right, dims):
    return lax.dot_general(left, right, (dims, ((), ())), preferred_element_type=jnp.float32)


def in_hbm(value):
    return pltpu.with_memory_space_constraint(value, pltpu.HBM)


def head_columns(head):
    return slice(head * HEAD_DIM, (head + 1) * HEAD_DIM)


def group_heads(group):
    return pl.ds(group * GROUP, GROUP)


def group_columns(group):
    return pl.ds(group * GROUP * HEAD_DIM, GROUP * HEAD_DIM)


def fold_kernel(first, query_hbm, key_hbm, folded_hbm, single_ref, query, key, folded, in_sems, out_sems):
    heads = folded.shape[0]

    def fetch(group):
        columns, held = group_columns(first // GROUP + group), group_columns(group)
        return (
            pltpu.make_async_copy(query_hbm.at[:, columns], query.at[:, held], in_sems.at[group, 0]),
            pltpu.make_async_copy(key_hbm.at[:, columns], key.at[:, held], in_sems.at[group, 1]),
        )

    def put(head):
        return pltpu.make_async_copy(folded.at[head], folded_hbm.at[head], out_sems.at[head])

    for group in range(heads // GROUP):
        for copy in fetch(group):
            copy.start()
    for head in range(heads):
        if head % GROUP == 0:
            for copy in fetch(head // GROUP):
                copy.wait()
        columns = head_columns(head)
        queries = pltpu.roll(query[:, columns].astype(jnp.float32), 1, 0).astype(jnp.bfloat16)
        rows = contract(queries, key[:, columns], ((1,), (1,))) * SCALE
        single_ref[head : head + 1, :] = rows[:1]
        folded[head] = rows.astype(jnp.bfloat16)
        put(head).start()
    for head in range(heads):
        put(head).wait()


def fold(first, heads, queries, w_key):
    count, width = queries.shape[0], w_key.shape[0]
    shape, columns = (heads, count, width), heads * HEAD_DIM
    return pl.pallas_call(
        functools.partial(fold_kernel, first),
        out_shape=(
            pltpu.HBM(shape, jnp.bfloat16),
            jax.ShapeDtypeStruct((heads, width), jnp.float32),
        ),
        in_specs=[HBM_SPEC] * 2,
        out_specs=(HBM_SPEC, VMEM_SPEC),
        scratch_shapes=[
            pltpu.VMEM((count, columns), jnp.bfloat16),
            pltpu.VMEM((width, columns), jnp.bfloat16),
            pltpu.VMEM(shape, jnp.bfloat16),
            pltpu.SemaphoreType.DMA((heads // GROUP, 2)),
            pltpu.SemaphoreType.DMA((heads,)),
        ],
        compiler_params=pltpu.CompilerParams(vmem_limit_bytes=16 * MIB),
        cost_estimate=pl.CostEstimate(
            flops=2 * count * columns * width, bytes_accessed=6 * MIB, transcendentals=0
        ),
        name="fold_queries",
    )(in_hbm(queries), in_hbm(w_key))


def normalise(raw, tokens_ref):
    widened = raw.astype(jnp.float32)
    factor = lax.rsqrt(jnp.mean(widened * widened, axis=-1, keepdims=True) + EPS)
    tokens_ref[...] = (widened * factor).astype(jnp.bfloat16)


def among(stores, first, source, act):
    if len(stores) == 1:
        pl.when(source == first)(lambda: act(stores[0]))
        return
    half = len(stores) // 2
    pl.when(source < first + half)(lambda: among(stores[:half], first, source, act))
    pl.when(source >= first + half)(lambda: among(stores[half:], first + half, source, act))


def locate(request, plan_refs, size, stored):
    here_ref, place_ref, before_ref, wanted_ref = plan_refs
    window, part = divmod(request, 2)
    wanted = before_ref[part, before_ref.shape[1] - 1] if window == 0 else wanted_ref[part, window - 1]
    owner, slot = wanted // stored, wanted % stored
    reach = (size - 1) // 2
    opposite = size - reach - 1
    here = here_ref[0]
    away = place_ref[here // CORES] - place_ref[owner // CORES]
    away = jnp.where(away < 0, away + size, away)
    core = owner % CORES
    holder = jnp.where((away == 0) | ((away > reach) & (away <= opposite)), core, jnp.where(away <= reach, 0, 1))
    step = jnp.where(away <= opposite, away, size - away)
    arrival = jnp.where(away == 0, 0, 2 * step - 1 + jnp.where(core == holder, 0, 1))
    return CORES * arrival + jnp.where(holder == here % CORES, 0, 1), slot


def weigh(scores):
    powers = jnp.exp2(scores - jnp.max(scores, axis=-1, keepdims=True))
    totals = jnp.sum(powers, axis=-1, keepdims=True)
    return (powers * (1.0 / totals)).astype(jnp.bfloat16)


def attend_kernel(size, *refs):
    plan_refs, (starts_ref, *folds, value_hbm) = refs[:4], refs[4 : 6 + 2 * FOLDS]
    rest = refs[6 + 2 * FOLDS :]
    *stores, out_hbm, tokens, raw, folded, value, scores, weights, mixed, out, sems, group_sems = rest
    requests, length, width = raw.shape
    blocks = requests // 2 - 1
    count = blocks * SPAN
    rows_at_once = GROUP * SPAN
    groups = HEADS // GROUP
    lone_window = blocks
    order = [*range(1, blocks), lone_window, 0]

    def fetch(request, store, block):
        return pltpu.make_async_copy(store.at[block], raw.at[request], sems.at[request])

    def fetch_group(group):
        columns = group_columns(group)
        piece, place = divmod(group, groups // FOLDS)
        return (
            pltpu.make_async_copy(
                folds[piece].at[group_heads(place)], folded.at[group_heads(group)], group_sems.at[group, 0]
            ),
            pltpu.make_async_copy(value_hbm.at[:, columns], value.at[:, columns], group_sems.at[group, 1]),
        )

    def put(group):
        columns = group_columns(group)
        return pltpu.make_async_copy(out.at[:, columns], out_hbm.at[:, columns], group_sems.at[group, 2])

    for window in order:
        for request in (2 * window, 2 * window + 1):
            source, block = locate(request, plan_refs, size, stores[0].shape[0])
            among(stores, 0, source, lambda store: fetch(request, store, block).start())
        if window == order[0]:
            fetch_group(0)[0].start()
    fetch_group(0)[1].start()
    for group in range(1, groups):
        for copy in fetch_group(group):
            copy.start()

    place = lax.broadcasted_iota(jnp.int32, (count, HEAD_DIM), 0)
    kept = place % SPAN == 0
    for block in range(blocks):
        fresh = starts_ref[block] == 0
        if block == 0:
            fresh = fresh & (plan_refs[0][0] > 0)
        kept = kept | ((place // SPAN == block) & fresh)

    def ready(window):
        for request in (2 * window, 2 * window + 1):
            fetch(request, stores[0], 0).wait()
        for request in (2 * window, 2 * window + 1):
            normalise(raw[request], tokens.at[request])

    def single_rows():
        return jnp.concatenate([single_ref[...] for single_ref in folds[FOLDS:]], axis=0).astype(jnp.bfloat16)

    def along(window):
        return tokens[2 * window : 2 * window + 2].reshape(2 * length, width)

    units = [(group, window) for group in range(groups) for window in order if group == 0 or window != lone_window]
    lone = {}

    def place_of(unit):
        group, window = units[unit]
        heads, rows = slice(group * GROUP, (group + 1) * GROUP), slice(window * SPAN, (window + 1) * SPAN)
        return unit % len(scores), heads, rows

    def score(unit):
        window = units[unit][1]
        if window == lone_window:
            lone["scores"] = contract(single_rows(), along(window), ((1,), (1,)))
            return
        slot, heads, rows = place_of(unit)
        taken = folded[heads, rows].reshape(rows_at_once, width)
        scores[slot] = contract(taken, along(window), ((1,), (1,)))

    parts = GROUP
    tile = -(-width // (parts * 128)) * 128

    def soften(unit, part):
        if units[unit][1] == lone_window:
            if part == 0:
                lone["weights"] = weigh(lone["scores"])
            return
        slot, _, _ = place_of(unit)
        rows = slice(part * SPAN, (part + 1) * SPAN)
        weights[slot, rows] = weigh(scores[slot, rows])

    def combine(unit, part):
        window = units[unit][1]
        columns = slice(part * tile, min(width, (part + 1) * tile))
        keys = tokens[2 * window : 2 * window + 2, :, columns].reshape(2 * length, columns.stop - columns.start)
        if window == lone_window:
            lone["sums", part] = contract(lone["weights"], keys, ((1,), (0,)))
            return
        slot, heads, rows = place_of(unit)
        sums = contract(weights[slot], keys, ((1,), (0,))).reshape(GROUP, SPAN, columns.stop - columns.start)
        if window == 0:
            first = lax.broadcasted_iota(jnp.int32, sums.shape, 1) == 0
            sums = jnp.where(first, lone["sums", part][heads][:, None, :], sums)
        mixed[units[unit][0] % 2, :, rows, columns] = sums.astype(jnp.bfloat16)

    def project(group):
        for head in range(group * GROUP, (group + 1) * GROUP):
            columns = head_columns(head)
            sums = contract(mixed[group % 2, head % GROUP], value[:, columns], ((1,), (0,)))
            sums = jnp.where(kept, sums, 0.0)
            out[:, columns] = pltpu.roll(sums, count - 1, 0).astype(jnp.bfloat16)
        put(group).start()

    ready(order[0])
    for step in range(len(units) + 2):
        if step == 0:
            fetch_group(0)[0].wait()
        if step == len(order):
            fetch_group(0)[1].wait()
            for group in range(1, groups):
                for copy in fetch_group(group):
                    copy.wait()
        if step + 1 < len(order):
            ready(order[step + 1])
        if step < len(units):
            score(step)
        for part in range(parts):
            if 1 <= step <= len(units):
                soften(step - 1, part)
            if step >= 2:
                combine(step - 2, part)
        if step >= 2 and units[step - 2][1] == order[-1]:
            project(units[step - 2][0])
    for group in range(groups):
        put(group).wait()


def attend(size, plan, doc_starts, folds, w_value, stores):
    folded, single = zip(*folds)
    requests = plan[-1].size + 2
    length, width = stores[0].shape[1:]
    count = folded[0].shape[1]
    groups = HEADS // GROUP
    model_width = w_value.shape[1]
    return pl.pallas_call(
        functools.partial(attend_kernel, size),
        out_shape=jax.ShapeDtypeStruct((count, model_width), jnp.bfloat16),
        in_specs=[SMEM_SPEC] * 5
        + [HBM_SPEC] * FOLDS
        + [VMEM_SPEC] * FOLDS
        + [HBM_SPEC]
        + [ANY_SPEC] * len(stores),
        out_specs=HBM_SPEC,
        scratch_shapes=[
            pltpu.VMEM((requests, length, width), jnp.bfloat16),
            pltpu.VMEM((requests, length, width), jnp.bfloat16),
            pltpu.VMEM((HEADS, count, width), jnp.bfloat16),
            pltpu.VMEM(w_value.shape, jnp.bfloat16),
            pltpu.VMEM((5, GROUP * SPAN, 2 * length), jnp.float32),
            pltpu.VMEM((5, GROUP * SPAN, 2 * length), jnp.bfloat16),
            pltpu.VMEM((2, GROUP, count, width), jnp.bfloat16),
            pltpu.VMEM((count, model_width), jnp.bfloat16),
            pltpu.SemaphoreType.DMA((requests,)),
            pltpu.SemaphoreType.DMA((groups, 3)),
        ],
        compiler_params=pltpu.CompilerParams(vmem_limit_bytes=28 * MIB),
        cost_estimate=pl.CostEstimate(
            flops=2 * HEADS * count * width * (4 * length + HEAD_DIM),
            bytes_accessed=16 * MIB,
            transcendentals=HEADS * count * 2 * length,
        ),
        name="attend_windows",
    )(*plan, doc_starts, *map(in_hbm, folded), *single, in_hbm(w_value), *stores)


def chip_ring(mesh):
    row = mesh.devices.reshape(-1, mesh.shape["seq"])[0]
    chips = list(range(len(row) // CORES))
    columns = [tuple(getattr(row[CORES * chip], "coords", (0, 0))[:2]) for chip in chips]
    if len(set(columns)) != 2:
        return chips
    up = [chip for chip in chips if columns[chip] == columns[0]]
    return up + [chip for chip in reversed(chips) if columns[chip] != columns[0]]


def after(values, others):
    return list(lax.optimization_barrier((tuple(values), tuple(others)))[0])


def body(ring, queries, neighbours, w_key, w_value, retrieval_owner, retrieval_slot, doc_starts):
    devices = lax.axis_size("seq")
    size = len(ring)
    reach = (size - 1) // 2

    ways = [
        (CORES * ring[i] + core, CORES * ring[(i + way) % size] + core)
        for i in range(size)
        for core, way in enumerate((1, -1))
    ]
    onwards = functools.partial(lax.ppermute, axis_name="seq", perm=ways)
    swapped = functools.partial(lax.ppermute, axis_name="seq", perm=[(i, i ^ 1) for i in range(devices)])

    stored = neighbours.shape[0]
    wanted = (retrieval_owner * stored + retrieval_slot).T
    chains = [neighbours, swapped(neighbours)]
    stores = [neighbours, in_hbm(chains[1])]
    half = HEADS // FOLDS
    folds = [fold(0, half, *after([queries], [chains[1]]), w_key)]

    asked = after([wanted], folds[0][1:])[0]
    before = lax.ppermute(asked, "seq", [(i, i + 1) for i in range(devices - 1)])
    beside = {(1, 0): folds[0], (1, 1): [before]}
    for step in range(reach):
        for chain in range(2):
            others = list(beside.get((step, chain), ())) + (stores[2 * chain + 4 * step - 5 :][:1] if step > 1 else [])
            sent = after([chains[chain]], others) if others else [chains[chain]]
            chains[chain] = onwards(sent[0])
            stores += [chains[chain], in_hbm(swapped(chains[chain]))]
            if (step, chain) == (0, 1):
                folds += [fold(part * half, half, *after([queries], [chains[1]]), w_key) for part in range(1, FOLDS)]
                beside[2, 0] = [value for part in folds[1:] for value in part]
    places = jnp.asarray([ring.index(chip) for chip in range(size)], jnp.int32)
    plan = [lax.axis_index("seq").reshape(1), places, before, wanted]
    if size % 2 == 0:
        sent = after([chains[0]], [before, *stores[-7:-4:2]]) if reach > 1 else [chains[0]]
        last = onwards(sent[0])
        if reach:
            stores[-1] = swapped(after([chains[1]], [last, stores[-3]])[0])
        stores += [last, swapped(last)]
    return attend(size, plan, doc_starts, folds, w_value, stores)


def solution(mesh):
    return jax.shard_map(
        functools.partial(body, chip_ring(mesh)),
        mesh=mesh,
        in_specs=(
            P(("groups", "seq"), None),
            P(("groups", "seq"), None, None),
            P(),
            P(),
            P(("groups", "seq"), None),
            P(("groups", "seq"), None),
            P(("groups", "seq")),
        ),
        out_specs=P(("groups", "seq"), None),
        check_vma=False,
    )
```

```python
import functools
import math

import jax
import jax.numpy as jnp
from jax import lax
from jax.experimental import pallas as pl
from jax.experimental.pallas import tpu as pltpu
from jax.sharding import PartitionSpec as P

SPAN = 64
HEADS = 16
HEAD_DIM = 128
EPS = 1e-6
SCALE = math.log2(math.e) / math.sqrt(HEAD_DIM)
CORES = 2
GROUP = 4
FOLDS = 2
MIB = 2**20


SMEM_SPEC = pl.BlockSpec(memory_space=pltpu.SMEM)
VMEM_SPEC = pl.BlockSpec(memory_space=pltpu.VMEM)
ANY_SPEC = pl.BlockSpec(memory_space=pl.ANY)
HBM_SPEC = pl.BlockSpec(memory_space=pltpu.HBM)


def contract(left, right, dims):
    return lax.dot_general(left, right, (dims, ((), ())), preferred_element_type=jnp.float32)


def in_hbm(value):
    return pltpu.with_memory_space_constraint(value, pltpu.HBM)


def head_columns(head):
    return slice(head * HEAD_DIM, (head + 1) * HEAD_DIM)


def group_heads(group):
    return pl.ds(group * GROUP, GROUP)


def group_columns(group):
    return pl.ds(group * GROUP * HEAD_DIM, GROUP * HEAD_DIM)


def fold_kernel(first, query_hbm, key_hbm, folded_hbm, single_ref, query, key, folded, in_sems, out_sems):
    heads = folded.shape[0]

    def fetch(group):
        columns, held = group_columns(first // GROUP + group), group_columns(group)
        return (
            pltpu.make_async_copy(query_hbm.at[:, columns], query.at[:, held], in_sems.at[group, 0]),
            pltpu.make_async_copy(key_hbm.at[:, columns], key.at[:, held], in_sems.at[group, 1]),
        )

    def put(head):
        return pltpu.make_async_copy(folded.at[head], folded_hbm.at[head], out_sems.at[head])

    for group in range(heads // GROUP):
        for copy in fetch(group):
            copy.start()
    for head in range(heads):
        if head % GROUP == 0:
            for copy in fetch(head // GROUP):
                copy.wait()
        columns = head_columns(head)
        queries = pltpu.roll(query[:, columns].astype(jnp.float32), 1, 0).astype(jnp.bfloat16)
        rows = contract(queries, key[:, columns], ((1,), (1,))) * SCALE
        single_ref[head : head + 1, :] = rows[:1]
        folded[head] = rows.astype(jnp.bfloat16)
        put(head).start()
    for head in range(heads):
        put(head).wait()


def fold(first, heads, queries, w_key):
    count, width = queries.shape[0], w_key.shape[0]
    shape, columns = (heads, count, width), heads * HEAD_DIM
    return pl.pallas_call(
        functools.partial(fold_kernel, first),
        out_shape=(
            pltpu.HBM(shape, jnp.bfloat16),
            jax.ShapeDtypeStruct((heads, width), jnp.float32),
        ),
        in_specs=[HBM_SPEC] * 2,
        out_specs=(HBM_SPEC, VMEM_SPEC),
        scratch_shapes=[
            pltpu.VMEM((count, columns), jnp.bfloat16),
            pltpu.VMEM((width, columns), jnp.bfloat16),
            pltpu.VMEM(shape, jnp.bfloat16),
            pltpu.SemaphoreType.DMA((heads // GROUP, 2)),
            pltpu.SemaphoreType.DMA((heads,)),
        ],
        compiler_params=pltpu.CompilerParams(vmem_limit_bytes=16 * MIB),
        cost_estimate=pl.CostEstimate(
            flops=2 * count * columns * width, bytes_accessed=6 * MIB, transcendentals=0
        ),
        name="fold_queries",
    )(in_hbm(queries), in_hbm(w_key))


def normalise(raw, tokens_ref):
    widened = raw.astype(jnp.float32)
    factor = lax.rsqrt(jnp.mean(widened * widened, axis=-1, keepdims=True) + EPS)
    tokens_ref[...] = (widened * factor).astype(jnp.bfloat16)


def among(stores, first, source, act):
    if len(stores) == 1:
        pl.when(source == first)(lambda: act(stores[0]))
        return
    half = len(stores) // 2
    pl.when(source < first + half)(lambda: among(stores[:half], first, source, act))
    pl.when(source >= first + half)(lambda: among(stores[half:], first + half, source, act))


def locate(request, plan_refs, size, stored):
    here_ref, place_ref, before_ref, wanted_ref = plan_refs
    window, part = divmod(request, 2)
    wanted = before_ref[part, before_ref.shape[1] - 1] if window == 0 else wanted_ref[part, window - 1]
    owner, slot = wanted // stored, wanted % stored
    reach = (size - 1) // 2
    opposite = size - reach - 1
    here = here_ref[0]
    away = place_ref[here // CORES] - place_ref[owner // CORES]
    away = jnp.where(away < 0, away + size, away)
    core = owner % CORES
    holder = jnp.where((away == 0) | ((away > reach) & (away <= opposite)), core, jnp.where(away <= reach, 0, 1))
    step = jnp.where(away <= opposite, away, size - away)
    arrival = jnp.where(away == 0, 0, 2 * step - 1 + jnp.where(core == holder, 0, 1))
    return CORES * arrival + jnp.where(holder == here % CORES, 0, 1), slot


def weigh(scores):
    powers = jnp.exp2(scores - jnp.max(scores, axis=-1, keepdims=True))
    totals = jnp.sum(powers, axis=-1, keepdims=True)
    return (powers * (1.0 / totals)).astype(jnp.bfloat16)


def attend_kernel(size, *refs):
    plan_refs, (starts_ref, *folds, value_hbm) = refs[:4], refs[4 : 6 + 2 * FOLDS]
    rest = refs[6 + 2 * FOLDS :]
    *stores, out_hbm, tokens, raw, folded, value, scores, weights, mixed, out, sems, group_sems = rest
    requests, length, width = raw.shape
    blocks = requests // 2 - 1
    count = blocks * SPAN
    rows_at_once = GROUP * SPAN
    groups = HEADS // GROUP
    lone_window = blocks
    order = [*range(1, blocks), lone_window, 0]

    def fetch(request, store, block):
        return pltpu.make_async_copy(store.at[block], raw.at[request], sems.at[request])

    def fetch_group(group):
        columns = group_columns(group)
        piece, place = divmod(group, groups // FOLDS)
        return (
            pltpu.make_async_copy(
                folds[piece].at[group_heads(place)], folded.at[group_heads(group)], group_sems.at[group, 0]
            ),
            pltpu.make_async_copy(value_hbm.at[:, columns], value.at[:, columns], group_sems.at[group, 1]),
        )

    def put(group):
        columns = group_columns(group)
        return pltpu.make_async_copy(out.at[:, columns], out_hbm.at[:, columns], group_sems.at[group, 2])

    for window in order:
        for request in (2 * window, 2 * window + 1):
            source, block = locate(request, plan_refs, size, stores[0].shape[0])
            among(stores, 0, source, lambda store: fetch(request, store, block).start())
        if window == order[0]:
            fetch_group(0)[0].start()
    fetch_group(0)[1].start()
    for group in range(1, groups):
        for copy in fetch_group(group):
            copy.start()

    place = lax.broadcasted_iota(jnp.int32, (count, HEAD_DIM), 0)
    kept = place % SPAN == 0
    for block in range(blocks):
        fresh = starts_ref[block] == 0
        if block == 0:
            fresh = fresh & (plan_refs[0][0] > 0)
        kept = kept | ((place // SPAN == block) & fresh)

    def ready(window):
        for request in (2 * window, 2 * window + 1):
            fetch(request, stores[0], 0).wait()
        for request in (2 * window, 2 * window + 1):
            normalise(raw[request], tokens.at[request])

    def single_rows():
        return jnp.concatenate([single_ref[...] for single_ref in folds[FOLDS:]], axis=0).astype(jnp.bfloat16)

    def along(window):
        return tokens[2 * window : 2 * window + 2].reshape(2 * length, width)

    units = [(group, window) for group in range(groups) for window in order if group == 0 or window != lone_window]
    lone = {}

    def place_of(unit):
        group, window = units[unit]
        heads, rows = slice(group * GROUP, (group + 1) * GROUP), slice(window * SPAN, (window + 1) * SPAN)
        return unit % len(scores), heads, rows

    def score(unit):
        window = units[unit][1]
        if window == lone_window:
            lone["scores"] = contract(single_rows(), along(window), ((1,), (1,)))
            return
        slot, heads, rows = place_of(unit)
        taken = folded[heads, rows].reshape(rows_at_once, width)
        scores[slot] = contract(taken, along(window), ((1,), (1,)))

    parts = GROUP
    tile = -(-width // (parts * 128)) * 128

    def soften(unit, part):
        if units[unit][1] == lone_window:
            if part == 0:
                lone["weights"] = weigh(lone["scores"])
            return
        slot, _, _ = place_of(unit)
        rows = slice(part * SPAN, (part + 1) * SPAN)
        weights[slot, rows] = weigh(scores[slot, rows])

    def combine(unit, part):
        window = units[unit][1]
        columns = slice(part * tile, min(width, (part + 1) * tile))
        keys = tokens[2 * window : 2 * window + 2, :, columns].reshape(2 * length, columns.stop - columns.start)
        if window == lone_window:
            lone["sums", part] = contract(lone["weights"], keys, ((1,), (0,)))
            return
        slot, heads, rows = place_of(unit)
        sums = contract(weights[slot], keys, ((1,), (0,))).reshape(GROUP, SPAN, columns.stop - columns.start)
        if window == 0:
            first = lax.broadcasted_iota(jnp.int32, sums.shape, 1) == 0
            sums = jnp.where(first, lone["sums", part][heads][:, None, :], sums)
        mixed[units[unit][0] % 2, :, rows, columns] = sums.astype(jnp.bfloat16)

    def project(group):
        for head in range(group * GROUP, (group + 1) * GROUP):
            columns = head_columns(head)
            sums = contract(mixed[group % 2, head % GROUP], value[:, columns], ((1,), (0,)))
            sums = jnp.where(kept, sums, 0.0)
            out[:, columns] = pltpu.roll(sums, count - 1, 0).astype(jnp.bfloat16)
        put(group).start()

    ready(order[0])
    for step in range(len(units) + 2):
        if step == 0:
            fetch_group(0)[0].wait()
        if step == len(order):
            fetch_group(0)[1].wait()
            for group in range(1, groups):
                for copy in fetch_group(group):
                    copy.wait()
        if step + 1 < len(order):
            ready(order[step + 1])
        if step < len(units):
            score(step)
        for part in range(parts):
            if 1 <= step <= len(units):
                soften(step - 1, part)
            if step >= 2:
                combine(step - 2, part)
        if step >= 2 and units[step - 2][1] == order[-1]:
            project(units[step - 2][0])
    for group in range(groups):
        put(group).wait()


def attend(size, plan, doc_starts, folds, w_value, stores):
    folded, single = zip(*folds)
    requests = plan[-1].size + 2
    length, width = stores[0].shape[1:]
    count = folded[0].shape[1]
    groups = HEADS // GROUP
    model_width = w_value.shape[1]
    return pl.pallas_call(
        functools.partial(attend_kernel, size),
        out_shape=jax.ShapeDtypeStruct((count, model_width), jnp.bfloat16),
        in_specs=[SMEM_SPEC] * 5
        + [HBM_SPEC] * FOLDS
        + [VMEM_SPEC] * FOLDS
        + [HBM_SPEC]
        + [ANY_SPEC] * len(stores),
        out_specs=HBM_SPEC,
        scratch_shapes=[
            pltpu.VMEM((requests, length, width), jnp.bfloat16),
            pltpu.VMEM((requests, length, width), jnp.bfloat16),
            pltpu.VMEM((HEADS, count, width), jnp.bfloat16),
            pltpu.VMEM(w_value.shape, jnp.bfloat16),
            pltpu.VMEM((5, GROUP * SPAN, 2 * length), jnp.float32),
            pltpu.VMEM((5, GROUP * SPAN, 2 * length), jnp.bfloat16),
            pltpu.VMEM((2, GROUP, count, width), jnp.bfloat16),
            pltpu.VMEM((count, model_width), jnp.bfloat16),
            pltpu.SemaphoreType.DMA((requests,)),
            pltpu.SemaphoreType.DMA((groups, 3)),
        ],
        compiler_params=pltpu.CompilerParams(vmem_limit_bytes=28 * MIB),
        cost_estimate=pl.CostEstimate(
            flops=2 * HEADS * count * width * (4 * length + HEAD_DIM),
            bytes_accessed=16 * MIB,
            transcendentals=HEADS * count * 2 * length,
        ),
        name="attend_windows",
    )(*plan, doc_starts, *map(in_hbm, folded), *single, in_hbm(w_value), *stores)


def chip_ring(mesh):
    row = mesh.devices.reshape(-1, mesh.shape["seq"])[0]
    chips = list(range(len(row) // CORES))
    columns = [tuple(getattr(row[CORES * chip], "coords", (0, 0))[:2]) for chip in chips]
    if len(set(columns)) != 2:
        return chips
    up = [chip for chip in chips if columns[chip] == columns[0]]
    return up + [chip for chip in reversed(chips) if columns[chip] != columns[0]]


def after(values, others):
    return list(lax.optimization_barrier((tuple(values), tuple(others)))[0])


def body(ring, queries, neighbours, w_key, w_value, retrieval_owner, retrieval_slot, doc_starts):
    devices = lax.axis_size("seq")
    size = len(ring)
    reach = (size - 1) // 2

    ways = [
        (CORES * ring[i] + core, CORES * ring[(i + way) % size] + core)
        for i in range(size)
        for core, way in enumerate((1, -1))
    ]
    onwards = functools.partial(lax.ppermute, axis_name="seq", perm=ways)
    swapped = functools.partial(lax.ppermute, axis_name="seq", perm=[(i, i ^ 1) for i in range(devices)])

    stored = neighbours.shape[0]
    wanted = (retrieval_owner * stored + retrieval_slot).T
    chains = [neighbours, swapped(neighbours)]
    stores = [neighbours, in_hbm(chains[1])]
    half = HEADS // FOLDS
    folds = [fold(0, half, *after([queries], [chains[1]]), w_key)]

    asked = after([wanted], folds[0][1:])[0]
    before = lax.ppermute(asked, "seq", [(i, i + 1) for i in range(devices - 1)])
    beside = {(1, 0): folds[0], (1, 1): [before]}
    for step in range(reach):
        for chain in range(2):
            others = list(beside.get((step, chain), ())) + (stores[2 * chain + 4 * step - 5 :][:1] if step > 1 else [])
            sent = after([chains[chain]], others) if others else [chains[chain]]
            chains[chain] = onwards(sent[0])
            stores += [chains[chain], in_hbm(swapped(chains[chain]))]
    places = jnp.asarray([ring.index(chip) for chip in range(size)], jnp.int32)
    plan = [lax.axis_index("seq").reshape(1), places, before, wanted]
    if size % 2 == 0:
        sent = after([chains[0]], [before, *stores[-7:-4:2]]) if reach > 1 else [chains[0]]
        last = onwards(sent[0])
        if reach:
            folds += [fold(part * half, half, *after([queries], [chains[0]]), w_key) for part in range(1, FOLDS)]
            others = [value for part in folds[1:] for value in part]
            stores[-1] = swapped(after([chains[1]], [last, stores[-3], *others])[0])
        stores += [last, swapped(last)]
    return attend(size, plan, doc_starts, folds, w_value, stores)


def solution(mesh):
    return jax.shard_map(
        functools.partial(body, chip_ring(mesh)),
        mesh=mesh,
        in_specs=(
            P(("groups", "seq"), None),
            P(("groups", "seq"), None, None),
            P(),
            P(),
            P(("groups", "seq"), None),
            P(("groups", "seq"), None),
            P(("groups", "seq")),
        ),
        out_specs=P(("groups", "seq"), None),
        check_vma=False,
    )
```

```python
import functools
import math

import jax
import jax.numpy as jnp
from jax import lax
from jax.experimental import pallas as pl
from jax.experimental.pallas import tpu as pltpu
from jax.sharding import PartitionSpec as P

SPAN = 64
HEADS = 16
HEAD_DIM = 128
EPS = 1e-6
SCALE = math.log2(math.e) / math.sqrt(HEAD_DIM)
CORES = 2
GROUP = 4
FOLDS = 2
MIB = 2**20


SMEM_SPEC = pl.BlockSpec(memory_space=pltpu.SMEM)
VMEM_SPEC = pl.BlockSpec(memory_space=pltpu.VMEM)
ANY_SPEC = pl.BlockSpec(memory_space=pl.ANY)
HBM_SPEC = pl.BlockSpec(memory_space=pltpu.HBM)


def contract(left, right, dims):
    return lax.dot_general(left, right, (dims, ((), ())), preferred_element_type=jnp.float32)


def in_hbm(value):
    return pltpu.with_memory_space_constraint(value, pltpu.HBM)


def head_columns(head):
    return slice(head * HEAD_DIM, (head + 1) * HEAD_DIM)


def group_heads(group):
    return pl.ds(group * GROUP, GROUP)


def group_columns(group):
    return pl.ds(group * GROUP * HEAD_DIM, GROUP * HEAD_DIM)


def fold_kernel(first, query_hbm, key_hbm, folded_hbm, single_ref, query, key, folded, in_sems, out_sems):
    heads = folded.shape[0]

    def fetch(group):
        columns, held = group_columns(first // GROUP + group), group_columns(group)
        return (
            pltpu.make_async_copy(query_hbm.at[:, columns], query.at[:, held], in_sems.at[group, 0]),
            pltpu.make_async_copy(key_hbm.at[:, columns], key.at[:, held], in_sems.at[group, 1]),
        )

    def put(head):
        return pltpu.make_async_copy(folded.at[head], folded_hbm.at[head], out_sems.at[head])

    for group in range(heads // GROUP):
        for copy in fetch(group):
            copy.start()
    for head in range(heads):
        if head % GROUP == 0:
            for copy in fetch(head // GROUP):
                copy.wait()
        columns = head_columns(head)
        queries = pltpu.roll(query[:, columns].astype(jnp.float32), 1, 0).astype(jnp.bfloat16)
        rows = contract(queries, key[:, columns], ((1,), (1,))) * SCALE
        single_ref[head : head + 1, :] = rows[:1]
        folded[head] = rows.astype(jnp.bfloat16)
        put(head).start()
    for head in range(heads):
        put(head).wait()


def fold(first, heads, queries, w_key):
    count, width = queries.shape[0], w_key.shape[0]
    shape, columns = (heads, count, width), heads * HEAD_DIM
    return pl.pallas_call(
        functools.partial(fold_kernel, first),
        out_shape=(
            pltpu.HBM(shape, jnp.bfloat16),
            jax.ShapeDtypeStruct((heads, width), jnp.float32),
        ),
        in_specs=[HBM_SPEC] * 2,
        out_specs=(HBM_SPEC, VMEM_SPEC),
        scratch_shapes=[
            pltpu.VMEM((count, columns), jnp.bfloat16),
            pltpu.VMEM((width, columns), jnp.bfloat16),
            pltpu.VMEM(shape, jnp.bfloat16),
            pltpu.SemaphoreType.DMA((heads // GROUP, 2)),
            pltpu.SemaphoreType.DMA((heads,)),
        ],
        compiler_params=pltpu.CompilerParams(vmem_limit_bytes=16 * MIB),
        cost_estimate=pl.CostEstimate(
            flops=2 * count * columns * width, bytes_accessed=6 * MIB, transcendentals=0
        ),
        name="fold_queries",
    )(in_hbm(queries), in_hbm(w_key))


def normalise(raw, tokens_ref):
    widened = raw.astype(jnp.float32)
    factor = lax.rsqrt(jnp.mean(widened * widened, axis=-1, keepdims=True) + EPS)
    tokens_ref[...] = (widened * factor).astype(jnp.bfloat16)


def among(stores, first, source, act):
    if len(stores) == 1:
        pl.when(source == first)(lambda: act(stores[0]))
        return
    half = len(stores) // 2
    pl.when(source < first + half)(lambda: among(stores[:half], first, source, act))
    pl.when(source >= first + half)(lambda: among(stores[half:], first + half, source, act))


def locate(request, plan_refs, size, stored):
    here_ref, place_ref, before_ref, wanted_ref = plan_refs
    window, part = divmod(request, 2)
    wanted = before_ref[part, before_ref.shape[1] - 1] if window == 0 else wanted_ref[part, window - 1]
    owner, slot = wanted // stored, wanted % stored
    reach = (size - 1) // 2
    opposite = size - reach - 1
    here = here_ref[0]
    away = place_ref[here // CORES] - place_ref[owner // CORES]
    away = jnp.where(away < 0, away + size, away)
    core = owner % CORES
    holder = jnp.where((away == 0) | ((away > reach) & (away <= opposite)), core, jnp.where(away <= reach, 0, 1))
    step = jnp.where(away <= opposite, away, size - away)
    arrival = jnp.where(away == 0, 0, 2 * step - 1 + jnp.where(core == holder, 0, 1))
    return CORES * arrival + jnp.where(holder == here % CORES, 0, 1), slot


def weigh(scores):
    powers = jnp.exp2(scores - jnp.max(scores, axis=-1, keepdims=True))
    totals = jnp.sum(powers, axis=-1, keepdims=True)
    return (powers * (1.0 / totals)).astype(jnp.bfloat16)


def attend_kernel(size, *refs):
    plan_refs, (starts_ref, *folds, value_hbm) = refs[:4], refs[4 : 6 + 2 * FOLDS]
    rest = refs[6 + 2 * FOLDS :]
    *stores, out_hbm, tokens, raw, folded, value, scores, weights, mixed, out, sems, group_sems = rest
    requests, length, width = raw.shape
    blocks = requests // 2 - 1
    count = blocks * SPAN
    rows_at_once = GROUP * SPAN
    groups = HEADS // GROUP
    lone_window = blocks
    order = [*range(1, blocks), lone_window, 0]

    def fetch(request, store, block):
        return pltpu.make_async_copy(store.at[block], raw.at[request], sems.at[request])

    def fetch_group(group):
        columns = group_columns(group)
        piece, place = divmod(group, groups // FOLDS)
        return (
            pltpu.make_async_copy(
                folds[piece].at[group_heads(place)], folded.at[group_heads(group)], group_sems.at[group, 0]
            ),
            pltpu.make_async_copy(value_hbm.at[:, columns], value.at[:, columns], group_sems.at[group, 1]),
        )

    def put(group):
        columns = group_columns(group)
        return pltpu.make_async_copy(out.at[:, columns], out_hbm.at[:, columns], group_sems.at[group, 2])

    for window in order:
        for request in (2 * window, 2 * window + 1):
            source, block = locate(request, plan_refs, size, stores[0].shape[0])
            among(stores, 0, source, lambda store: fetch(request, store, block).start())
        if window == order[0]:
            fetch_group(0)[0].start()
    fetch_group(0)[1].start()
    for group in range(1, groups):
        for copy in fetch_group(group):
            copy.start()

    place = lax.broadcasted_iota(jnp.int32, (count, HEAD_DIM), 0)
    kept = place % SPAN == 0
    for block in range(blocks):
        fresh = starts_ref[block] == 0
        if block == 0:
            fresh = fresh & (plan_refs[0][0] > 0)
        kept = kept | ((place // SPAN == block) & fresh)

    def ready(window):
        for request in (2 * window, 2 * window + 1):
            fetch(request, stores[0], 0).wait()
        for request in (2 * window, 2 * window + 1):
            normalise(raw[request], tokens.at[request])

    def single_rows():
        return jnp.concatenate([single_ref[...] for single_ref in folds[FOLDS:]], axis=0).astype(jnp.bfloat16)

    def along(window):
        return tokens[2 * window : 2 * window + 2].reshape(2 * length, width)

    units = [(group, window) for group in range(groups) for window in order if group == 0 or window != lone_window]
    lone = {}

    def place_of(unit):
        group, window = units[unit]
        heads, rows = slice(group * GROUP, (group + 1) * GROUP), slice(window * SPAN, (window + 1) * SPAN)
        return unit % len(scores), heads, rows

    def score(unit):
        window = units[unit][1]
        if window == lone_window:
            lone["scores"] = contract(single_rows(), along(window), ((1,), (1,)))
            return
        slot, heads, rows = place_of(unit)
        taken = folded[heads, rows].reshape(rows_at_once, width)
        scores[slot] = contract(taken, along(window), ((1,), (1,)))

    parts = GROUP
    tile = -(-width // (parts * 128)) * 128

    def soften(unit, part):
        if units[unit][1] == lone_window:
            if part == 0:
                lone["weights"] = weigh(lone["scores"])
            return
        slot, _, _ = place_of(unit)
        rows = slice(part * SPAN, (part + 1) * SPAN)
        weights[slot, rows] = weigh(scores[slot, rows])

    def combine(unit, part):
        window = units[unit][1]
        columns = slice(part * tile, min(width, (part + 1) * tile))
        keys = tokens[2 * window : 2 * window + 2, :, columns].reshape(2 * length, columns.stop - columns.start)
        if window == lone_window:
            lone["sums", part] = contract(lone["weights"], keys, ((1,), (0,)))
            return
        slot, heads, rows = place_of(unit)
        sums = contract(weights[slot], keys, ((1,), (0,))).reshape(GROUP, SPAN, columns.stop - columns.start)
        if window == 0:
            first = lax.broadcasted_iota(jnp.int32, sums.shape, 1) == 0
            sums = jnp.where(first, lone["sums", part][heads][:, None, :], sums)
        mixed[units[unit][0] % 2, :, rows, columns] = sums.astype(jnp.bfloat16)

    def project(group):
        for head in range(group * GROUP, (group + 1) * GROUP):
            columns = head_columns(head)
            sums = contract(mixed[group % 2, head % GROUP], value[:, columns], ((1,), (0,)))
            sums = jnp.where(kept, sums, 0.0)
            out[:, columns] = pltpu.roll(sums, count - 1, 0).astype(jnp.bfloat16)
        put(group).start()

    ready(order[0])
    for step in range(len(units) + 2):
        if step == 0:
            fetch_group(0)[0].wait()
        if step == len(order):
            fetch_group(0)[1].wait()
            for group in range(1, groups):
                for copy in fetch_group(group):
                    copy.wait()
        if step + 1 < len(order):
            ready(order[step + 1])
        if step < len(units):
            score(step)
        for part in range(parts):
            if 1 <= step <= len(units):
                soften(step - 1, part)
            if step >= 2:
                combine(step - 2, part)
        if step >= 2 and units[step - 2][1] == order[-1]:
            project(units[step - 2][0])
    for group in range(groups):
        put(group).wait()


def attend(size, plan, doc_starts, folds, w_value, stores):
    folded, single = zip(*folds)
    requests = plan[-1].size + 2
    length, width = stores[0].shape[1:]
    count = folded[0].shape[1]
    groups = HEADS // GROUP
    model_width = w_value.shape[1]
    return pl.pallas_call(
        functools.partial(attend_kernel, size),
        out_shape=jax.ShapeDtypeStruct((count, model_width), jnp.bfloat16),
        in_specs=[SMEM_SPEC] * 5
        + [HBM_SPEC] * FOLDS
        + [VMEM_SPEC] * FOLDS
        + [HBM_SPEC]
        + [ANY_SPEC] * len(stores),
        out_specs=HBM_SPEC,
        scratch_shapes=[
            pltpu.VMEM((requests, length, width), jnp.bfloat16),
            pltpu.VMEM((requests, length, width), jnp.bfloat16),
            pltpu.VMEM((HEADS, count, width), jnp.bfloat16),
            pltpu.VMEM(w_value.shape, jnp.bfloat16),
            pltpu.VMEM((5, GROUP * SPAN, 2 * length), jnp.float32),
            pltpu.VMEM((5, GROUP * SPAN, 2 * length), jnp.bfloat16),
            pltpu.VMEM((2, GROUP, count, width), jnp.bfloat16),
            pltpu.VMEM((count, model_width), jnp.bfloat16),
            pltpu.SemaphoreType.DMA((requests,)),
            pltpu.SemaphoreType.DMA((groups, 3)),
        ],
        compiler_params=pltpu.CompilerParams(vmem_limit_bytes=28 * MIB),
        cost_estimate=pl.CostEstimate(
            flops=2 * HEADS * count * width * (4 * length + HEAD_DIM),
            bytes_accessed=16 * MIB,
            transcendentals=HEADS * count * 2 * length,
        ),
        name="attend_windows",
    )(*plan, doc_starts, *map(in_hbm, folded), *single, in_hbm(w_value), *stores)


def chip_ring(mesh):
    row = mesh.devices.reshape(-1, mesh.shape["seq"])[0]
    chips = list(range(len(row) // CORES))
    columns = [tuple(getattr(row[CORES * chip], "coords", (0, 0))[:2]) for chip in chips]
    if len(set(columns)) != 2:
        return chips
    up = [chip for chip in chips if columns[chip] == columns[0]]
    return up + [chip for chip in reversed(chips) if columns[chip] != columns[0]]


def after(values, others):
    return list(lax.optimization_barrier((tuple(values), tuple(others)))[0])


def body(ring, queries, neighbours, w_key, w_value, retrieval_owner, retrieval_slot, doc_starts):
    devices = lax.axis_size("seq")
    size = len(ring)
    reach = (size - 1) // 2

    ways = [
        (CORES * ring[i] + core, CORES * ring[(i + way) % size] + core)
        for i in range(size)
        for core, way in enumerate((1, -1))
    ]
    onwards = functools.partial(lax.ppermute, axis_name="seq", perm=ways)
    swapped = functools.partial(lax.ppermute, axis_name="seq", perm=[(i, i ^ 1) for i in range(devices)])

    stored = neighbours.shape[0]
    wanted = (retrieval_owner * stored + retrieval_slot).T
    chains = [neighbours, swapped(neighbours)]
    stores = [neighbours, in_hbm(chains[1])]
    half = HEADS // FOLDS
    folds = [fold(0, half, *after([queries], [chains[1]]), w_key)]

    beside = {(1, 0): folds[0]}
    swaps = []
    for step in range(reach):
        for chain in range(2):
            others = list(beside.get((step, chain), ()))
            if step > 1:
                others.append(swaps[2 * step - 4 + chain])
            sent = after([chains[chain]], others) if others else [chains[chain]]
            chains[chain] = onwards(sent[0])
            swaps.append(swapped(chains[chain]))
            stores += [chains[chain], in_hbm(swaps[-1])]
    asked = after([wanted], chains[1:])[0]
    before = lax.ppermute(asked, "seq", [(i, i + 1) for i in range(devices - 1)])
    places = jnp.asarray([ring.index(chip) for chip in range(size)], jnp.int32)
    plan = [lax.axis_index("seq").reshape(1), places, before, wanted]
    if size % 2 == 0:
        sent = after([chains[0]], swaps[-4:-2]) if reach > 1 else [chains[0]]
        last = onwards(sent[0])
        if reach:
            folds += [fold(part * half, half, *after([queries], [chains[0]]), w_key) for part in range(1, FOLDS)]
            others = [value for part in folds[1:] for value in part]
            stores[-1] = swapped(after([chains[1]], [last, swaps[-2], before, *others])[0])
        stores += [last, swapped(last)]
    return attend(size, plan, doc_starts, folds, w_value, stores)


def solution(mesh):
    return jax.shard_map(
        functools.partial(body, chip_ring(mesh)),
        mesh=mesh,
        in_specs=(
            P(("groups", "seq"), None),
            P(("groups", "seq"), None, None),
            P(),
            P(),
            P(("groups", "seq"), None),
            P(("groups", "seq"), None),
            P(("groups", "seq")),
        ),
        out_specs=P(("groups", "seq"), None),
        check_vma=False,
    )
```

```python
import functools
import math

import jax
import jax.numpy as jnp
from jax import lax
from jax.experimental import pallas as pl
from jax.experimental.pallas import tpu as pltpu
from jax.sharding import PartitionSpec as P

SPAN = 64
HEADS = 16
HEAD_DIM = 128
EPS = 1e-6
SCALE = math.log2(math.e) / math.sqrt(HEAD_DIM)
CORES = 2
GROUP = 4
FOLDS = 1
MIB = 2**20


SMEM_SPEC = pl.BlockSpec(memory_space=pltpu.SMEM)
VMEM_SPEC = pl.BlockSpec(memory_space=pltpu.VMEM)
ANY_SPEC = pl.BlockSpec(memory_space=pl.ANY)
HBM_SPEC = pl.BlockSpec(memory_space=pltpu.HBM)


def contract(left, right, dims):
    return lax.dot_general(left, right, (dims, ((), ())), preferred_element_type=jnp.float32)


def in_hbm(value):
    return pltpu.with_memory_space_constraint(value, pltpu.HBM)


def head_columns(head):
    return slice(head * HEAD_DIM, (head + 1) * HEAD_DIM)


def group_heads(group):
    return pl.ds(group * GROUP, GROUP)


def group_columns(group):
    return pl.ds(group * GROUP * HEAD_DIM, GROUP * HEAD_DIM)


def fold_kernel(first, query_hbm, key_hbm, folded_hbm, single_ref, query, key, folded, in_sems, out_sems):
    heads = folded.shape[0]

    def fetch(group):
        columns, held = group_columns(first // GROUP + group), group_columns(group)
        return (
            pltpu.make_async_copy(query_hbm.at[:, columns], query.at[:, held], in_sems.at[group, 0]),
            pltpu.make_async_copy(key_hbm.at[:, columns], key.at[:, held], in_sems.at[group, 1]),
        )

    def put(head):
        return pltpu.make_async_copy(folded.at[head], folded_hbm.at[head], out_sems.at[head])

    for group in range(heads // GROUP):
        for copy in fetch(group):
            copy.start()
    for head in range(heads):
        if head % GROUP == 0:
            for copy in fetch(head // GROUP):
                copy.wait()
        columns = head_columns(head)
        queries = pltpu.roll(query[:, columns].astype(jnp.float32), 1, 0).astype(jnp.bfloat16)
        rows = contract(queries, key[:, columns], ((1,), (1,))) * SCALE
        single_ref[head : head + 1, :] = rows[:1]
        folded[head] = rows.astype(jnp.bfloat16)
        put(head).start()
    for head in range(heads):
        put(head).wait()


def fold(first, heads, queries, w_key):
    count, width = queries.shape[0], w_key.shape[0]
    shape, columns = (heads, count, width), heads * HEAD_DIM
    return pl.pallas_call(
        functools.partial(fold_kernel, first),
        out_shape=(
            pltpu.HBM(shape, jnp.bfloat16),
            jax.ShapeDtypeStruct((heads, width), jnp.float32),
        ),
        in_specs=[HBM_SPEC] * 2,
        out_specs=(HBM_SPEC, VMEM_SPEC),
        scratch_shapes=[
            pltpu.VMEM((count, columns), jnp.bfloat16),
            pltpu.VMEM((width, columns), jnp.bfloat16),
            pltpu.VMEM(shape, jnp.bfloat16),
            pltpu.SemaphoreType.DMA((heads // GROUP, 2)),
            pltpu.SemaphoreType.DMA((heads,)),
        ],
        compiler_params=pltpu.CompilerParams(vmem_limit_bytes=16 * MIB),
        cost_estimate=pl.CostEstimate(
            flops=2 * count * columns * width, bytes_accessed=6 * MIB, transcendentals=0
        ),
        name="fold_queries",
    )(in_hbm(queries), in_hbm(w_key))


def normalise(raw, tokens_ref):
    widened = raw.astype(jnp.float32)
    factor = lax.rsqrt(jnp.mean(widened * widened, axis=-1, keepdims=True) + EPS)
    tokens_ref[...] = (widened * factor).astype(jnp.bfloat16)


def among(stores, first, source, act):
    if len(stores) == 1:
        pl.when(source == first)(lambda: act(stores[0]))
        return
    half = len(stores) // 2
    pl.when(source < first + half)(lambda: among(stores[:half], first, source, act))
    pl.when(source >= first + half)(lambda: among(stores[half:], first + half, source, act))


def locate(request, plan_refs, size, stored):
    here_ref, place_ref, before_ref, wanted_ref = plan_refs
    window, part = divmod(request, 2)
    wanted = before_ref[part, before_ref.shape[1] - 1] if window == 0 else wanted_ref[part, window - 1]
    owner, slot = wanted // stored, wanted % stored
    reach = (size - 1) // 2
    opposite = size - reach - 1
    here = here_ref[0]
    away = place_ref[here // CORES] - place_ref[owner // CORES]
    away = jnp.where(away < 0, away + size, away)
    core = owner % CORES
    holder = jnp.where((away == 0) | ((away > reach) & (away <= opposite)), core, jnp.where(away <= reach, 0, 1))
    step = jnp.where(away <= opposite, away, size - away)
    arrival = jnp.where(away == 0, 0, 2 * step - 1 + jnp.where(core == holder, 0, 1))
    return CORES * arrival + jnp.where(holder == here % CORES, 0, 1), slot


def weigh(scores):
    powers = jnp.exp2(scores - jnp.max(scores, axis=-1, keepdims=True))
    totals = jnp.sum(powers, axis=-1, keepdims=True)
    return (powers * (1.0 / totals)).astype(jnp.bfloat16)


def attend_kernel(size, *refs):
    plan_refs, (starts_ref, *folds, value_hbm) = refs[:4], refs[4 : 6 + 2 * FOLDS]
    rest = refs[6 + 2 * FOLDS :]
    *stores, out_hbm, tokens, raw, folded, value, scores, weights, mixed, out, sems, group_sems = rest
    requests, length, width = raw.shape
    blocks = requests // 2 - 1
    count = blocks * SPAN
    rows_at_once = GROUP * SPAN
    groups = HEADS // GROUP
    lone_window = blocks
    order = [*range(1, blocks), lone_window, 0]

    def fetch(request, store, block):
        return pltpu.make_async_copy(store.at[block], raw.at[request], sems.at[request])

    def fetch_group(group):
        columns = group_columns(group)
        piece, place = divmod(group, groups // FOLDS)
        return (
            pltpu.make_async_copy(
                folds[piece].at[group_heads(place)], folded.at[group_heads(group)], group_sems.at[group, 0]
            ),
            pltpu.make_async_copy(value_hbm.at[:, columns], value.at[:, columns], group_sems.at[group, 1]),
        )

    def put(group):
        columns = group_columns(group)
        return pltpu.make_async_copy(out.at[:, columns], out_hbm.at[:, columns], group_sems.at[group, 2])

    for window in order:
        for request in (2 * window, 2 * window + 1):
            source, block = locate(request, plan_refs, size, stores[0].shape[0])
            among(stores, 0, source, lambda store: fetch(request, store, block).start())
        if window == order[0]:
            fetch_group(0)[0].start()
    fetch_group(0)[1].start()
    for group in range(1, groups):
        for copy in fetch_group(group):
            copy.start()

    place = lax.broadcasted_iota(jnp.int32, (count, HEAD_DIM), 0)
    kept = place % SPAN == 0
    for block in range(blocks):
        fresh = starts_ref[block] == 0
        if block == 0:
            fresh = fresh & (plan_refs[0][0] > 0)
        kept = kept | ((place // SPAN == block) & fresh)

    def ready(window):
        for request in (2 * window, 2 * window + 1):
            fetch(request, stores[0], 0).wait()
        for request in (2 * window, 2 * window + 1):
            normalise(raw[request], tokens.at[request])

    def single_rows():
        return jnp.concatenate([single_ref[...] for single_ref in folds[FOLDS:]], axis=0).astype(jnp.bfloat16)

    def along(window):
        return tokens[2 * window : 2 * window + 2].reshape(2 * length, width)

    units = [(group, window) for group in range(groups) for window in order if group == 0 or window != lone_window]
    lone = {}

    def place_of(unit):
        group, window = units[unit]
        heads, rows = slice(group * GROUP, (group + 1) * GROUP), slice(window * SPAN, (window + 1) * SPAN)
        return unit % len(scores), heads, rows

    def score(unit):
        window = units[unit][1]
        if window == lone_window:
            lone["scores"] = contract(single_rows(), along(window), ((1,), (1,)))
            return
        slot, heads, rows = place_of(unit)
        taken = folded[heads, rows].reshape(rows_at_once, width)
        scores[slot] = contract(taken, along(window), ((1,), (1,)))

    parts = GROUP
    tile = -(-width // (parts * 128)) * 128

    def soften(unit, part):
        if units[unit][1] == lone_window:
            if part == 0:
                lone["weights"] = weigh(lone["scores"])
            return
        slot, _, _ = place_of(unit)
        rows = slice(part * SPAN, (part + 1) * SPAN)
        weights[slot, rows] = weigh(scores[slot, rows])

    def combine(unit, part):
        window = units[unit][1]
        columns = slice(part * tile, min(width, (part + 1) * tile))
        keys = tokens[2 * window : 2 * window + 2, :, columns].reshape(2 * length, columns.stop - columns.start)
        if window == lone_window:
            lone["sums", part] = contract(lone["weights"], keys, ((1,), (0,)))
            return
        slot, heads, rows = place_of(unit)
        sums = contract(weights[slot], keys, ((1,), (0,))).reshape(GROUP, SPAN, columns.stop - columns.start)
        if window == 0:
            first = lax.broadcasted_iota(jnp.int32, sums.shape, 1) == 0
            sums = jnp.where(first, lone["sums", part][heads][:, None, :], sums)
        mixed[units[unit][0] % 2, :, rows, columns] = sums.astype(jnp.bfloat16)

    def project(group):
        for head in range(group * GROUP, (group + 1) * GROUP):
            columns = head_columns(head)
            sums = contract(mixed[group % 2, head % GROUP], value[:, columns], ((1,), (0,)))
            sums = jnp.where(kept, sums, 0.0)
            out[:, columns] = pltpu.roll(sums, count - 1, 0).astype(jnp.bfloat16)
        put(group).start()

    ready(order[0])
    for step in range(len(units) + 2):
        if step == 0:
            fetch_group(0)[0].wait()
        if step == len(order):
            fetch_group(0)[1].wait()
            for group in range(1, groups):
                for copy in fetch_group(group):
                    copy.wait()
        if step + 1 < len(order):
            ready(order[step + 1])
        if step < len(units):
            score(step)
        for part in range(parts):
            if 1 <= step <= len(units):
                soften(step - 1, part)
            if step >= 2:
                combine(step - 2, part)
        if step >= 2 and units[step - 2][1] == order[-1]:
            project(units[step - 2][0])
    for group in range(groups):
        put(group).wait()


def attend(size, plan, doc_starts, folds, w_value, stores):
    folded, single = zip(*folds)
    requests = plan[-1].size + 2
    length, width = stores[0].shape[1:]
    count = folded[0].shape[1]
    groups = HEADS // GROUP
    model_width = w_value.shape[1]
    return pl.pallas_call(
        functools.partial(attend_kernel, size),
        out_shape=jax.ShapeDtypeStruct((count, model_width), jnp.bfloat16),
        in_specs=[SMEM_SPEC] * 5
        + [HBM_SPEC] * FOLDS
        + [VMEM_SPEC] * FOLDS
        + [HBM_SPEC]
        + [ANY_SPEC] * len(stores),
        out_specs=HBM_SPEC,
        scratch_shapes=[
            pltpu.VMEM((requests, length, width), jnp.bfloat16),
            pltpu.VMEM((requests, length, width), jnp.bfloat16),
            pltpu.VMEM((HEADS, count, width), jnp.bfloat16),
            pltpu.VMEM(w_value.shape, jnp.bfloat16),
            pltpu.VMEM((5, GROUP * SPAN, 2 * length), jnp.float32),
            pltpu.VMEM((5, GROUP * SPAN, 2 * length), jnp.bfloat16),
            pltpu.VMEM((2, GROUP, count, width), jnp.bfloat16),
            pltpu.VMEM((count, model_width), jnp.bfloat16),
            pltpu.SemaphoreType.DMA((requests,)),
            pltpu.SemaphoreType.DMA((groups, 3)),
        ],
        compiler_params=pltpu.CompilerParams(vmem_limit_bytes=28 * MIB),
        cost_estimate=pl.CostEstimate(
            flops=2 * HEADS * count * width * (4 * length + HEAD_DIM),
            bytes_accessed=16 * MIB,
            transcendentals=HEADS * count * 2 * length,
        ),
        name="attend_windows",
    )(*plan, doc_starts, *map(in_hbm, folded), *single, in_hbm(w_value), *stores)


def chip_ring(mesh):
    row = mesh.devices.reshape(-1, mesh.shape["seq"])[0]
    chips = list(range(len(row) // CORES))
    columns = [tuple(getattr(row[CORES * chip], "coords", (0, 0))[:2]) for chip in chips]
    if len(set(columns)) != 2:
        return chips
    up = [chip for chip in chips if columns[chip] == columns[0]]
    return up + [chip for chip in reversed(chips) if columns[chip] != columns[0]]


def after(values, others):
    return list(lax.optimization_barrier((tuple(values), tuple(others)))[0])


def body(ring, queries, neighbours, w_key, w_value, retrieval_owner, retrieval_slot, doc_starts):
    devices = lax.axis_size("seq")
    size = len(ring)
    reach = (size - 1) // 2

    ways = [
        (CORES * ring[i] + core, CORES * ring[(i + way) % size] + core)
        for i in range(size)
        for core, way in enumerate((1, -1))
    ]
    onwards = functools.partial(lax.ppermute, axis_name="seq", perm=ways)
    swapped = functools.partial(lax.ppermute, axis_name="seq", perm=[(i, i ^ 1) for i in range(devices)])

    stored = neighbours.shape[0]
    wanted = (retrieval_owner * stored + retrieval_slot).T
    chains = [neighbours, swapped(neighbours)]
    stores = [neighbours, in_hbm(chains[1])]
    half = HEADS // FOLDS
    folds = [fold(0, half, *after([queries], [chains[1]]), w_key)]

    beside = {(1, 0): folds[0]}
    swaps = []
    for step in range(reach):
        for chain in range(2):
            others = list(beside.get((step, chain), ()))
            if step > 1:
                others.append(swaps[2 * step - 4 + chain])
            sent = after([chains[chain]], others) if others else [chains[chain]]
            chains[chain] = onwards(sent[0])
            swaps.append(swapped(chains[chain]))
            stores += [chains[chain], in_hbm(swaps[-1]) if step + 2 < reach else swaps[-1]]
    asked = after([wanted], chains[1:])[0]
    before = lax.ppermute(asked, "seq", [(i, i + 1) for i in range(devices - 1)])
    places = jnp.asarray([ring.index(chip) for chip in range(size)], jnp.int32)
    plan = [lax.axis_index("seq").reshape(1), places, before, wanted]
    if size % 2 == 0:
        last = onwards(chains[0])
        if reach:
            folds += [fold(part * half, half, *after([queries], [chains[0]]), w_key) for part in range(1, FOLDS)]
            others = [value for part in folds[1:] for value in part]
            stores[-1] = swapped(after([chains[1]], [last, *swaps[-4:-1], before, *others])[0])
        stores += [last, swapped(last)]
    return attend(size, plan, doc_starts, folds, w_value, stores)


def solution(mesh):
    return jax.shard_map(
        functools.partial(body, chip_ring(mesh)),
        mesh=mesh,
        in_specs=(
            P(("groups", "seq"), None),
            P(("groups", "seq"), None, None),
            P(),
            P(),
            P(("groups", "seq"), None),
            P(("groups", "seq"), None),
            P(("groups", "seq")),
        ),
        out_specs=P(("groups", "seq"), None),
        check_vma=False,
    )
```

```python
import functools
import math

import jax
import jax.numpy as jnp
from jax import lax
from jax.experimental import pallas as pl
from jax.experimental.pallas import tpu as pltpu
from jax.sharding import PartitionSpec as P

SPAN = 64
HEADS = 16
HEAD_DIM = 128
EPS = 1e-6
SCALE = math.log2(math.e) / math.sqrt(HEAD_DIM)
CORES = 2
GROUP = 4
FOLDS = 1
MIB = 2**20


SMEM_SPEC = pl.BlockSpec(memory_space=pltpu.SMEM)
VMEM_SPEC = pl.BlockSpec(memory_space=pltpu.VMEM)
ANY_SPEC = pl.BlockSpec(memory_space=pl.ANY)
HBM_SPEC = pl.BlockSpec(memory_space=pltpu.HBM)


def contract(left, right, dims):
    return lax.dot_general(left, right, (dims, ((), ())), preferred_element_type=jnp.float32)


def in_hbm(value):
    return pltpu.with_memory_space_constraint(value, pltpu.HBM)


def head_columns(head):
    return slice(head * HEAD_DIM, (head + 1) * HEAD_DIM)


def group_heads(group):
    return pl.ds(group * GROUP, GROUP)


def group_columns(group):
    return pl.ds(group * GROUP * HEAD_DIM, GROUP * HEAD_DIM)


def fold_kernel(first, query_hbm, key_hbm, folded_hbm, single_ref, query, key, folded, in_sems, out_sems):
    heads = folded.shape[0]

    def fetch(group):
        columns, held = group_columns(first // GROUP + group), group_columns(group)
        return (
            pltpu.make_async_copy(query_hbm.at[:, columns], query.at[:, held], in_sems.at[group, 0]),
            pltpu.make_async_copy(key_hbm.at[:, columns], key.at[:, held], in_sems.at[group, 1]),
        )

    def put(head):
        return pltpu.make_async_copy(folded.at[head], folded_hbm.at[head], out_sems.at[head])

    for group in range(heads // GROUP):
        for copy in fetch(group):
            copy.start()
    for head in range(heads):
        if head % GROUP == 0:
            for copy in fetch(head // GROUP):
                copy.wait()
        columns = head_columns(head)
        queries = pltpu.roll(query[:, columns].astype(jnp.float32), 1, 0).astype(jnp.bfloat16)
        rows = contract(queries, key[:, columns], ((1,), (1,))) * SCALE
        single_ref[head : head + 1, :] = rows[:1]
        folded[head] = rows.astype(jnp.bfloat16)
        put(head).start()
    for head in range(heads):
        put(head).wait()


def fold(first, heads, queries, w_key):
    count, width = queries.shape[0], w_key.shape[0]
    shape, columns = (heads, count, width), heads * HEAD_DIM
    return pl.pallas_call(
        functools.partial(fold_kernel, first),
        out_shape=(
            pltpu.HBM(shape, jnp.bfloat16),
            jax.ShapeDtypeStruct((heads, width), jnp.float32),
        ),
        in_specs=[HBM_SPEC] * 2,
        out_specs=(HBM_SPEC, VMEM_SPEC),
        scratch_shapes=[
            pltpu.VMEM((count, columns), jnp.bfloat16),
            pltpu.VMEM((width, columns), jnp.bfloat16),
            pltpu.VMEM(shape, jnp.bfloat16),
            pltpu.SemaphoreType.DMA((heads // GROUP, 2)),
            pltpu.SemaphoreType.DMA((heads,)),
        ],
        compiler_params=pltpu.CompilerParams(vmem_limit_bytes=16 * MIB),
        cost_estimate=pl.CostEstimate(
            flops=2 * count * columns * width, bytes_accessed=6 * MIB, transcendentals=0
        ),
        name="fold_queries",
    )(in_hbm(queries), in_hbm(w_key))


def normalise(raw, tokens_ref):
    widened = raw.astype(jnp.float32)
    factor = lax.rsqrt(jnp.mean(widened * widened, axis=-1, keepdims=True) + EPS)
    tokens_ref[...] = (widened * factor).astype(jnp.bfloat16)


def among(stores, first, source, act):
    if len(stores) == 1:
        pl.when(source == first)(lambda: act(stores[0]))
        return
    half = len(stores) // 2
    pl.when(source < first + half)(lambda: among(stores[:half], first, source, act))
    pl.when(source >= first + half)(lambda: among(stores[half:], first + half, source, act))


def locate(request, plan_refs, size, stored):
    here_ref, place_ref, before_ref, wanted_ref = plan_refs
    window, part = divmod(request, 2)
    wanted = before_ref[part, before_ref.shape[1] - 1] if window == 0 else wanted_ref[part, window - 1]
    owner, slot = wanted // stored, wanted % stored
    reach = (size - 1) // 2
    opposite = size - reach - 1
    here = here_ref[0]
    away = place_ref[here // CORES] - place_ref[owner // CORES]
    away = jnp.where(away < 0, away + size, away)
    core = owner % CORES
    holder = jnp.where((away == 0) | ((away > reach) & (away <= opposite)), core, jnp.where(away <= reach, 0, 1))
    step = jnp.where(away <= opposite, away, size - away)
    arrival = jnp.where(away == 0, 0, 2 * step - 1 + jnp.where(core == holder, 0, 1))
    return CORES * arrival + jnp.where(holder == here % CORES, 0, 1), slot


def weigh(scores):
    powers = jnp.exp2(scores - jnp.max(scores, axis=-1, keepdims=True))
    totals = jnp.sum(powers, axis=-1, keepdims=True)
    return (powers * (1.0 / totals)).astype(jnp.bfloat16)


def attend_kernel(size, *refs):
    plan_refs, (starts_ref, *folds, value_hbm) = refs[:4], refs[4 : 6 + 2 * FOLDS]
    rest = refs[6 + 2 * FOLDS :]
    *stores, out_hbm, tokens, raw, folded, value, scores, weights, mixed, out, sems, group_sems = rest
    requests, length, width = raw.shape
    blocks = requests // 2 - 1
    count = blocks * SPAN
    rows_at_once = GROUP * SPAN
    groups = HEADS // GROUP
    lone_window = blocks
    order = [*range(1, blocks), lone_window, 0]

    def fetch(request, store, block):
        return pltpu.make_async_copy(store.at[block], raw.at[request], sems.at[request])

    def fetch_group(group):
        columns = group_columns(group)
        piece, place = divmod(group, groups // FOLDS)
        return (
            pltpu.make_async_copy(
                folds[piece].at[group_heads(place)], folded.at[group_heads(group)], group_sems.at[group, 0]
            ),
            pltpu.make_async_copy(value_hbm.at[:, columns], value.at[:, columns], group_sems.at[group, 1]),
        )

    def put(group):
        columns = group_columns(group)
        return pltpu.make_async_copy(out.at[:, columns], out_hbm.at[:, columns], group_sems.at[group, 2])

    for window in order:
        for request in (2 * window, 2 * window + 1):
            source, block = locate(request, plan_refs, size, stores[0].shape[0])
            among(stores, 0, source, lambda store: fetch(request, store, block).start())
        if window == order[0]:
            fetch_group(0)[0].start()
    fetch_group(0)[1].start()
    for group in range(1, groups):
        for copy in fetch_group(group):
            copy.start()

    place = lax.broadcasted_iota(jnp.int32, (count, HEAD_DIM), 0)
    kept = place % SPAN == 0
    for block in range(blocks):
        fresh = starts_ref[block] == 0
        if block == 0:
            fresh = fresh & (plan_refs[0][0] > 0)
        kept = kept | ((place // SPAN == block) & fresh)

    def ready(window):
        for request in (2 * window, 2 * window + 1):
            fetch(request, stores[0], 0).wait()
        for request in (2 * window, 2 * window + 1):
            normalise(raw[request], tokens.at[request])

    def single_rows():
        return jnp.concatenate([single_ref[...] for single_ref in folds[FOLDS:]], axis=0).astype(jnp.bfloat16)

    def along(window):
        return tokens[2 * window : 2 * window + 2].reshape(2 * length, width)

    units = [(group, window) for group in range(groups) for window in order if group == 0 or window != lone_window]
    lone = {}

    def place_of(unit):
        group, window = units[unit]
        heads, rows = slice(group * GROUP, (group + 1) * GROUP), slice(window * SPAN, (window + 1) * SPAN)
        return unit % len(scores), heads, rows

    def score(unit):
        window = units[unit][1]
        if window == lone_window:
            lone["scores"] = contract(single_rows(), along(window), ((1,), (1,)))
            return
        slot, heads, rows = place_of(unit)
        taken = folded[heads, rows].reshape(rows_at_once, width)
        scores[slot] = contract(taken, along(window), ((1,), (1,)))

    parts = GROUP
    tile = -(-width // (parts * 128)) * 128

    def soften(unit, part):
        if units[unit][1] == lone_window:
            if part == 0:
                lone["weights"] = weigh(lone["scores"])
            return
        slot, _, _ = place_of(unit)
        rows = slice(part * SPAN, (part + 1) * SPAN)
        weights[slot, rows] = weigh(scores[slot, rows])

    def combine(unit, part):
        window = units[unit][1]
        columns = slice(part * tile, min(width, (part + 1) * tile))
        keys = tokens[2 * window : 2 * window + 2, :, columns].reshape(2 * length, columns.stop - columns.start)
        if window == lone_window:
            lone["sums", part] = contract(lone["weights"], keys, ((1,), (0,)))
            return
        slot, heads, rows = place_of(unit)
        sums = contract(weights[slot], keys, ((1,), (0,))).reshape(GROUP, SPAN, columns.stop - columns.start)
        if window == 0:
            first = lax.broadcasted_iota(jnp.int32, sums.shape, 1) == 0
            sums = jnp.where(first, lone["sums", part][heads][:, None, :], sums)
        mixed[units[unit][0] % 2, :, rows, columns] = sums.astype(jnp.bfloat16)

    def project(group):
        for head in range(group * GROUP, (group + 1) * GROUP):
            columns = head_columns(head)
            sums = contract(mixed[group % 2, head % GROUP], value[:, columns], ((1,), (0,)))
            sums = jnp.where(kept, sums, 0.0)
            out[:, columns] = pltpu.roll(sums, count - 1, 0).astype(jnp.bfloat16)
        put(group).start()

    ready(order[0])
    for step in range(len(units) + 2):
        if step == 0:
            fetch_group(0)[0].wait()
        if step == len(order):
            fetch_group(0)[1].wait()
            for group in range(1, groups):
                for copy in fetch_group(group):
                    copy.wait()
        if step + 1 < len(order):
            ready(order[step + 1])
        if step < len(units):
            score(step)
        for part in range(parts):
            if 1 <= step <= len(units):
                soften(step - 1, part)
            if step >= 2:
                combine(step - 2, part)
        if step >= 2 and units[step - 2][1] == order[-1]:
            project(units[step - 2][0])
    for group in range(groups):
        put(group).wait()


def attend(size, plan, doc_starts, folds, w_value, stores):
    folded, single = zip(*folds)
    requests = plan[-1].size + 2
    length, width = stores[0].shape[1:]
    count = folded[0].shape[1]
    groups = HEADS // GROUP
    model_width = w_value.shape[1]
    return pl.pallas_call(
        functools.partial(attend_kernel, size),
        out_shape=jax.ShapeDtypeStruct((count, model_width), jnp.bfloat16),
        in_specs=[SMEM_SPEC] * 5
        + [HBM_SPEC] * FOLDS
        + [VMEM_SPEC] * FOLDS
        + [HBM_SPEC]
        + [ANY_SPEC] * len(stores),
        out_specs=HBM_SPEC,
        scratch_shapes=[
            pltpu.VMEM((requests, length, width), jnp.bfloat16),
            pltpu.VMEM((requests, length, width), jnp.bfloat16),
            pltpu.VMEM((HEADS, count, width), jnp.bfloat16),
            pltpu.VMEM(w_value.shape, jnp.bfloat16),
            pltpu.VMEM((5, GROUP * SPAN, 2 * length), jnp.float32),
            pltpu.VMEM((5, GROUP * SPAN, 2 * length), jnp.bfloat16),
            pltpu.VMEM((2, GROUP, count, width), jnp.bfloat16),
            pltpu.VMEM((count, model_width), jnp.bfloat16),
            pltpu.SemaphoreType.DMA((requests,)),
            pltpu.SemaphoreType.DMA((groups, 3)),
        ],
        compiler_params=pltpu.CompilerParams(vmem_limit_bytes=28 * MIB),
        cost_estimate=pl.CostEstimate(
            flops=2 * HEADS * count * width * (4 * length + HEAD_DIM),
            bytes_accessed=16 * MIB,
            transcendentals=HEADS * count * 2 * length,
        ),
        name="attend_windows",
    )(*plan, doc_starts, *map(in_hbm, folded), *single, in_hbm(w_value), *stores)


def chip_ring(mesh):
    row = mesh.devices.reshape(-1, mesh.shape["seq"])[0]
    chips = list(range(len(row) // CORES))
    columns = [tuple(getattr(row[CORES * chip], "coords", (0, 0))[:2]) for chip in chips]
    if len(set(columns)) != 2:
        return chips
    up = [chip for chip in chips if columns[chip] == columns[0]]
    return up + [chip for chip in reversed(chips) if columns[chip] != columns[0]]


def after(values, others):
    return list(lax.optimization_barrier((tuple(values), tuple(others)))[0])


def body(ring, queries, neighbours, w_key, w_value, retrieval_owner, retrieval_slot, doc_starts):
    devices = lax.axis_size("seq")
    size = len(ring)
    reach = (size - 1) // 2

    ways = [
        (CORES * ring[i] + core, CORES * ring[(i + way) % size] + core)
        for i in range(size)
        for core, way in enumerate((1, -1))
    ]
    onwards = functools.partial(lax.ppermute, axis_name="seq", perm=ways)
    swapped = functools.partial(lax.ppermute, axis_name="seq", perm=[(i, i ^ 1) for i in range(devices)])

    stored = neighbours.shape[0]
    wanted = (retrieval_owner * stored + retrieval_slot).T
    chains = [neighbours, swapped(neighbours)]
    stores = [neighbours, in_hbm(chains[1])]
    half = HEADS // FOLDS
    folds = [fold(0, half, *after([queries], [chains[1]]), w_key)]

    beside = {(1, 0): folds[0]}
    swaps = []
    for step in range(reach):
        for chain in range(2):
            others = list(beside.get((step, chain), ()))
            if step > 1:
                others.append(swaps[2 * step - 4 + chain])
            sent = after([chains[chain]], others) if others else [chains[chain]]
            chains[chain] = onwards(sent[0])
            swaps.append(swapped(chains[chain]))
            stores += [chains[chain], in_hbm(swaps[-1])]
    asked = after([wanted], [chains[1], *swaps[-4:-1]])[0]
    before = lax.ppermute(asked, "seq", [(i, i + 1) for i in range(devices - 1)])
    places = jnp.asarray([ring.index(chip) for chip in range(size)], jnp.int32)
    plan = [lax.axis_index("seq").reshape(1), places, before, wanted]
    if size % 2 == 0:
        last = onwards(chains[0])
        if reach:
            folds += [fold(part * half, half, *after([queries], [chains[0]]), w_key) for part in range(1, FOLDS)]
            others = [value for part in folds[1:] for value in part]
            stores[-1] = swapped(after([chains[1]], [last, before, *others])[0])
        stores += [last, swapped(last)]
    return attend(size, plan, doc_starts, folds, w_value, stores)


def solution(mesh):
    return jax.shard_map(
        functools.partial(body, chip_ring(mesh)),
        mesh=mesh,
        in_specs=(
            P(("groups", "seq"), None),
            P(("groups", "seq"), None, None),
            P(),
            P(),
            P(("groups", "seq"), None),
            P(("groups", "seq"), None),
            P(("groups", "seq")),
        ),
        out_specs=P(("groups", "seq"), None),
        check_vma=False,
    )
```

```python
import functools
import math

import jax
import jax.numpy as jnp
from jax import lax
from jax.experimental import pallas as pl
from jax.experimental.pallas import tpu as pltpu
from jax.sharding import PartitionSpec as P

SPAN = 64
HEADS = 16
HEAD_DIM = 128
EPS = 1e-6
SCALE = math.log2(math.e) / math.sqrt(HEAD_DIM)
CORES = 2
GROUP = 4
FOLDS = 1
MIB = 2**20


SMEM_SPEC = pl.BlockSpec(memory_space=pltpu.SMEM)
VMEM_SPEC = pl.BlockSpec(memory_space=pltpu.VMEM)
ANY_SPEC = pl.BlockSpec(memory_space=pl.ANY)
HBM_SPEC = pl.BlockSpec(memory_space=pltpu.HBM)


def contract(left, right, dims):
    return lax.dot_general(left, right, (dims, ((), ())), preferred_element_type=jnp.float32)


def in_hbm(value):
    return pltpu.with_memory_space_constraint(value, pltpu.HBM)


def head_columns(head):
    return slice(head * HEAD_DIM, (head + 1) * HEAD_DIM)


def group_heads(group):
    return pl.ds(group * GROUP, GROUP)


def group_columns(group):
    return pl.ds(group * GROUP * HEAD_DIM, GROUP * HEAD_DIM)


def fold_kernel(first, query_hbm, key_hbm, folded_hbm, single_ref, query, key, folded, in_sems, out_sems):
    heads = folded.shape[0]

    def fetch(group):
        columns, held = group_columns(first // GROUP + group), group_columns(group)
        return (
            pltpu.make_async_copy(query_hbm.at[:, columns], query.at[:, held], in_sems.at[group, 0]),
            pltpu.make_async_copy(key_hbm.at[:, columns], key.at[:, held], in_sems.at[group, 1]),
        )

    def put(head):
        return pltpu.make_async_copy(folded.at[head], folded_hbm.at[head], out_sems.at[head])

    for group in range(heads // GROUP):
        for copy in fetch(group):
            copy.start()
    for head in range(heads):
        if head % GROUP == 0:
            for copy in fetch(head // GROUP):
                copy.wait()
        columns = head_columns(head)
        queries = pltpu.roll(query[:, columns].astype(jnp.float32), 1, 0).astype(jnp.bfloat16)
        rows = contract(queries, key[:, columns], ((1,), (1,))) * SCALE
        single_ref[head : head + 1, :] = rows[:1]
        folded[head] = rows.astype(jnp.bfloat16)
        put(head).start()
    for head in range(heads):
        put(head).wait()


def fold(first, heads, queries, w_key):
    count, width = queries.shape[0], w_key.shape[0]
    shape, columns = (heads, count, width), heads * HEAD_DIM
    return pl.pallas_call(
        functools.partial(fold_kernel, first),
        out_shape=(
            pltpu.HBM(shape, jnp.bfloat16),
            jax.ShapeDtypeStruct((heads, width), jnp.float32),
        ),
        in_specs=[HBM_SPEC] * 2,
        out_specs=(HBM_SPEC, VMEM_SPEC),
        scratch_shapes=[
            pltpu.VMEM((count, columns), jnp.bfloat16),
            pltpu.VMEM((width, columns), jnp.bfloat16),
            pltpu.VMEM(shape, jnp.bfloat16),
            pltpu.SemaphoreType.DMA((heads // GROUP, 2)),
            pltpu.SemaphoreType.DMA((heads,)),
        ],
        compiler_params=pltpu.CompilerParams(vmem_limit_bytes=16 * MIB),
        cost_estimate=pl.CostEstimate(
            flops=2 * count * columns * width, bytes_accessed=6 * MIB, transcendentals=0
        ),
        name="fold_queries",
    )(in_hbm(queries), in_hbm(w_key))


def normalise(raw, tokens_ref):
    widened = raw.astype(jnp.float32)
    factor = lax.rsqrt(jnp.mean(widened * widened, axis=-1, keepdims=True) + EPS)
    tokens_ref[...] = (widened * factor).astype(jnp.bfloat16)


def among(stores, first, source, act):
    if len(stores) == 1:
        act(stores[0])
        return
    half = len(stores) // 2
    lax.cond(
        source < first + half,
        lambda: among(stores[:half], first, source, act),
        lambda: among(stores[half:], first + half, source, act),
    )


def split(value, count):
    if count & (count - 1):
        return lax.div(value, count), lax.rem(value, count)
    return value >> (count.bit_length() - 1), value & (count - 1)


def locate(request, plan_refs, size, stored):
    here_ref, place_ref, before_ref, wanted_ref = plan_refs
    window, part = divmod(request, 2)
    wanted = before_ref[part, before_ref.shape[1] - 1] if window == 0 else wanted_ref[part, window - 1]
    owner, slot = split(wanted, stored)
    chip, core = split(owner, CORES)
    here_chip, here_core = split(here_ref[0], CORES)
    reach = (size - 1) // 2
    opposite = size - reach - 1
    away = place_ref[here_chip] - place_ref[chip]
    away = jnp.where(away < 0, away + size, away)
    holder = jnp.where((away == 0) | ((away > reach) & (away <= opposite)), core, jnp.where(away <= reach, 0, 1))
    step = jnp.where(away <= opposite, away, size - away)
    arrival = jnp.where(away == 0, 0, 2 * step - 1 + jnp.where(core == holder, 0, 1))
    return CORES * arrival + jnp.where(holder == here_core, 0, 1), slot


def weigh(scores):
    powers = jnp.exp2(scores - jnp.max(scores, axis=-1, keepdims=True))
    totals = jnp.sum(powers, axis=-1, keepdims=True)
    return (powers * (1.0 / totals)).astype(jnp.bfloat16)


def attend_kernel(size, *refs):
    plan_refs, (starts_ref, *folds, value_hbm) = refs[:4], refs[4 : 6 + 2 * FOLDS]
    rest = refs[6 + 2 * FOLDS :]
    *stores, out_hbm, tokens, raw, folded, value, scores, weights, mixed, out, sems, group_sems = rest
    requests, length, width = raw.shape
    blocks = requests // 2 - 1
    count = blocks * SPAN
    rows_at_once = GROUP * SPAN
    groups = HEADS // GROUP
    lone_window = blocks
    order = [*range(1, blocks), lone_window, 0]

    def fetch(request, store, block):
        return pltpu.make_async_copy(store.at[block], raw.at[request], sems.at[request])

    def fetch_group(group):
        columns = group_columns(group)
        piece, place = divmod(group, groups // FOLDS)
        return (
            pltpu.make_async_copy(
                folds[piece].at[group_heads(place)], folded.at[group_heads(group)], group_sems.at[group, 0]
            ),
            pltpu.make_async_copy(value_hbm.at[:, columns], value.at[:, columns], group_sems.at[group, 1]),
        )

    def put(group):
        columns = group_columns(group)
        return pltpu.make_async_copy(out.at[:, columns], out_hbm.at[:, columns], group_sems.at[group, 2])

    for window in order:
        for request in (2 * window, 2 * window + 1):
            source, block = locate(request, plan_refs, size, stores[0].shape[0])
            among(stores, 0, source, lambda store: fetch(request, store, block).start())
        if window == order[0]:
            fetch_group(0)[0].start()
    fetch_group(0)[1].start()
    for group in range(1, groups):
        for copy in fetch_group(group):
            copy.start()

    place = lax.broadcasted_iota(jnp.int32, (count, HEAD_DIM), 0)
    kept = place % SPAN == 0
    for block in range(blocks):
        fresh = starts_ref[block] == 0
        if block == 0:
            fresh = fresh & (plan_refs[0][0] > 0)
        kept = kept | ((place // SPAN == block) & fresh)

    def ready(window):
        for request in (2 * window, 2 * window + 1):
            fetch(request, stores[0], 0).wait()
        for request in (2 * window, 2 * window + 1):
            normalise(raw[request], tokens.at[request])

    def single_rows():
        return jnp.concatenate([single_ref[...] for single_ref in folds[FOLDS:]], axis=0).astype(jnp.bfloat16)

    def along(window):
        return tokens[2 * window : 2 * window + 2].reshape(2 * length, width)

    units = [(group, window) for group in range(groups) for window in order if group == 0 or window != lone_window]
    lone = {}

    def place_of(unit):
        group, window = units[unit]
        heads, rows = slice(group * GROUP, (group + 1) * GROUP), slice(window * SPAN, (window + 1) * SPAN)
        return unit % len(scores), heads, rows

    def score(unit):
        window = units[unit][1]
        if window == lone_window:
            lone["scores"] = contract(single_rows(), along(window), ((1,), (1,)))
            return
        slot, heads, rows = place_of(unit)
        taken = folded[heads, rows].reshape(rows_at_once, width)
        scores[slot] = contract(taken, along(window), ((1,), (1,)))

    parts = GROUP
    tile = -(-width // (parts * 128)) * 128

    def soften(unit, part):
        if units[unit][1] == lone_window:
            if part == 0:
                lone["weights"] = weigh(lone["scores"])
            return
        slot, _, _ = place_of(unit)
        rows = slice(part * SPAN, (part + 1) * SPAN)
        weights[slot, rows] = weigh(scores[slot, rows])

    def combine(unit, part):
        window = units[unit][1]
        columns = slice(part * tile, min(width, (part + 1) * tile))
        keys = tokens[2 * window : 2 * window + 2, :, columns].reshape(2 * length, columns.stop - columns.start)
        if window == lone_window:
            lone["sums", part] = contract(lone["weights"], keys, ((1,), (0,)))
            return
        slot, heads, rows = place_of(unit)
        sums = contract(weights[slot], keys, ((1,), (0,))).reshape(GROUP, SPAN, columns.stop - columns.start)
        if window == 0:
            first = lax.broadcasted_iota(jnp.int32, sums.shape, 1) == 0
            sums = jnp.where(first, lone["sums", part][heads][:, None, :], sums)
        mixed[units[unit][0] % 2, :, rows, columns] = sums.astype(jnp.bfloat16)

    def project(group):
        for head in range(group * GROUP, (group + 1) * GROUP):
            columns = head_columns(head)
            sums = contract(mixed[group % 2, head % GROUP], value[:, columns], ((1,), (0,)))
            sums = jnp.where(kept, sums, 0.0)
            out[:, columns] = pltpu.roll(sums, count - 1, 0).astype(jnp.bfloat16)
        put(group).start()

    ready(order[0])
    for step in range(len(units) + 2):
        if step == 0:
            fetch_group(0)[0].wait()
        if step == len(order):
            fetch_group(0)[1].wait()
            for group in range(1, groups):
                for copy in fetch_group(group):
                    copy.wait()
        if step + 1 < len(order):
            ready(order[step + 1])
        if step < len(units):
            score(step)
        for part in range(parts):
            if 1 <= step <= len(units):
                soften(step - 1, part)
            if step >= 2:
                combine(step - 2, part)
        if step >= 2 and units[step - 2][1] == order[-1]:
            project(units[step - 2][0])
    for group in range(groups):
        put(group).wait()


def attend(size, plan, doc_starts, folds, w_value, stores):
    folded, single = zip(*folds)
    requests = plan[-1].size + 2
    length, width = stores[0].shape[1:]
    count = folded[0].shape[1]
    groups = HEADS // GROUP
    model_width = w_value.shape[1]
    return pl.pallas_call(
        functools.partial(attend_kernel, size),
        out_shape=jax.ShapeDtypeStruct((count, model_width), jnp.bfloat16),
        in_specs=[SMEM_SPEC] * 5
        + [HBM_SPEC] * FOLDS
        + [VMEM_SPEC] * FOLDS
        + [HBM_SPEC]
        + [ANY_SPEC] * len(stores),
        out_specs=HBM_SPEC,
        scratch_shapes=[
            pltpu.VMEM((requests, length, width), jnp.bfloat16),
            pltpu.VMEM((requests, length, width), jnp.bfloat16),
            pltpu.VMEM((HEADS, count, width), jnp.bfloat16),
            pltpu.VMEM(w_value.shape, jnp.bfloat16),
            pltpu.VMEM((5, GROUP * SPAN, 2 * length), jnp.float32),
            pltpu.VMEM((5, GROUP * SPAN, 2 * length), jnp.bfloat16),
            pltpu.VMEM((2, GROUP, count, width), jnp.bfloat16),
            pltpu.VMEM((count, model_width), jnp.bfloat16),
            pltpu.SemaphoreType.DMA((requests,)),
            pltpu.SemaphoreType.DMA((groups, 3)),
        ],
        compiler_params=pltpu.CompilerParams(vmem_limit_bytes=28 * MIB),
        cost_estimate=pl.CostEstimate(
            flops=2 * HEADS * count * width * (4 * length + HEAD_DIM),
            bytes_accessed=16 * MIB,
            transcendentals=HEADS * count * 2 * length,
        ),
        name="attend_windows",
    )(*plan, doc_starts, *map(in_hbm, folded), *single, in_hbm(w_value), *stores)


def chip_ring(mesh):
    row = mesh.devices.reshape(-1, mesh.shape["seq"])[0]
    chips = list(range(len(row) // CORES))
    columns = [tuple(getattr(row[CORES * chip], "coords", (0, 0))[:2]) for chip in chips]
    if len(set(columns)) != 2:
        return chips
    up = [chip for chip in chips if columns[chip] == columns[0]]
    return up + [chip for chip in reversed(chips) if columns[chip] != columns[0]]


def after(values, others):
    return list(lax.optimization_barrier((tuple(values), tuple(others)))[0])


def body(ring, queries, neighbours, w_key, w_value, retrieval_owner, retrieval_slot, doc_starts):
    devices = lax.axis_size("seq")
    size = len(ring)
    reach = (size - 1) // 2

    ways = [
        (CORES * ring[i] + core, CORES * ring[(i + way) % size] + core)
        for i in range(size)
        for core, way in enumerate((1, -1))
    ]
    onwards = functools.partial(lax.ppermute, axis_name="seq", perm=ways)
    swapped = functools.partial(lax.ppermute, axis_name="seq", perm=[(i, i ^ 1) for i in range(devices)])

    stored = neighbours.shape[0]
    wanted = (retrieval_owner * stored + retrieval_slot).T
    chains = [neighbours, swapped(neighbours)]
    stores = [neighbours, in_hbm(chains[1])]
    half = HEADS // FOLDS
    folds = [fold(0, half, *after([queries], [chains[1]]), w_key)]

    beside = {(1, 0): folds[0]}
    swaps = []
    for step in range(reach):
        for chain in range(2):
            others = list(beside.get((step, chain), ()))
            if step > 1:
                others.append(swaps[2 * step - 4 + chain])
            sent = after([chains[chain]], others) if others else [chains[chain]]
            chains[chain] = onwards(sent[0])
            swaps.append(swapped(chains[chain]))
            stores += [chains[chain], in_hbm(swaps[-1])]
    asked = after([wanted], [chains[1], *swaps[-4:-1]])[0]
    before = lax.ppermute(asked, "seq", [(i, i + 1) for i in range(devices - 1)])
    places = jnp.asarray([ring.index(chip) for chip in range(size)], jnp.int32)
    plan = [lax.axis_index("seq").reshape(1), places, before, wanted]
    if size % 2 == 0:
        last = onwards(chains[0])
        if reach:
            folds += [fold(part * half, half, *after([queries], [chains[0]]), w_key) for part in range(1, FOLDS)]
            others = [value for part in folds[1:] for value in part]
            stores[-1] = swapped(after([chains[1]], [last, before, *others])[0])
        stores += [last, swapped(last)]
    return attend(size, plan, doc_starts, folds, w_value, stores)


def solution(mesh):
    return jax.shard_map(
        functools.partial(body, chip_ring(mesh)),
        mesh=mesh,
        in_specs=(
            P(("groups", "seq"), None),
            P(("groups", "seq"), None, None),
            P(),
            P(),
            P(("groups", "seq"), None),
            P(("groups", "seq"), None),
            P(("groups", "seq")),
        ),
        out_specs=P(("groups", "seq"), None),
        check_vma=False,
    )
```

```python
import functools
import math

import jax
import jax.numpy as jnp
from jax import lax
from jax.experimental import pallas as pl
from jax.experimental.pallas import tpu as pltpu
from jax.sharding import PartitionSpec as P

SPAN = 64
HEADS = 16
HEAD_DIM = 128
EPS = 1e-6
SCALE = math.log2(math.e) / math.sqrt(HEAD_DIM)
CORES = 2
GROUP = 4
FOLDS = 1
MIB = 2**20


SMEM_SPEC = pl.BlockSpec(memory_space=pltpu.SMEM)
VMEM_SPEC = pl.BlockSpec(memory_space=pltpu.VMEM)
ANY_SPEC = pl.BlockSpec(memory_space=pl.ANY)
HBM_SPEC = pl.BlockSpec(memory_space=pltpu.HBM)


def contract(left, right, dims):
    return lax.dot_general(left, right, (dims, ((), ())), preferred_element_type=jnp.float32)


def in_hbm(value):
    return pltpu.with_memory_space_constraint(value, pltpu.HBM)


def head_columns(head):
    return slice(head * HEAD_DIM, (head + 1) * HEAD_DIM)


def group_heads(group):
    return pl.ds(group * GROUP, GROUP)


def group_columns(group):
    return pl.ds(group * GROUP * HEAD_DIM, GROUP * HEAD_DIM)


def fold_kernel(first, query_hbm, key_hbm, folded_hbm, single_ref, query, key, folded, in_sems, out_sems):
    heads = folded.shape[0]

    def fetch(group):
        columns, held = group_columns(first // GROUP + group), group_columns(group)
        return (
            pltpu.make_async_copy(query_hbm.at[:, columns], query.at[:, held], in_sems.at[group, 0]),
            pltpu.make_async_copy(key_hbm.at[:, columns], key.at[:, held], in_sems.at[group, 1]),
        )

    def put(head):
        return pltpu.make_async_copy(folded.at[head], folded_hbm.at[head], out_sems.at[head])

    for group in range(heads // GROUP):
        for copy in fetch(group):
            copy.start()
    for head in range(heads):
        if head % GROUP == 0:
            for copy in fetch(head // GROUP):
                copy.wait()
        columns = head_columns(head)
        queries = pltpu.roll(query[:, columns].astype(jnp.float32), 1, 0).astype(jnp.bfloat16)
        rows = contract(queries, key[:, columns], ((1,), (1,))) * SCALE
        single_ref[head : head + 1, :] = rows[:1]
        folded[head] = rows.astype(jnp.bfloat16)
        put(head).start()
    for head in range(heads):
        put(head).wait()


def fold(first, heads, queries, w_key):
    count, width = queries.shape[0], w_key.shape[0]
    shape, columns = (heads, count, width), heads * HEAD_DIM
    return pl.pallas_call(
        functools.partial(fold_kernel, first),
        out_shape=(
            pltpu.HBM(shape, jnp.bfloat16),
            jax.ShapeDtypeStruct((heads, width), jnp.float32),
        ),
        in_specs=[HBM_SPEC] * 2,
        out_specs=(HBM_SPEC, VMEM_SPEC),
        scratch_shapes=[
            pltpu.VMEM((count, columns), jnp.bfloat16),
            pltpu.VMEM((width, columns), jnp.bfloat16),
            pltpu.VMEM(shape, jnp.bfloat16),
            pltpu.SemaphoreType.DMA((heads // GROUP, 2)),
            pltpu.SemaphoreType.DMA((heads,)),
        ],
        compiler_params=pltpu.CompilerParams(vmem_limit_bytes=16 * MIB),
        cost_estimate=pl.CostEstimate(
            flops=2 * count * columns * width, bytes_accessed=6 * MIB, transcendentals=0
        ),
        name="fold_queries",
    )(in_hbm(queries), in_hbm(w_key))


def normalise(raw, tokens_ref):
    widened = raw.astype(jnp.float32)
    factor = lax.rsqrt(jnp.mean(widened * widened, axis=-1, keepdims=True) + EPS)
    tokens_ref[...] = (widened * factor).astype(jnp.bfloat16)


def among(stores, first, source, act):
    if len(stores) == 1:
        act(stores[0])
        return
    half = len(stores) // 2
    lax.cond(
        source < first + half,
        lambda: among(stores[:half], first, source, act),
        lambda: among(stores[half:], first + half, source, act),
    )


def split(value, count):
    if count & (count - 1):
        return lax.div(value, count), lax.rem(value, count)
    return value >> (count.bit_length() - 1), value & (count - 1)


def locate(request, plan_refs, size, stored):
    here_ref, place_ref, before_ref, wanted_ref = plan_refs
    window, part = divmod(request, 2)
    wanted = before_ref[part, before_ref.shape[1] - 1] if window == 0 else wanted_ref[part, window - 1]
    owner, slot = split(wanted, stored)
    chip, core = split(owner, CORES)
    here_chip, here_core = split(here_ref[0], CORES)
    reach = (size - 1) // 2
    opposite = size - reach - 1
    away = place_ref[here_chip] - place_ref[chip]
    away = jnp.where(away < 0, away + size, away)
    holder = jnp.where((away == 0) | ((away > reach) & (away <= opposite)), core, jnp.where(away <= reach, 0, 1))
    step = jnp.where(away <= opposite, away, size - away)
    arrival = jnp.where(away == 0, 0, 2 * step - 1 + jnp.where(core == holder, 0, 1))
    return CORES * arrival + jnp.where(holder == here_core, 0, 1), slot


def weigh(scores):
    powers = jnp.exp2(scores - jnp.max(scores, axis=-1, keepdims=True))
    totals = jnp.sum(powers, axis=-1, keepdims=True)
    return (powers * (1.0 / totals)).astype(jnp.bfloat16)


def attend_kernel(size, *refs):
    plan_refs, (starts_ref, *folds, value_hbm) = refs[:4], refs[4 : 6 + 2 * FOLDS]
    rest = refs[6 + 2 * FOLDS :]
    *stores, out_hbm, tokens, raw, folded, value, scores, weights, mixed, out, sems, group_sems = rest
    requests, length, width = raw.shape
    blocks = requests // 2 - 1
    count = blocks * SPAN
    rows_at_once = GROUP * SPAN
    groups = HEADS // GROUP
    lone_window = blocks
    order = [*range(1, blocks), lone_window, 0]

    def fetch(request, store, block):
        return pltpu.make_async_copy(store.at[block], raw.at[request], sems.at[request])

    def fetch_group(group):
        columns = group_columns(group)
        piece, place = divmod(group, groups // FOLDS)
        return (
            pltpu.make_async_copy(
                folds[piece].at[group_heads(place)], folded.at[group_heads(group)], group_sems.at[group, 0]
            ),
            pltpu.make_async_copy(value_hbm.at[:, columns], value.at[:, columns], group_sems.at[group, 1]),
        )

    def put(group):
        columns = group_columns(group)
        return pltpu.make_async_copy(out.at[:, columns], out_hbm.at[:, columns], group_sems.at[group, 2])

    fetch_group(0)[0].start()
    for window in order:
        for request in (2 * window, 2 * window + 1):
            source, block = locate(request, plan_refs, size, stores[0].shape[0])
            among(stores, 0, source, lambda store: fetch(request, store, block).start())
    fetch_group(0)[1].start()
    for group in range(1, groups):
        for copy in fetch_group(group):
            copy.start()

    place = lax.broadcasted_iota(jnp.int32, (count, HEAD_DIM), 0)
    kept = place % SPAN == 0
    for block in range(blocks):
        fresh = starts_ref[block] == 0
        if block == 0:
            fresh = fresh & (plan_refs[0][0] > 0)
        kept = kept | ((place // SPAN == block) & fresh)

    def ready(window):
        for request in (2 * window, 2 * window + 1):
            fetch(request, stores[0], 0).wait()
        for request in (2 * window, 2 * window + 1):
            normalise(raw[request], tokens.at[request])

    def single_rows():
        return jnp.concatenate([single_ref[...] for single_ref in folds[FOLDS:]], axis=0).astype(jnp.bfloat16)

    def along(window):
        return tokens[2 * window : 2 * window + 2].reshape(2 * length, width)

    units = [(group, window) for group in range(groups) for window in order if group == 0 or window != lone_window]
    lone = {}

    def place_of(unit):
        group, window = units[unit]
        heads, rows = slice(group * GROUP, (group + 1) * GROUP), slice(window * SPAN, (window + 1) * SPAN)
        return unit % len(scores), heads, rows

    def score(unit):
        window = units[unit][1]
        if window == lone_window:
            lone["scores"] = contract(single_rows(), along(window), ((1,), (1,)))
            return
        slot, heads, rows = place_of(unit)
        taken = folded[heads, rows].reshape(rows_at_once, width)
        scores[slot] = contract(taken, along(window), ((1,), (1,)))

    parts = GROUP
    tile = -(-width // (parts * 128)) * 128

    def soften(unit, part):
        if units[unit][1] == lone_window:
            if part == 0:
                lone["weights"] = weigh(lone["scores"])
            return
        slot, _, _ = place_of(unit)
        rows = slice(part * SPAN, (part + 1) * SPAN)
        weights[slot, rows] = weigh(scores[slot, rows])

    def combine(unit, part):
        window = units[unit][1]
        columns = slice(part * tile, min(width, (part + 1) * tile))
        keys = tokens[2 * window : 2 * window + 2, :, columns].reshape(2 * length, columns.stop - columns.start)
        if window == lone_window:
            lone["sums", part] = contract(lone["weights"], keys, ((1,), (0,)))
            return
        slot, heads, rows = place_of(unit)
        sums = contract(weights[slot], keys, ((1,), (0,))).reshape(GROUP, SPAN, columns.stop - columns.start)
        if window == 0:
            first = lax.broadcasted_iota(jnp.int32, sums.shape, 1) == 0
            sums = jnp.where(first, lone["sums", part][heads][:, None, :], sums)
        mixed[units[unit][0] % 2, :, rows, columns] = sums.astype(jnp.bfloat16)

    def project(group):
        for head in range(group * GROUP, (group + 1) * GROUP):
            columns = head_columns(head)
            sums = contract(mixed[group % 2, head % GROUP], value[:, columns], ((1,), (0,)))
            sums = jnp.where(kept, sums, 0.0)
            out[:, columns] = pltpu.roll(sums, count - 1, 0).astype(jnp.bfloat16)
        put(group).start()

    ready(order[0])
    for step in range(len(units) + 2):
        if step == 0:
            fetch_group(0)[0].wait()
        if step == len(order):
            fetch_group(0)[1].wait()
            for group in range(1, groups):
                for copy in fetch_group(group):
                    copy.wait()
        if step + 1 < len(order):
            ready(order[step + 1])
        if step < len(units):
            score(step)
        for part in range(parts):
            if 1 <= step <= len(units):
                soften(step - 1, part)
            if step >= 2:
                combine(step - 2, part)
        if step >= 2 and units[step - 2][1] == order[-1]:
            project(units[step - 2][0])
    for group in range(groups):
        put(group).wait()


def attend(size, plan, doc_starts, folds, w_value, stores):
    folded, single = zip(*folds)
    requests = plan[-1].size + 2
    length, width = stores[0].shape[1:]
    count = folded[0].shape[1]
    groups = HEADS // GROUP
    model_width = w_value.shape[1]
    return pl.pallas_call(
        functools.partial(attend_kernel, size),
        out_shape=jax.ShapeDtypeStruct((count, model_width), jnp.bfloat16),
        in_specs=[SMEM_SPEC] * 5
        + [HBM_SPEC] * FOLDS
        + [VMEM_SPEC] * FOLDS
        + [HBM_SPEC]
        + [ANY_SPEC] * len(stores),
        out_specs=HBM_SPEC,
        scratch_shapes=[
            pltpu.VMEM((requests, length, width), jnp.bfloat16),
            pltpu.VMEM((requests, length, width), jnp.bfloat16),
            pltpu.VMEM((HEADS, count, width), jnp.bfloat16),
            pltpu.VMEM(w_value.shape, jnp.bfloat16),
            pltpu.VMEM((5, GROUP * SPAN, 2 * length), jnp.float32),
            pltpu.VMEM((5, GROUP * SPAN, 2 * length), jnp.bfloat16),
            pltpu.VMEM((2, GROUP, count, width), jnp.bfloat16),
            pltpu.VMEM((count, model_width), jnp.bfloat16),
            pltpu.SemaphoreType.DMA((requests,)),
            pltpu.SemaphoreType.DMA((groups, 3)),
        ],
        compiler_params=pltpu.CompilerParams(vmem_limit_bytes=28 * MIB),
        cost_estimate=pl.CostEstimate(
            flops=2 * HEADS * count * width * (4 * length + HEAD_DIM),
            bytes_accessed=16 * MIB,
            transcendentals=HEADS * count * 2 * length,
        ),
        name="attend_windows",
    )(*plan, doc_starts, *map(in_hbm, folded), *single, in_hbm(w_value), *stores)


def chip_ring(mesh):
    row = mesh.devices.reshape(-1, mesh.shape["seq"])[0]
    chips = list(range(len(row) // CORES))
    columns = [tuple(getattr(row[CORES * chip], "coords", (0, 0))[:2]) for chip in chips]
    if len(set(columns)) != 2:
        return chips
    up = [chip for chip in chips if columns[chip] == columns[0]]
    return up + [chip for chip in reversed(chips) if columns[chip] != columns[0]]


def after(values, others):
    return list(lax.optimization_barrier((tuple(values), tuple(others)))[0])


def body(ring, queries, neighbours, w_key, w_value, retrieval_owner, retrieval_slot, doc_starts):
    devices = lax.axis_size("seq")
    size = len(ring)
    reach = (size - 1) // 2

    ways = [
        (CORES * ring[i] + core, CORES * ring[(i + way) % size] + core)
        for i in range(size)
        for core, way in enumerate((1, -1))
    ]
    onwards = functools.partial(lax.ppermute, axis_name="seq", perm=ways)
    swapped = functools.partial(lax.ppermute, axis_name="seq", perm=[(i, i ^ 1) for i in range(devices)])

    stored = neighbours.shape[0]
    wanted = (retrieval_owner * stored + retrieval_slot).T
    chains = [neighbours, swapped(neighbours)]
    stores = [neighbours, in_hbm(chains[1])]
    half = HEADS // FOLDS
    folds = [fold(0, half, *after([queries], [chains[1]]), w_key)]

    beside = {(1, 0): folds[0]}
    swaps = []
    for step in range(reach):
        for chain in range(2):
            others = list(beside.get((step, chain), ()))
            if step > 1:
                others.append(swaps[2 * step - 4 + chain])
            sent = after([chains[chain]], others) if others else [chains[chain]]
            chains[chain] = onwards(sent[0])
            swaps.append(swapped(chains[chain]))
            stores += [chains[chain], in_hbm(swaps[-1])]
    asked = after([wanted], [chains[1], *swaps[-4:-1]])[0]
    before = lax.ppermute(asked, "seq", [(i, i + 1) for i in range(devices - 1)])
    places = jnp.asarray([ring.index(chip) for chip in range(size)], jnp.int32)
    plan = [lax.axis_index("seq").reshape(1), places, before, wanted]
    if size % 2 == 0:
        last = onwards(chains[0])
        if reach:
            folds += [fold(part * half, half, *after([queries], [chains[0]]), w_key) for part in range(1, FOLDS)]
            others = [value for part in folds[1:] for value in part]
            stores[-1] = swapped(after([chains[1]], [last, before, *others])[0])
        stores += [last, swapped(last)]
    return attend(size, plan, doc_starts, folds, w_value, stores)


def solution(mesh):
    return jax.shard_map(
        functools.partial(body, chip_ring(mesh)),
        mesh=mesh,
        in_specs=(
            P(("groups", "seq"), None),
            P(("groups", "seq"), None, None),
            P(),
            P(),
            P(("groups", "seq"), None),
            P(("groups", "seq"), None),
            P(("groups", "seq")),
        ),
        out_specs=P(("groups", "seq"), None),
        check_vma=False,
    )
```
